128 devices in a mesh: chord: 8 (over z_hi, y), span: 16 (over x, z_lo, core).
Axes of the slice: x: 4, y: 4, z: 4 (z_hi: 2, z_lo: 2; z = z_hi * 2 + z_lo), core: 2. Of those that a mesh axis runs over, the one named last changes fastest.
Arguments:
- flow_state: float32 [6, 12, 64, 2048], P(None, None, 'chord', 'span'), may hold values from -0.25 to 3, as said below
- displacement: float32 [3, 12, 64, 2048], P(None, None, 'chord', 'span'), may hold values from -0.2 to 0.2
- wall_distance: float32 [12, 64, 2048], P(None, 'chord', 'span'), may hold values from 0.5 to 4
- face_codes: int32 [64, 2048], P('chord', 'span'), may hold values from 0 to 2
- cost_gradient: float32 [6, 12, 64, 2048], P(None, None, 'chord', 'span'), may hold values from -20 to 20
Outputs:
- basis_next: float32 [6, 12, 64, 2048], P(None, None, 'chord', 'span')
- hessenberg: float32 [5], replicated
The draws below stay inside these ranges and needn't reach their ends.
Inputs may be any that keep to these rules, and one draw needn't show every extreme that they name: `flow_state`: density lies in 0.8 to 1.2, each momentum in -0.25 to 0.25, energy in 2 to 3, and the last variable is the density times a value in 0.02 to 0.2. `face_codes`: 0 slip wall, 1 no-slip wall, 2 far field.
All inputs are finite; a program needn't handle non-finite values.
Results may differ from the reference program's by a relative error of at most 0.0003.
Values sent between devices are 32-bit elements; how exact they have to be, the bound alone decides.
A program may use at most 128 MiB of HBM per device.

```python
import math
import jax
import jax.numpy as jnp
from jax import lax

NZ = 12
CX = 8
CY = 128
NX = 64
NY = 2048
N_SPAN = 16


def draw_flow_state(key, part):
    key = jax.random.fold_in(key, 11)
    keys = jax.random.split(key, 4)
    shape = (NZ, NX, NY)
    density = jax.random.uniform(keys[0], shape, jnp.float32, 0.8, 1.2)
    momenta = jax.random.uniform(keys[1], (3,) + shape, jnp.float32, -0.25, 0.25)
    energy = jax.random.uniform(keys[2], shape, jnp.float32, 2.0, 3.0)
    turbulence = jax.random.uniform(keys[3], shape, jnp.float32, 0.02, 0.2)
    return jnp.concatenate([density[None], momenta, energy[None], (density * turbulence)[None]], axis=0).astype(jnp.float32)


def draw_cost_gradient(key, part):
    key = jax.random.fold_in(key, 23)
    keys = jax.random.split(key, 2)
    chord_scale = 1.0 + 2.0 * jnp.arange(NX, dtype=jnp.float32) / NX
    span_scale = 1.0 + 2.0 * jnp.arange(NY, dtype=jnp.float32) / NY
    level_grid = jnp.exp(jax.random.uniform(keys[0], (NX // CX, NY // CY), jnp.float32, -0.5, 0.5))
    level_plane = jnp.repeat(jnp.repeat(level_grid, CX, axis=0), CY, axis=1)
    scale_plane = jnp.sqrt(chord_scale[:, None] * span_scale[None, :]) * level_plane
    values = jax.random.truncated_normal(keys[1], -4.0, 4.0, (6, NZ, NX, NY), jnp.float32)
    return (values * scale_plane).astype(jnp.float32)


def plant(entries, key, low, high):
    longest = entries.shape.index(max(entries.shape))
    spots = []
    for shift in (0, 1):
        where = [jax.random.randint(jax.random.fold_in(key, axis), (), 0, length) for axis, length in enumerate(entries.shape)]
        where[longest] = (where[longest] + shift) % entries.shape[longest]
        spots.append(tuple(where))
    return entries.at[spots[0]].set(low).at[spots[1]].set(high)


def levels(own_key, shape, cuts, low, largest):
    gain = 1.0
    for dim, shards_of in cuts:
        steps = jax.random.uniform(jax.random.fold_in(jax.random.fold_in(own_key, 6), dim), (shards_of,), jnp.float32, low / len(cuts), largest / len(cuts))
        gain = gain * jnp.repeat(jnp.exp(steps), shape[dim] // shards_of).reshape((-1,) + (1,) * (len(shape) - 1 - dim))
    return gain


def setup_inputs(seed: int = 0) -> dict:
    key_of = jax.random.split(jax.random.key(seed), 6)
    flow_state = draw_flow_state(jax.random.fold_in(key_of[5], 71), 0)
    displacement = jnp.clip(jax.random.uniform(key_of[1], (3, NZ, NX, NY), jnp.float32, -0.2, 0.2) * levels(key_of[1], (3, NZ, NX, NY), ((2, 8), (3, 16)), -0.4, 0.0), -0.2, 0.2)
    wall_distance = jnp.clip(jnp.exp(math.log(4.0) - 2.0794415 * jax.random.uniform(key_of[2], (NZ, NX, NY), jnp.float32) ** levels(key_of[2], (NZ, NX, NY), ((1, 8), (2, 16)), -0.2, 0.2)), 0.5, 4.0)
    face_codes = plant(jax.random.randint(key_of[3], (NX, NY), 0, 3), jax.random.fold_in(key_of[3], 1), 0, 2).astype(jnp.int32)
    cost_gradient = draw_cost_gradient(jax.random.fold_in(key_of[5], 71), 0)
    return {"flow_state": flow_state, "displacement": displacement, "wall_distance": wall_distance, "face_codes": face_codes, "cost_gradient": cost_gradient}


HEAT_RATIO = 1.4
GAMMA_LESS = 0.4
VISCOSITY = 0.2
HEAT_FACTOR = 1.4 / (0.4 * 0.72)
CB_ONE = 0.1355
CW_ONE = 3.239
CV_CUBE = 7.1 * 7.1 * 7.1
TURB_SIGMA = 2.0 / 3.0
LIMIT_EPS = 0.01
NORM_EPS = 1e-06
FREESTREAM = (1.0, 0.2, 0.0, 0.05, 2.5, 0.1)
SLIP_SIGNS = (1.0, 1.0, 1.0, -1.0, 1.0, 1.0)
WALL_SIGNS = (1.0, -1.0, -1.0, -1.0, 1.0, -1.0)

def limiter(upwind, downwind):
    return ((downwind * downwind + LIMIT_EPS) * upwind + (upwind * upwind + LIMIT_EPS) * downwind) / (upwind * upwind + downwind * downwind + 2.0 * LIMIT_EPS)

def primitive(state):
    density = state[0]
    velocity = state[1:4] / density
    pressure = GAMMA_LESS * (state[4] - 0.5 * density * lax.optimization_barrier(jnp.sum(velocity * velocity, axis=0)))
    return (density, velocity, pressure)

def normal_flux(state, normal):
    density, velocity, pressure = primitive(state)
    normal_speed = lax.optimization_barrier(jnp.sum(velocity * normal, axis=0))
    momentum = state[1:4] * normal_speed + pressure * normal
    return jnp.concatenate([(state[0] * normal_speed)[None], momentum, ((state[4] + pressure) * normal_speed)[None], (state[5] * normal_speed)[None]], axis=0)

def face_flux(before, left_cell, right_cell, beyond, direction):
    offsets = right_cell[6:] - left_cell[6:]
    unit_vector = jnp.array([1.0 if member == direction else 0.0 for member in range(3)], jnp.float32)
    spacing = offsets + unit_vector.reshape((3,) + (1,) * (offsets.ndim - 1))
    distance = jnp.sqrt(lax.optimization_barrier(jnp.sum(spacing * spacing, axis=0)))
    normal = spacing / distance
    weight = 1.0 / distance
    left_state = left_cell[:6] + 0.5 * limiter(left_cell[:6] - before[:6], right_cell[:6] - left_cell[:6])
    right_state = right_cell[:6] - 0.5 * limiter(right_cell[:6] - left_cell[:6], beyond[:6] - right_cell[:6])
    mean_density, mean_velocity, mean_pressure = primitive(0.5 * (left_state + right_state))
    wave_speed = jnp.abs(lax.optimization_barrier(jnp.sum(mean_velocity * normal, axis=0))) + jnp.sqrt(HEAT_RATIO * mean_pressure / mean_density)
    convective = 0.5 * (normal_flux(left_state, normal) + normal_flux(right_state, normal)) - 0.5 * wave_speed * (right_state - left_state)
    density_left, velocity_left, pressure_left = primitive(left_cell[:6])
    density_right, velocity_right, pressure_right = primitive(right_cell[:6])
    turb_left = left_cell[5] / density_left
    turb_right = right_cell[5] / density_right
    face_density = 0.5 * (density_left + density_right)
    face_turb = 0.5 * (turb_left + turb_right)
    visc_ratio = face_density * face_turb / VISCOSITY
    ratio_cube = visc_ratio * visc_ratio * visc_ratio
    effective = (VISCOSITY + face_density * face_turb * ratio_cube / (ratio_cube + CV_CUBE)) * weight
    energy_jump = HEAT_FACTOR * (pressure_right / density_right - pressure_left / density_left) + 0.5 * (lax.optimization_barrier(jnp.sum(velocity_right * velocity_right, axis=0)) - lax.optimization_barrier(jnp.sum(velocity_left * velocity_left, axis=0)))
    turb_flux = (VISCOSITY + face_density * face_turb) / TURB_SIGMA * weight * (turb_right - turb_left)
    viscous = jnp.concatenate([jnp.zeros_like(face_density)[None], -effective * (velocity_right - velocity_left), (-effective * energy_jump)[None], (-turb_flux)[None]], axis=0)
    return convective + viscous

def boundary_ghost(state, face_codes):
    slip_state = jnp.array(SLIP_SIGNS, jnp.float32)[:, None, None] * state
    wall_state = jnp.array(WALL_SIGNS, jnp.float32)[:, None, None] * state
    far_state = jnp.broadcast_to(jnp.array(FREESTREAM, jnp.float32)[:, None, None], state.shape)
    code_plane = face_codes[None]
    return jnp.where(code_plane == 0, slip_state, jnp.where(code_plane == 1, wall_state, far_state))

def axis_pullback(window, face_cot, grid_dim):
    metric_part = window[6:]
    extent = window.shape[grid_dim]

    def fluxes(flow_part):
        full_state = jnp.concatenate([flow_part, metric_part], axis=0)
        pieces = [lax.slice_in_dim(full_state, offset, offset + extent - 3, axis=grid_dim) for offset in range(4)]
        return face_flux(pieces[0], pieces[1], pieces[2], pieces[3], grid_dim - 2)
    unused, pullback = jax.vjp(fluxes, window[:6])
    return pullback(face_cot)[0]

def wide_pullback(window, beside_all, grid_dim):
    interior = beside_all.shape[grid_dim] - 4
    upper_part = lax.slice_in_dim(beside_all, 0, interior + 3, axis=grid_dim)
    lower_part = lax.slice_in_dim(beside_all, 1, interior + 4, axis=grid_dim)
    result = axis_pullback(window, upper_part - lower_part, grid_dim)
    return lax.slice_in_dim(result, 3, interior + 3, axis=grid_dim)

def column_pullback(block_cells, adjoint, face_codes, wall_distance):
    metric_part = block_cells[6:]
    layers = block_cells.shape[1]

    def column_terms(flow_part):
        ghost_near = boundary_ghost(flow_part[:, 0], face_codes)
        ghost_far = boundary_ghost(flow_part[:, 1], face_codes)
        far_state = jnp.broadcast_to(jnp.array(FREESTREAM, jnp.float32)[:, None, None], ghost_near.shape)
        flow_layers = jnp.concatenate([ghost_far[:, None], ghost_near[:, None], flow_part, far_state[:, None], far_state[:, None]], axis=1)
        metric = jnp.concatenate([metric_part[:, 1:2], metric_part[:, 0:1], metric_part, metric_part[:, -1:], metric_part[:, -1:]], axis=1)
        full_state = jnp.concatenate([flow_layers, metric], axis=0)
        pieces = [lax.slice_in_dim(full_state, offset, offset + layers + 1, axis=1) for offset in range(4)]
        fluxes = face_flux(pieces[0], pieces[1], pieces[2], pieces[3], 2)
        density = flow_part[0]
        velocity = flow_part[1:4] / density
        turbulence = flow_part[5] / density
        shear_rate = jnp.sqrt(lax.optimization_barrier(jnp.sum(velocity * velocity, axis=0)) + 0.01) / wall_distance
        scaled = turbulence / wall_distance
        source = density * (CB_ONE * shear_rate * turbulence - CW_ONE * scaled * scaled)
        return (fluxes, source)
    zero_layers = jnp.zeros_like(adjoint[:, :2])
    padded = jnp.concatenate([zero_layers, adjoint, zero_layers], axis=1)
    face_cot = padded[:, 1:layers + 2] - padded[:, 2:layers + 3]
    unused, pullback = jax.vjp(column_terms, block_cells[:6])
    return pullback((face_cot, -adjoint[5]))[0]

def transpose_product(state, adjoint, face_codes, wall_distance):
    columns_total = state.shape[3]

    def span_block(member):
        offset = member * CY
        columns = ((offset - 3 + jnp.arange(CY + 6, dtype=jnp.int32)) % columns_total).astype(jnp.int32)
        window = jnp.take(state, columns, axis=3)
        beside_all = jnp.take(adjoint, columns[1:-1], axis=3)
        block_cells = window[:, :, :, 3:-3]
        block_adjoint = beside_all[:, :, :, 2:-2]
        chord_window = jnp.concatenate([block_cells[:, :, -3:], block_cells, block_cells[:, :, :3]], axis=2)
        chord_around = jnp.concatenate([block_adjoint[:, :, -2:], block_adjoint, block_adjoint[:, :, :2]], axis=2)
        block_codes = jnp.take(face_codes, columns[3:-3], axis=1)
        block_wall = jnp.take(wall_distance, columns[3:-3], axis=2)
        return wide_pullback(chord_window, chord_around, 2) + wide_pullback(window, beside_all, 3) + column_pullback(block_cells, block_adjoint, block_codes, block_wall)
    span_parts = lax.map(span_block, jnp.arange(N_SPAN, dtype=jnp.int32))
    return jnp.moveaxis(span_parts, 0, 3).reshape(adjoint.shape)

def reference(flow_state, displacement, wall_distance, face_codes, cost_gradient):
    state = jnp.concatenate([flow_state, displacement], axis=0)
    seed_scale = jnp.sqrt(jnp.mean(cost_gradient * cost_gradient) + NORM_EPS)
    leading = cost_gradient / seed_scale
    mapped = transpose_product(state, leading, face_codes, wall_distance)
    h_one_one = jnp.mean(mapped * leading)
    mapped = mapped - h_one_one * leading
    h_two_one = jnp.sqrt(jnp.mean(mapped * mapped) + NORM_EPS)
    second = mapped / h_two_one
    mapped = transpose_product(state, second, face_codes, wall_distance)
    h_one_two = jnp.mean(mapped * leading)
    h_two_two = jnp.mean(mapped * second)
    mapped = mapped - h_one_two * leading
    mapped = mapped - h_two_two * second
    h_three_two = jnp.sqrt(jnp.mean(mapped * mapped) + NORM_EPS)
    basis_next = mapped / h_three_two
    hessenberg = jnp.stack([h_one_one, h_two_one, h_one_two, h_two_two, h_three_two])
    return (basis_next, hessenberg)
```

```python
import functools

import jax
import jax.numpy as jnp
from jax import lax
from jax.experimental import pallas as pl
from jax.experimental.pallas import tpu as pltpu
from jax.sharding import PartitionSpec as P

HEAT_RATIO = 1.4
GAMMA_LESS = 0.4
VISCOSITY = 0.2
HEAT_FACTOR = 1.4 / (0.4 * 0.72)
CB_ONE = 0.1355
CW_ONE = 3.239
CV_CUBE = 7.1 * 7.1 * 7.1
TURB_SIGMA = 2.0 / 3.0
LIMIT_EPS = 0.01
NORM_EPS = 1e-06
FREESTREAM = (1.0, 0.2, 0.0, 0.05, 2.5, 0.1)
SLIP_SIGNS = (1.0, 1.0, 1.0, -1.0, 1.0, 1.0)
WALL_SIGNS = (1.0, -1.0, -1.0, -1.0, 1.0, -1.0)

HEAT_E = GAMMA_LESS * HEAT_FACTOR
HEAT_K = 1.0 - GAMMA_LESS * HEAT_FACTOR
CUBE_SHIFT = VISCOSITY * VISCOSITY * VISCOSITY * CV_CUBE

LAYERS, CX, CY = 12, 8, 128
ROWS = LAYERS * CX

COL_STEP, COL_OWN, COL_ROWS = 8, 32, 160
CHORD_STEP, CHORD_OWN, CHORD_ROWS = 12, 40, 176
SPAN_STEP, SPAN_OWN, SPAN_ROWS = 1, 16, 160

FL, FR, FN, FD, FM, FS, FQ, FK, FE, FRH, FTH = 0, 7, 14, 17, 23, 28, 29, 30, 31, 36, 37
FACE_COUNT = 38
GL, GR, PU, PH, TL, TR, RB = 0, 6, 12, 15, 16, 17, 18
RESULT_COUNT = 19


def blocks(first, last, size, body):
    def step(index, carry):
        body(pl.multiple_of(first + index * size, 8))
        return carry

    lax.fori_loop(0, (last - first) // size, step, 0)


def dot3(a, b):
    return a[0] * b[0] + a[1] * b[1] + a[2] * b[2]


def primitives(state):
    inverse = 1.0 / state[0]
    velocity = [state[1 + j] * inverse for j in range(3)]
    return inverse, velocity, state[5] * inverse, state[4] * inverse


def slopes_stage(step, first, last, size, window, halves, pulls, prims):
    def body(row):
        here_all = []
        for k in range(6):
            before = window[k, pl.ds(row - step, size), :]
            here = window[k, pl.ds(row, size), :]
            after = window[k, pl.ds(row + step, size), :]
            p = here - before
            q = after - here
            pp = p * p + LIMIT_EPS
            qq = q * q + LIMIT_EPS
            inverse = 1.0 / (pp + qq)
            slope = (qq * p + pp * q) * inverse
            half_inverse = 0.5 * inverse
            a = (qq + 2.0 * p * (q - slope)) * half_inverse
            b = (pp + 2.0 * q * (p - slope)) * half_inverse
            rows = pl.ds(row, size)
            halves[k, rows, :] = here + 0.5 * slope
            halves[6 + k, rows, :] = here - 0.5 * slope
            pulls[k, rows, :] = a
            pulls[6 + k, rows, :] = b
            pulls[12 + k, rows, :] = a - b
            here_all.append(here)
        inverse, velocity, turbulence, specific = primitives(here_all)
        rows = pl.ds(row, size)
        prims[0, rows, :] = inverse
        for j in range(3):
            prims[1 + j, rows, :] = velocity[j]
        prims[4, rows, :] = turbulence
        prims[5, rows, :] = specific

    blocks(first, last, size, body)


def side_coefficients(state, normal):
    inverse, velocity, turbulence, specific = primitives(state)
    kinetic = 0.5 * dot3(velocity, velocity)
    pressure_ratio = GAMMA_LESS * (specific - kinetic)
    return velocity + [kinetic, specific + pressure_ratio, turbulence, dot3(velocity, normal)]


def faces_stage(step, direction, first, last, size, window, offsets, halves, prims, faces):
    def body(row):
        here = pl.ds(row, size)
        after = pl.ds(row + step, size)
        spacing = [offsets[j, after, :] - offsets[j, here, :] for j in range(3)]
        spacing[direction] = spacing[direction] + 1.0
        weight = lax.rsqrt(dot3(spacing, spacing))
        normal = [spacing[j] * weight for j in range(3)]
        left = [halves[k, here, :] for k in range(6)]
        right = [halves[6 + k, after, :] for k in range(6)]
        for slot, value in enumerate(side_coefficients(left, normal)):
            faces[FL + slot, here, :] = value
        for slot, value in enumerate(side_coefficients(right, normal)):
            faces[FR + slot, here, :] = value
        for j in range(3):
            faces[FN + j, here, :] = normal[j]
        for k in range(6):
            faces[FD + k, here, :] = left[k] - right[k]
        middle = [0.5 * (left[k] + right[k]) for k in range(5)] + [left[5]]
        inverse, velocity, unused, specific = primitives(middle)
        kinetic = 0.5 * dot3(velocity, velocity)
        speed = dot3(velocity, normal)
        sound_square = HEAT_RATIO * GAMMA_LESS * (specific - kinetic)
        sound_inverse = lax.rsqrt(sound_square)
        size_speed = jnp.abs(speed)
        sign = jnp.where(speed > 0.0, 1.0, jnp.where(speed < 0.0, -1.0, 0.0))
        half_inverse = 0.5 * inverse
        factor = 0.5 * HEAT_RATIO * GAMMA_LESS * sound_inverse
        faces[FS, here, :] = size_speed + sound_square * sound_inverse
        faces[FM, here, :] = half_inverse * (factor * (2.0 * kinetic - specific) - size_speed)
        for j in range(3):
            faces[FM + 1 + j, here, :] = half_inverse * (sign * normal[j] - factor * velocity[j])
        faces[FM + 4, here, :] = half_inverse * factor
        velocity_l = [prims[1 + j, here, :] for j in range(3)]
        velocity_r = [prims[1 + j, after, :] for j in range(3)]
        jump = [velocity_r[j] - velocity_l[j] for j in range(3)]
        kinetic_jump = 0.5 * (dot3(velocity_r, velocity_r) - dot3(velocity_l, velocity_l))
        heat_jump = HEAT_E * (prims[5, after, :] - prims[5, here, :]) + HEAT_K * kinetic_jump
        turbulence_l, turbulence_r = prims[4, here, :], prims[4, after, :]
        half_density = 0.25 * (window[0, here, :] + window[0, after, :])
        half_turbulence = 0.25 * (turbulence_l + turbulence_r)
        mixed = 4.0 * half_density * half_turbulence
        cube = mixed * mixed * mixed
        ratio = cube / (cube + CUBE_SHIFT)
        twice = 2.0 * weight
        pull = -twice * ratio * (4.0 - 3.0 * ratio)
        faces[FQ, here, :] = twice * (VISCOSITY + mixed * ratio)
        faces[FK, here, :] = (VISCOSITY + mixed) * (twice / TURB_SIGMA)
        for j in range(3):
            faces[FE + j, here, :] = pull * jump[j]
        faces[FE + 3, here, :] = pull * heat_jump
        faces[FE + 4, here, :] = -(twice / TURB_SIGMA) * (turbulence_r - turbulence_l)
        faces[FRH, here, :] = half_density
        faces[FTH, here, :] = half_turbulence

    blocks(first, last, size, body)


def side_pullback(faces, here, base, normal, wave, shared, g):
    velocity = [faces[base + j, here, :] for j in range(3)]
    kinetic = faces[base + 3, here, :]
    enthalpy = faces[base + 4, here, :]
    turbulence = faces[base + 5, here, :]
    speed = faces[base + 6, here, :]
    total = g[0] + dot3(velocity, g[1:4]) + enthalpy * g[4] + turbulence * g[5]
    pressure = GAMMA_LESS * (shared + speed * g[4])
    carried = speed + wave
    result = [carried * g[0] - total * speed + pressure * kinetic]
    for j in range(3):
        result.append(carried * g[1 + j] + total * normal[j] - pressure * velocity[j])
    result.append(carried * g[4] + pressure)
    result.append(carried * g[5])
    return result


def pull_stage(step, first, last, size, vector, faces, results):
    def body(row):
        here = pl.ds(row, size)
        after = pl.ds(row + step, size)
        g = [vector[k, here, :] - vector[k, after, :] for k in range(6)]
        normal = [faces[FN + j, here, :] for j in range(3)]
        wave = faces[FS, here, :]
        shared = dot3(normal, g[1:4])
        left = side_pullback(faces, here, FL, normal, wave, shared, g)
        right = side_pullback(faces, here, FR, normal, -wave, shared, g)
        wave_bar = faces[FD, here, :] * g[0]
        for k in range(1, 6):
            wave_bar = wave_bar + faces[FD + k, here, :] * g[k]
        for k in range(6):
            if k < 5:
                middle = wave_bar * faces[FM + k, here, :]
                results[GL + k, here, :] = left[k] + middle
                results[GR + k, here, :] = right[k] + middle
            else:
                results[GL + k, here, :] = left[k]
                results[GR + k, here, :] = right[k]
        viscous = faces[FQ, here, :]
        mixed_bar = faces[FE, here, :] * g[1]
        for k in range(1, 5):
            mixed_bar = mixed_bar + faces[FE + k, here, :] * g[1 + k]
        for j in range(3):
            results[PU + j, here, :] = viscous * g[1 + j]
        results[PH, here, :] = viscous * g[4]
        diffused = faces[FK, here, :] * g[5]
        shift = faces[FRH, here, :] * mixed_bar
        results[TL, here, :] = shift + diffused
        results[TR, here, :] = shift - diffused
        results[RB, here, :] = faces[FTH, here, :] * mixed_bar

    blocks(first, last, size, body)


def cells_stage(step, first, last, size, pulls, prims, results, store, extra=None):
    def body(row):
        here = pl.ds(row, size)
        before = pl.ds(row - step, size)
        after = pl.ds(row + step, size)
        twice = pl.ds(row - 2 * step, size)
        outcome = []
        for k in range(6):
            gl, gr = results[GL + k, here, :], results[GR + k, before, :]
            value = gl + gr + pulls[12 + k, here, :] * (gl - gr)
            value = value + pulls[6 + k, before, :] * (
                results[GL + k, before, :] - results[GR + k, twice, :]
            )
            value = value - pulls[k, after, :] * (
                results[GL + k, after, :] - results[GR + k, here, :]
            )
            outcome.append(value)
        velocity_bar = [results[PU + j, here, :] - results[PU + j, before, :] for j in range(3)]
        heat_bar = results[PH, here, :] - results[PH, before, :]
        turbulence_bar = results[TL, here, :] + results[TR, before, :]
        density_bar = results[RB, here, :] + results[RB, before, :]
        inverse = prims[0, here, :]
        velocity = [prims[1 + j, here, :] for j in range(3)]
        if extra is not None:
            velocity_bar, turbulence_bar, density_bar = extra(
                row, velocity, velocity_bar, turbulence_bar, density_bar
            )
        kinetic_bar = HEAT_K * heat_bar
        energy_bar = HEAT_E * heat_bar
        velocity_bar = [velocity_bar[j] + kinetic_bar * velocity[j] for j in range(3)]
        scaled = (
            dot3(velocity_bar, velocity)
            + energy_bar * prims[5, here, :]
            + turbulence_bar * prims[4, here, :]
        )
        outcome[0] = outcome[0] + density_bar - scaled * inverse
        for j in range(3):
            outcome[1 + j] = outcome[1 + j] + velocity_bar[j] * inverse
        outcome[4] = outcome[4] + energy_bar * inverse
        outcome[5] = outcome[5] + turbulence_bar * inverse
        store(row, outcome)

    blocks(first, last, size, body)


def kernel(
    chord_count, span_count, entries,
    flow, offset, wall, codes, cost, basis, hessenberg,
    wu, wd, wv, cu, cd, cv, su, sd, sv, halves,
    col_pulls, col_prims, col_faces, chord_pulls, chord_prims, chord_faces,
    span_pulls, span_prims, span_faces, results, source, signs, col_out, chord_out, span_out,
    mapped, span_sums, chord_sums, send_sem, recv_sem, sum_send, sum_recv,
):
    chord_id, span_id = lax.axis_index("chord"), lax.axis_index("span")

    def chord_at(distance):
        return lax.rem(chord_id + (distance + chord_count), chord_count)

    def span_at(distance):
        return lax.rem(span_id + (distance + span_count), span_count)

    barrier = pltpu.get_barrier_semaphore()
    for d in range(1, chord_count):
        pl.semaphore_signal(barrier, inc=1, device_id=(chord_at(d), span_id), device_id_type=pl.DeviceIdType.MESH)
    for d in range(1, span_count):
        pl.semaphore_signal(barrier, inc=1, device_id=(chord_id, span_at(d)), device_id_type=pl.DeviceIdType.MESH)

    def to_chord_rows(source_ref, target, count):
        def body(k, carry):
            for cell in range(CX):
                base = CHORD_OWN + cell * LAYERS
                target[k, pl.ds(base, 8), :] = source_ref[k, pl.ds(COL_OWN + cell, 8, stride=CX), :]
                target[k, pl.ds(base + 8, 4), :] = source_ref[
                    k, pl.ds(COL_OWN + 8 * CX + cell, 4, stride=CX), :
                ]
            return carry

        lax.fori_loop(0, count, body, 0)

    def to_span_rows(source_ref, target, count):
        def body(k, carry):
            target[k, pl.ds(SPAN_OWN, CY), :] = source_ref[k, pl.ds(COL_OWN, CY), :].T
            return carry

        lax.fori_loop(0, count, body, 0)

    started = []

    def exchange(slot, ref, chordwise, depth):
        if chordwise:
            rows = 40 if depth == 3 else 24
            tail = CHORD_OWN + ROWS - rows
            moves = (
                (tail, CHORD_OWN - rows, (chord_at(1), span_id)),
                (CHORD_OWN, CHORD_OWN + ROWS, (chord_at(-1), span_id)),
            )
        else:
            rows = 8
            moves = (
                (SPAN_OWN + CY - rows, SPAN_OWN - rows, (chord_id, span_at(1))),
                (SPAN_OWN, SPAN_OWN + CY, (chord_id, span_at(-1))),
            )
        copies = []
        for side, (first, landing, target) in enumerate(moves):
            copy = pltpu.make_async_remote_copy(
                src_ref=ref.at[:, pl.ds(first, rows), :],
                dst_ref=ref.at[:, pl.ds(landing, rows), :],
                send_sem=send_sem.at[slot, side],
                recv_sem=recv_sem.at[slot, side],
                device_id=target,
                device_id_type=pl.DeviceIdType.MESH,
            )
            copy.start()
            copies.append(copy)
        started.extend(copies)
        return copies

    def arrive(copies):
        for copy in copies:
            copy.wait_recv()

    own = pl.ds(COL_OWN, ROWS)
    code = codes[...]
    for k in range(6):
        near, far = flow[k, 0:8, :], flow[k, 8:16, :]
        sign = jnp.where(code == 0, SLIP_SIGNS[k], jnp.where(code == 1, WALL_SIGNS[k], 0.0))
        level = jnp.where((code == 0) | (code == 1), 0.0, FREESTREAM[k])
        signs[k] = sign
        wu[k, 0:16, :] = jnp.full((16, CY), FREESTREAM[k], jnp.float32)
        wu[k, 16:24, :] = sign * far + level
        wu[k, 24:32, :] = sign * near + level
        wu[k, own, :] = flow[k]
        wu[k, 128:160, :] = jnp.full((32, CY), FREESTREAM[k], jnp.float32)
        wv[0, k, 0:32, :] = jnp.zeros((32, CY), jnp.float32)
        wv[0, k, own, :] = 0.5 * cost[k]
        wv[0, k, 128:160, :] = jnp.zeros((32, CY), jnp.float32)
        wv[1, k, 0:32, :] = jnp.zeros((32, CY), jnp.float32)
        wv[1, k, 128:160, :] = jnp.zeros((32, CY), jnp.float32)
    for j in range(3):
        near, far, top = offset[j, 0:8, :], offset[j, 8:16, :], offset[j, 88:96, :]
        wd[j, 0:8, :] = far
        wd[j, 8:16, :] = far
        wd[j, 16:24, :] = far
        wd[j, 24:32, :] = near
        wd[j, own, :] = offset[j]
        for layer in range(4):
            wd[j, 128 + 8 * layer : 136 + 8 * layer, :] = top

    to_chord_rows(wu, cu, 6)
    to_span_rows(wu, su, 6)
    to_chord_rows(wd, cd, 3)
    to_span_rows(wd, sd, 3)
    to_chord_rows(wv.at[0], cv.at[0], 6)
    to_span_rows(wv.at[0], sv.at[0], 6)

    pl.semaphore_wait(barrier, chord_count + span_count - 2)
    chord_flow = exchange(0, cu, True, 3)
    span_flow = exchange(1, su, False, 3)
    chord_offset = exchange(2, cd, True, 2)
    span_offset = exchange(3, sd, False, 2)
    chord_vector = exchange(4, cv.at[0], True, 2)
    span_vector = exchange(5, sv.at[0], False, 2)

    def source_body(row):
        here = pl.ds(row, 16)
        cells = pl.ds(row + COL_OWN, 16)
        density = wu[0, cells, :]
        inverse = 1.0 / density
        velocity = [wu[1 + j, cells, :] * inverse for j in range(3)]
        turbulence = wu[5, cells, :] * inverse
        near = 1.0 / wall[here, :]
        square = dot3(velocity, velocity) + 0.01
        root_inverse = lax.rsqrt(square)
        slope = CB_ONE * near
        shear = slope * (square * root_inverse)
        decay = CW_ONE * turbulence * near * near
        source[0, here, :] = -2.0 * turbulence * (shear - decay)
        source[1, here, :] = -2.0 * density * (shear - 2.0 * decay)
        source[2, here, :] = -2.0 * density * turbulence * slope * root_inverse

    blocks(0, ROWS, 16, source_body)

    def column_ready():
        slopes_stage(COL_STEP, 16, 144, 16, wu, halves, col_pulls, col_prims)
        faces_stage(COL_STEP, 2, 24, 136, 16, wu, wd, halves, col_prims, col_faces)
        for k in range(6):
            col_pulls[6 + k, 8:16, :] = jnp.zeros((8, CY), jnp.float32)

    def column_product(vector):
        for slot in range(RESULT_COUNT):
            results[slot, 0:24, :] = jnp.zeros((24, CY), jnp.float32)
        pull_stage(COL_STEP, 24, 136, 16, vector, col_faces, results)

        def ghost_store(row, outcome):
            for k in range(6):
                col_out[k, pl.ds(row, 16), :] = outcome[k]

        def with_source(row, velocity, velocity_bar, turbulence_bar, density_bar):
            here = pl.ds(pl.multiple_of(row - COL_OWN, 8), 16)
            value = vector[5, pl.ds(row, 16), :]
            pulled = source[2, here, :] * value
            return (
                [velocity_bar[j] + pulled * velocity[j] for j in range(3)],
                turbulence_bar + source[1, here, :] * value,
                density_bar + source[0, here, :] * value,
            )

        cells_stage(COL_STEP, 16, 32, 16, col_pulls, col_prims, results, ghost_store)
        cells_stage(COL_STEP, 32, 128, 16, col_pulls, col_prims, results, ghost_store, with_source)
        for k in range(6):
            sign = signs[k]
            col_out[k, 32:40, :] = col_out[k, 32:40, :] + sign * col_out[k, 24:32, :]
            col_out[k, 40:48, :] = col_out[k, 40:48, :] + sign * col_out[k, 16:24, :]

    def span_ready():
        slopes_stage(SPAN_STEP, 8, 152, 16, su, halves, span_pulls, span_prims)
        faces_stage(SPAN_STEP, 1, 8, 152, 16, su, sd, halves, span_prims, span_faces)

    def span_product(vector):
        pull_stage(SPAN_STEP, 8, 152, 16, vector, span_faces, results)

        def store(row, outcome):
            for k in range(6):
                span_out[k, pl.ds(pl.multiple_of(row - SPAN_OWN, 8), 16), :] = outcome[k]

        cells_stage(SPAN_STEP, 16, 144, 16, span_pulls, span_prims, results, store)

    def chord_ready():
        slopes_stage(CHORD_STEP, 16, 160, 16, cu, halves, chord_pulls, chord_prims)
        faces_stage(CHORD_STEP, 0, 16, 160, 16, cu, cd, halves, chord_prims, chord_faces)

    def chord_product(vector):
        pull_stage(CHORD_STEP, 16, 160, 16, vector, chord_faces, results)

        def store(row, outcome):
            for k in range(6):
                chord_out[k, pl.ds(pl.multiple_of(row - CHORD_OWN, 8), 16), :] = outcome[k]

        cells_stage(CHORD_STEP, 40, 136, 16, chord_pulls, chord_prims, results, store)

    def combine(target, halved):
        def body(k, carry):
            turned = span_out[k].T
            for layer in range(LAYERS):
                rows = slice(layer * CX, layer * CX + CX)
                value = turned[rows, :] + col_out[k, COL_OWN + layer * CX : COL_OWN + layer * CX + CX, :]
                value = value + chord_out[k, pl.ds(layer, CX, stride=LAYERS), :]
                mapped[target, k, rows, :] = value
                if halved:
                    wv[1, k, COL_OWN + layer * CX : COL_OWN + layer * CX + CX, :] = 0.5 * value
            return carry

        lax.fori_loop(0, 6, body, 0)

    column_ready()
    column_product(wv.at[0])
    arrive(span_flow + span_offset)
    span_ready()
    arrive(span_vector)
    span_product(sv.at[0])
    arrive(chord_flow + chord_offset)
    chord_ready()
    arrive(chord_vector)
    chord_product(cv.at[0])
    combine(0, True)

    to_chord_rows(wv.at[1], cv.at[1], 6)
    chord_vector = exchange(6, cv.at[1], True, 2)
    to_span_rows(wv.at[1], sv.at[1], 6)
    span_vector = exchange(7, sv.at[1], False, 2)

    def inner(pairs):
        def body(k, sums):
            sums = list(sums)
            for layer in range(LAYERS):
                rows = slice(layer * CX, layer * CX + CX)
                values = [cost[k, rows, :], mapped[0, k, rows, :], mapped[1, k, rows, :]]
                for index, (one, two) in enumerate(pairs):
                    sums[index] = sums[index] + values[one] * values[two]
            return tuple(sums)

        return lax.fori_loop(0, 6, body, tuple(jnp.zeros((CX, CY), jnp.float32) for _ in pairs))

    first_sums = inner(((0, 0), (0, 1), (1, 1)))
    column_product(wv.at[1])
    arrive(span_vector)
    span_product(sv.at[1])
    arrive(chord_vector)
    chord_product(cv.at[1])
    combine(1, False)
    second_sums = inner(((0, 2), (1, 2), (2, 2)))

    row_of = lax.broadcasted_iota(jnp.int32, (8, CY), 0)
    packed = jnp.zeros((8, CY), jnp.float32)
    for index, value in enumerate(first_sums + second_sums):
        packed = jnp.where(row_of == index, jnp.sum(value, axis=0, keepdims=True), packed)

    def total_over(value, buffer, count, me, at, first_slot):
        buffer[me] = value
        copies = []
        for d in range(1, count):
            copy = pltpu.make_async_remote_copy(
                src_ref=buffer.at[me],
                dst_ref=buffer.at[me],
                send_sem=sum_send.at[first_slot + d],
                recv_sem=sum_recv.at[first_slot + d],
                device_id=at(d),
                device_id_type=pl.DeviceIdType.MESH,
            )
            copy.start()
            copies.append(copy)
        started.extend(copies)
        arrive(copies)
        total = buffer[0]
        for index in range(1, count):
            total = total + buffer[index]
        return total

    packed = total_over(packed, span_sums, span_count, span_id, lambda d: (chord_id, span_at(d)), 0)
    packed = total_over(packed, chord_sums, chord_count, chord_id, lambda d: (chord_at(d), span_id), span_count)
    means = jnp.sum(packed, axis=1, keepdims=True) * (1.0 / entries)
    means = jnp.broadcast_to(means, (8, CY))
    cc, cm, mm, cn, mn, nn = [means[index : index + 1, :] for index in range(6)]

    scale = lax.rsqrt(cc + NORM_EPS)
    h11 = cm * scale * scale
    fresh = jnp.maximum(mm - 2.0 * h11 * cm + h11 * h11 * cc, 0.0)
    square = fresh * scale * scale + NORM_EPS
    inverse = lax.rsqrt(square)
    h21 = square * inverse
    gain = scale * inverse
    h12 = gain * scale * (cn - h11 * cm)
    h22 = gain * gain * (mn - h11 * cn - h11 * mm + h11 * h11 * cm)
    along_m = -gain * (h11 + h22)
    along_c = h22 * gain * h11 - h12 * scale
    fresh = (
        gain * gain * nn + along_m * along_m * mm + along_c * along_c * cc
        + 2.0 * (gain * along_m * mn + gain * along_c * cn + along_m * along_c * cm)
    )
    square = jnp.maximum(fresh, 0.0) + NORM_EPS
    inverse = lax.rsqrt(square)
    h32 = square * inverse
    factors = [jnp.broadcast_to(f * inverse, (CX, CY)) for f in (along_c, along_m, gain)]
    entries_out = jnp.zeros((8, CY), jnp.float32)
    for index, value in enumerate((h11, h21, h12, h22, h32)):
        entries_out = jnp.where(row_of == index, value, entries_out)
    hessenberg[...] = entries_out

    def final_body(k, carry):
        for layer in range(LAYERS):
            rows = slice(layer * CX, layer * CX + CX)
            basis[k, rows, :] = (
                factors[0] * cost[k, rows, :]
                + factors[1] * mapped[0, k, rows, :]
                + factors[2] * mapped[1, k, rows, :]
            )
        return carry

    lax.fori_loop(0, 6, final_body, 0)
    for copy in started:
        copy.wait_send()


def on_device(chord_count, span_count, flow_state, displacement, wall_distance, face_codes, cost_gradient):
    entries = float(cost_gradient.size * chord_count * span_count)

    def vmem(*shape):
        return pltpu.VMEM(shape, jnp.float32)

    whole = pl.BlockSpec(memory_space=pltpu.VMEM)
    basis, table = pl.pallas_call(
        functools.partial(kernel, chord_count, span_count, entries),
        out_shape=(
            jax.ShapeDtypeStruct((6, ROWS, CY), jnp.float32),
            jax.ShapeDtypeStruct((8, CY), jnp.float32),
        ),
        in_specs=[whole] * 5,
        out_specs=(whole, whole),
        scratch_shapes=[
            vmem(6, COL_ROWS, CY), vmem(3, COL_ROWS, CY), vmem(2, 6, COL_ROWS, CY),
            vmem(6, CHORD_ROWS, CY), vmem(3, CHORD_ROWS, CY), vmem(2, 6, CHORD_ROWS, CY),
            vmem(6, SPAN_ROWS, CY), vmem(3, SPAN_ROWS, CY), vmem(2, 6, SPAN_ROWS, CY),
            vmem(12, CHORD_ROWS, CY),
            vmem(18, COL_ROWS, CY), vmem(6, COL_ROWS, CY), vmem(FACE_COUNT, COL_ROWS, CY),
            vmem(18, CHORD_ROWS, CY), vmem(6, CHORD_ROWS, CY), vmem(FACE_COUNT, CHORD_ROWS, CY),
            vmem(18, SPAN_ROWS, CY), vmem(6, SPAN_ROWS, CY), vmem(FACE_COUNT, SPAN_ROWS, CY),
            vmem(RESULT_COUNT, CHORD_ROWS, CY), vmem(3, ROWS, CY), vmem(6, CX, CY),
            vmem(6, COL_ROWS, CY), vmem(6, ROWS, CY), vmem(6, CY, CY),
            vmem(2, 6, ROWS, CY), vmem(span_count, 8, CY), vmem(chord_count, 8, CY),
            pltpu.SemaphoreType.DMA((8, 2)), pltpu.SemaphoreType.DMA((8, 2)),
            pltpu.SemaphoreType.DMA((span_count + chord_count,)),
            pltpu.SemaphoreType.DMA((span_count + chord_count,)),
        ],
        compiler_params=pltpu.CompilerParams(
            collective_id=0, has_side_effects=True, vmem_limit_bytes=48 * 1024 * 1024
        ),
        name="arnoldi",
    )(
        flow_state.reshape(6, ROWS, CY),
        displacement.reshape(3, ROWS, CY),
        wall_distance.reshape(ROWS, CY),
        face_codes,
        cost_gradient.reshape(6, ROWS, CY),
    )
    return basis.reshape(cost_gradient.shape), table[:5, 0]


def solution(mesh):
    return jax.shard_map(
        functools.partial(on_device, mesh.shape["chord"], mesh.shape["span"]),
        mesh=mesh,
        in_specs=(
            P(None, None, "chord", "span"),
            P(None, None, "chord", "span"),
            P(None, "chord", "span"),
            P("chord", "span"),
            P(None, None, "chord", "span"),
        ),
        out_specs=(P(None, None, "chord", "span"), P()),
        check_vma=False,
    )
```

```python
import functools

import jax
import jax.numpy as jnp
from jax import lax
from jax.experimental import pallas as pl
from jax.experimental.pallas import tpu as pltpu
from jax.sharding import PartitionSpec as P

HEAT_RATIO = 1.4
GAMMA_LESS = 0.4
VISCOSITY = 0.2
HEAT_FACTOR = 1.4 / (0.4 * 0.72)
CB_ONE = 0.1355
CW_ONE = 3.239
CV_CUBE = 7.1 * 7.1 * 7.1
TURB_SIGMA = 2.0 / 3.0
LIMIT_EPS = 0.01
NORM_EPS = 1e-06
FREESTREAM = (1.0, 0.2, 0.0, 0.05, 2.5, 0.1)
SLIP_SIGNS = (1.0, 1.0, 1.0, -1.0, 1.0, 1.0)
WALL_SIGNS = (1.0, -1.0, -1.0, -1.0, 1.0, -1.0)

HEAT_E = GAMMA_LESS * HEAT_FACTOR
HEAT_K = 1.0 - GAMMA_LESS * HEAT_FACTOR
CUBE_SHIFT = VISCOSITY * VISCOSITY * VISCOSITY * CV_CUBE

LAYERS, CX, CY = 12, 8, 128
ROWS = LAYERS * CX

COL_STEP, COL_OWN, COL_ROWS = 8, 32, 160
CHORD_STEP, CHORD_OWN, CHORD_ROWS = 12, 40, 176
SPAN_STEP, SPAN_OWN, SPAN_ROWS = 1, 16, 160

FL, FR, FN, FD, FM, FS, FQ, FK, FE, FRH, FTH = 0, 7, 14, 17, 23, 28, 29, 30, 31, 36, 37
FACE_COUNT = 38
GL, GR, PU, PH, TL, TR, RB = 0, 6, 12, 15, 16, 17, 18
RESULT_COUNT = 19


def blocks(first, last, size, body, start=0):
    def step(index, carry):
        result = body(pl.multiple_of(first + index * size, 8), carry)
        return carry if result is None else result

    return lax.fori_loop(0, (last - first) // size, step, start)


def dot3(a, b):
    return a[0] * b[0] + a[1] * b[1] + a[2] * b[2]


def primitives(state):
    inverse = 1.0 / state[0]
    velocity = [state[1 + j] * inverse for j in range(3)]
    return inverse, velocity, state[5] * inverse, state[4] * inverse


def slopes_stage(step, first, last, size, window, halves, pulls, prims):
    def body(row, carry):
        here_all = []
        for k in range(6):
            before = window[k, pl.ds(row - step, size), :]
            here = window[k, pl.ds(row, size), :]
            after = window[k, pl.ds(row + step, size), :]
            p = here - before
            q = after - here
            pp = p * p + LIMIT_EPS
            qq = q * q + LIMIT_EPS
            inverse = 1.0 / (pp + qq)
            slope = (qq * p + pp * q) * inverse
            half_inverse = 0.5 * inverse
            a = (qq + 2.0 * p * (q - slope)) * half_inverse
            b = (pp + 2.0 * q * (p - slope)) * half_inverse
            rows = pl.ds(row, size)
            halves[k, rows, :] = here + 0.5 * slope
            halves[6 + k, rows, :] = here - 0.5 * slope
            pulls[k, rows, :] = a
            pulls[6 + k, rows, :] = b
            pulls[12 + k, rows, :] = a - b
            here_all.append(here)
        inverse, velocity, turbulence, specific = primitives(here_all)
        rows = pl.ds(row, size)
        prims[0, rows, :] = inverse
        for j in range(3):
            prims[1 + j, rows, :] = velocity[j]
        prims[4, rows, :] = turbulence
        prims[5, rows, :] = specific

    blocks(first, last, size, body)


def side_coefficients(state, normal):
    inverse, velocity, turbulence, specific = primitives(state)
    kinetic = 0.5 * dot3(velocity, velocity)
    pressure_ratio = GAMMA_LESS * (specific - kinetic)
    return velocity + [kinetic, specific + pressure_ratio, turbulence, dot3(velocity, normal)]


def faces_stage(step, direction, first, last, size, window, offsets, halves, prims, faces):
    def body(row, carry):
        here = pl.ds(row, size)
        after = pl.ds(row + step, size)
        spacing = [offsets[j, after, :] - offsets[j, here, :] for j in range(3)]
        spacing[direction] = spacing[direction] + 1.0
        weight = lax.rsqrt(dot3(spacing, spacing))
        normal = [spacing[j] * weight for j in range(3)]
        left = [halves[k, here, :] for k in range(6)]
        right = [halves[6 + k, after, :] for k in range(6)]
        for slot, value in enumerate(side_coefficients(left, normal)):
            faces[FL + slot, here, :] = value
        for slot, value in enumerate(side_coefficients(right, normal)):
            faces[FR + slot, here, :] = value
        for j in range(3):
            faces[FN + j, here, :] = normal[j]
        for k in range(6):
            faces[FD + k, here, :] = left[k] - right[k]
        middle = [0.5 * (left[k] + right[k]) for k in range(5)] + [left[5]]
        inverse, velocity, unused, specific = primitives(middle)
        kinetic = 0.5 * dot3(velocity, velocity)
        speed = dot3(velocity, normal)
        sound_square = HEAT_RATIO * GAMMA_LESS * (specific - kinetic)
        sound_inverse = lax.rsqrt(sound_square)
        size_speed = jnp.abs(speed)
        sign = jnp.where(speed > 0.0, 1.0, jnp.where(speed < 0.0, -1.0, 0.0))
        half_inverse = 0.5 * inverse
        factor = 0.5 * HEAT_RATIO * GAMMA_LESS * sound_inverse
        faces[FS, here, :] = size_speed + sound_square * sound_inverse
        faces[FM, here, :] = half_inverse * (factor * (2.0 * kinetic - specific) - size_speed)
        for j in range(3):
            faces[FM + 1 + j, here, :] = half_inverse * (sign * normal[j] - factor * velocity[j])
        faces[FM + 4, here, :] = half_inverse * factor
        velocity_l = [prims[1 + j, here, :] for j in range(3)]
        velocity_r = [prims[1 + j, after, :] for j in range(3)]
        jump = [velocity_r[j] - velocity_l[j] for j in range(3)]
        kinetic_jump = 0.5 * (dot3(velocity_r, velocity_r) - dot3(velocity_l, velocity_l))
        heat_jump = HEAT_E * (prims[5, after, :] - prims[5, here, :]) + HEAT_K * kinetic_jump
        turbulence_l, turbulence_r = prims[4, here, :], prims[4, after, :]
        half_density = 0.25 * (window[0, here, :] + window[0, after, :])
        half_turbulence = 0.25 * (turbulence_l + turbulence_r)
        mixed = 4.0 * half_density * half_turbulence
        cube = mixed * mixed * mixed
        ratio = cube / (cube + CUBE_SHIFT)
        twice = 2.0 * weight
        pull = -twice * ratio * (4.0 - 3.0 * ratio)
        faces[FQ, here, :] = twice * (VISCOSITY + mixed * ratio)
        faces[FK, here, :] = (VISCOSITY + mixed) * (twice / TURB_SIGMA)
        for j in range(3):
            faces[FE + j, here, :] = pull * jump[j]
        faces[FE + 3, here, :] = pull * heat_jump
        faces[FE + 4, here, :] = -(twice / TURB_SIGMA) * (turbulence_r - turbulence_l)
        faces[FRH, here, :] = half_density
        faces[FTH, here, :] = half_turbulence

    blocks(first, last, size, body)


def side_pullback(faces, here, base, normal, wave, shared, g):
    velocity = [faces[base + j, here, :] for j in range(3)]
    kinetic = faces[base + 3, here, :]
    enthalpy = faces[base + 4, here, :]
    turbulence = faces[base + 5, here, :]
    speed = faces[base + 6, here, :]
    total = g[0] + dot3(velocity, g[1:4]) + enthalpy * g[4] + turbulence * g[5]
    pressure = GAMMA_LESS * (shared + speed * g[4])
    carried = speed + wave
    result = [carried * g[0] - total * speed + pressure * kinetic]
    for j in range(3):
        result.append(carried * g[1 + j] + total * normal[j] - pressure * velocity[j])
    result.append(carried * g[4] + pressure)
    result.append(carried * g[5])
    return result


def pull_stage(step, first, last, size, vector, faces, results):
    def body(row, carry):
        here = pl.ds(row, size)
        after = pl.ds(row + step, size)
        g = [vector[k, here, :] - vector[k, after, :] for k in range(6)]
        normal = [faces[FN + j, here, :] for j in range(3)]
        wave = faces[FS, here, :]
        shared = dot3(normal, g[1:4])
        left = side_pullback(faces, here, FL, normal, wave, shared, g)
        right = side_pullback(faces, here, FR, normal, -wave, shared, g)
        wave_bar = faces[FD, here, :] * g[0]
        for k in range(1, 6):
            wave_bar = wave_bar + faces[FD + k, here, :] * g[k]
        for k in range(6):
            if k < 5:
                middle = wave_bar * faces[FM + k, here, :]
                results[GL + k, here, :] = left[k] + middle
                results[GR + k, here, :] = right[k] + middle
            else:
                results[GL + k, here, :] = left[k]
                results[GR + k, here, :] = right[k]
        viscous = faces[FQ, here, :]
        mixed_bar = faces[FE, here, :] * g[1]
        for k in range(1, 5):
            mixed_bar = mixed_bar + faces[FE + k, here, :] * g[1 + k]
        for j in range(3):
            results[PU + j, here, :] = viscous * g[1 + j]
        results[PH, here, :] = viscous * g[4]
        diffused = faces[FK, here, :] * g[5]
        shift = faces[FRH, here, :] * mixed_bar
        results[TL, here, :] = shift + diffused
        results[TR, here, :] = shift - diffused
        results[RB, here, :] = faces[FTH, here, :] * mixed_bar

    blocks(first, last, size, body)


def cells_stage(step, first, last, size, pulls, prims, results, store, extra=None, start=0):
    def body(row, carry):
        here = pl.ds(row, size)
        before = pl.ds(row - step, size)
        after = pl.ds(row + step, size)
        twice = pl.ds(row - 2 * step, size)
        outcome = []
        for k in range(6):
            gl, gr = results[GL + k, here, :], results[GR + k, before, :]
            value = gl + gr + pulls[12 + k, here, :] * (gl - gr)
            value = value + pulls[6 + k, before, :] * (
                results[GL + k, before, :] - results[GR + k, twice, :]
            )
            value = value - pulls[k, after, :] * (
                results[GL + k, after, :] - results[GR + k, here, :]
            )
            outcome.append(value)
        velocity_bar = [results[PU + j, here, :] - results[PU + j, before, :] for j in range(3)]
        heat_bar = results[PH, here, :] - results[PH, before, :]
        turbulence_bar = results[TL, here, :] + results[TR, before, :]
        density_bar = results[RB, here, :] + results[RB, before, :]
        inverse = prims[0, here, :]
        velocity = [prims[1 + j, here, :] for j in range(3)]
        if extra is not None:
            velocity_bar, turbulence_bar, density_bar = extra(
                row, velocity, velocity_bar, turbulence_bar, density_bar
            )
        kinetic_bar = HEAT_K * heat_bar
        energy_bar = HEAT_E * heat_bar
        velocity_bar = [velocity_bar[j] + kinetic_bar * velocity[j] for j in range(3)]
        scaled = (
            dot3(velocity_bar, velocity)
            + energy_bar * prims[5, here, :]
            + turbulence_bar * prims[4, here, :]
        )
        outcome[0] = outcome[0] + density_bar - scaled * inverse
        for j in range(3):
            outcome[1 + j] = outcome[1 + j] + velocity_bar[j] * inverse
        outcome[4] = outcome[4] + energy_bar * inverse
        outcome[5] = outcome[5] + turbulence_bar * inverse
        return store(row, outcome, carry)

    return blocks(first, last, size, body, start)


def kernel(
    chord_count, span_count, entries,
    flow_in, offset_in, wall_in, codes_in, cost_in, m_out, n_out, table,
    flow, offset, wall, codes, cost,
    wu, wd, wv, cu, cd, cv, su, sd, sv, halves,
    col_pulls, col_prims, col_faces, chord_pulls, chord_prims, chord_faces,
    span_pulls, span_prims, span_faces, results, source, signs, col_out, span_out,
    plain, partial, last, last_plain, sums, load_sem, keep_sem, send_sem, recv_sem, sum_send, sum_recv, hello,
):
    chord_id, span_id = lax.axis_index("chord"), lax.axis_index("span")
    mesh_ids = pl.DeviceIdType.MESH

    def chord_at(distance):
        return lax.rem(chord_id + (distance + chord_count), chord_count)

    def span_at(distance):
        return lax.rem(span_id + (distance + span_count), span_count)

    barrier = pltpu.get_barrier_semaphore()
    chord_mates = sorted(range(1, chord_count), key=lambda d: min(d, chord_count - d))
    span_mates = sorted(range(1, span_count), key=lambda d: min(d, span_count - d))
    mates = [(chord_at(d), span_id) for d in chord_mates[:2]]
    mates += [(chord_id, span_at(d)) for d in span_mates]
    mates += [(chord_at(d), span_id) for d in chord_mates[2:]]
    for mate in mates[:4]:
        pl.semaphore_signal(barrier, inc=1, device_id=mate, device_id_type=mesh_ids)

    loads = [
        pltpu.make_async_copy(source_ref, target, load_sem.at[index])
        for index, (source_ref, target) in enumerate(
            ((flow_in, flow), (offset_in, offset), (cost_in, cost), (codes_in, codes), (wall_in, wall))
        )
    ]
    for load in loads:
        load.start()
    for mate in mates[4:]:
        pl.semaphore_signal(barrier, inc=1, device_id=mate, device_id_type=mesh_ids)

    def to_chord_rows(source_ref, target, count, first=0, gain=None):
        def body(k, carry):
            for cell in range(CX):
                base = CHORD_OWN + cell * LAYERS
                high = source_ref[k, pl.ds(first + cell, 8, stride=CX), :]
                low = source_ref[k, pl.ds(first + 8 * CX + cell, 4, stride=CX), :]
                target[k, pl.ds(base, 8), :] = high if gain is None else gain * high
                target[k, pl.ds(base + 8, 4), :] = low if gain is None else gain * low
            return carry

        lax.fori_loop(0, count, body, 0)

    def to_span_rows(source_ref, target, count):
        def body(k, carry):
            target[k, pl.ds(SPAN_OWN, CY), :] = source_ref[k, pl.ds(COL_OWN, CY), :].T
            return carry

        lax.fori_loop(0, count, body, 0)

    started = []

    def exchange(slot, ref, chordwise, depth):
        if chordwise:
            rows = 40 if depth == 3 else 24
            tail = CHORD_OWN + ROWS - rows
            moves = (
                (tail, CHORD_OWN - rows, (chord_at(1), span_id)),
                (CHORD_OWN, CHORD_OWN + ROWS, (chord_at(-1), span_id)),
            )
        else:
            rows = 8
            moves = (
                (SPAN_OWN + CY - rows, SPAN_OWN - rows, (chord_id, span_at(1))),
                (SPAN_OWN, SPAN_OWN + CY, (chord_id, span_at(-1))),
            )
        copies = []
        for side, (first, landing, target) in enumerate(moves):
            copy = pltpu.make_async_remote_copy(
                src_ref=ref.at[:, pl.ds(first, rows), :],
                dst_ref=ref.at[:, pl.ds(landing, rows), :],
                send_sem=send_sem.at[slot, side],
                recv_sem=recv_sem.at[slot, side],
                device_id=target,
                device_id_type=mesh_ids,
            )
            copy.start()
            copies.append(copy)
        started.extend(copies)
        return copies

    def arrive(copies):
        for copy in copies:
            copy.wait_recv()

    loads[0].wait()
    to_chord_rows(flow, cu, 6)
    loads[1].wait()
    to_chord_rows(offset, cd, 3)
    loads[2].wait()
    to_chord_rows(cost, cv.at[0], 6, gain=0.5)
    loads[3].wait()
    loads[4].wait()
    pl.semaphore_wait(barrier, len(mates))
    chord_flow = exchange(0, cu, True, 3)
    chord_offset = exchange(2, cd, True, 2)
    chord_vector = exchange(4, cv.at[0], True, 2)
    for d in chord_mates:
        pl.semaphore_signal(hello, inc=1, device_id=(chord_at(d), span_id), device_id_type=mesh_ids)

    own = pl.ds(COL_OWN, ROWS)
    code = codes[...]
    for k in range(6):
        near, far = flow[k, 0:8, :], flow[k, 8:16, :]
        sign = jnp.where(code == 0, SLIP_SIGNS[k], jnp.where(code == 1, WALL_SIGNS[k], 0.0))
        level = jnp.where((code == 0) | (code == 1), 0.0, FREESTREAM[k])
        signs[k] = sign
        wu[k, 0:16, :] = jnp.full((16, CY), FREESTREAM[k], jnp.float32)
        wu[k, 16:24, :] = sign * far + level
        wu[k, 24:32, :] = sign * near + level
        wu[k, own, :] = flow[k]
        wu[k, 128:160, :] = jnp.full((32, CY), FREESTREAM[k], jnp.float32)
        wv[0, k, 0:32, :] = jnp.zeros((32, CY), jnp.float32)
        wv[0, k, own, :] = 0.5 * cost[k]
        wv[0, k, 128:160, :] = jnp.zeros((32, CY), jnp.float32)
        wv[1, k, 0:32, :] = jnp.zeros((32, CY), jnp.float32)
        wv[1, k, 128:160, :] = jnp.zeros((32, CY), jnp.float32)
    for j in range(3):
        near, far, top = offset[j, 0:8, :], offset[j, 8:16, :], offset[j, 88:96, :]
        wd[j, 0:8, :] = far
        wd[j, 8:16, :] = far
        wd[j, 16:24, :] = far
        wd[j, 24:32, :] = near
        wd[j, own, :] = offset[j]
        for layer in range(4):
            wd[j, 128 + 8 * layer : 136 + 8 * layer, :] = top

    to_span_rows(wu, su, 6)
    span_flow = exchange(1, su, False, 3)
    to_span_rows(wd, sd, 3)
    span_offset = exchange(3, sd, False, 2)
    to_span_rows(wv.at[0], sv.at[0], 6)
    span_vector = exchange(5, sv.at[0], False, 2)

    def source_body(row, carry):
        here = pl.ds(row, 16)
        cells = pl.ds(row + COL_OWN, 16)
        density = wu[0, cells, :]
        inverse = 1.0 / density
        velocity = [wu[1 + j, cells, :] * inverse for j in range(3)]
        turbulence = wu[5, cells, :] * inverse
        near = 1.0 / wall[here, :]
        square = dot3(velocity, velocity) + 0.01
        root_inverse = lax.rsqrt(square)
        slope = CB_ONE * near
        shear = slope * (square * root_inverse)
        decay = CW_ONE * turbulence * near * near
        source[0, here, :] = -2.0 * turbulence * (shear - decay)
        source[1, here, :] = -2.0 * density * (shear - 2.0 * decay)
        source[2, here, :] = -2.0 * density * turbulence * slope * root_inverse

    blocks(0, ROWS, 16, source_body)

    def column_ready():
        slopes_stage(COL_STEP, 16, 144, 16, wu, halves, col_pulls, col_prims)
        faces_stage(COL_STEP, 2, 24, 136, 16, wu, wd, halves, col_prims, col_faces)
        for k in range(6):
            col_pulls[6 + k, 8:16, :] = jnp.zeros((8, CY), jnp.float32)

    def column_product(vector):
        for slot in range(RESULT_COUNT):
            results[slot, 0:24, :] = jnp.zeros((24, CY), jnp.float32)
        pull_stage(COL_STEP, 24, 136, 16, vector, col_faces, results)

        def column_store(row, outcome, carry):
            for k in range(6):
                col_out[k, pl.ds(row, 16), :] = outcome[k]

        def with_source(row, velocity, velocity_bar, turbulence_bar, density_bar):
            here = pl.ds(pl.multiple_of(row - COL_OWN, 8), 16)
            value = vector[5, pl.ds(row, 16), :]
            pulled = source[2, here, :] * value
            return (
                [velocity_bar[j] + pulled * velocity[j] for j in range(3)],
                turbulence_bar + source[1, here, :] * value,
                density_bar + source[0, here, :] * value,
            )

        cells_stage(COL_STEP, 16, 32, 16, col_pulls, col_prims, results, column_store)
        cells_stage(COL_STEP, 32, 128, 16, col_pulls, col_prims, results, column_store, with_source)
        for k in range(6):
            sign = signs[k]
            col_out[k, 32:40, :] = col_out[k, 32:40, :] + sign * col_out[k, 24:32, :]
            col_out[k, 40:48, :] = col_out[k, 40:48, :] + sign * col_out[k, 16:24, :]

    def span_ready():
        slopes_stage(SPAN_STEP, 8, 152, 16, su, halves, span_pulls, span_prims)
        faces_stage(SPAN_STEP, 1, 8, 152, 16, su, sd, halves, span_prims, span_faces)

    def span_product(vector):
        pull_stage(SPAN_STEP, 8, 152, 16, vector, span_faces, results)

        def span_store(row, outcome, carry):
            for k in range(6):
                span_out[k, pl.ds(pl.multiple_of(row - SPAN_OWN, 8), 16), :] = outcome[k]

        cells_stage(SPAN_STEP, 16, 144, 16, span_pulls, span_prims, results, span_store)

    def column_and_span():
        def body(k, carry):
            plain[k] = span_out[k].T[0:ROWS, :] + col_out[k, own, :]
            return carry

        lax.fori_loop(0, 6, body, 0)
        to_chord_rows(plain, partial, 6)

    def chord_product(vector, store, start=0):
        pull_stage(CHORD_STEP, 16, 160, 16, vector, chord_faces, results)

        def add_store(row, outcome, carry):
            here = pl.ds(row, 16)
            return store(row, [outcome[k] + partial[k, here, :] for k in range(6)], carry)

        return cells_stage(
            CHORD_STEP, 40, 136, 16, chord_pulls, chord_prims, results, add_store, None, start
        )

    def from_chord_rows(source_ref, target, first):
        def body(k, carry):
            for layer in range(LAYERS):
                rows = pl.ds(CHORD_OWN + layer, CX, stride=LAYERS)
                target[k, pl.ds(first + layer * CX, CX), :] = source_ref[k, rows, :]
            return carry

        lax.fori_loop(0, 6, body, 0)

    column_ready()
    column_product(wv.at[0])
    arrive(span_flow + span_offset)
    span_ready()
    arrive(span_vector)
    span_product(sv.at[0])
    column_and_span()
    arrive(chord_flow)
    slopes_stage(CHORD_STEP, 16, 160, 16, cu, halves, chord_pulls, chord_prims)
    arrive(chord_offset)
    faces_stage(CHORD_STEP, 0, 16, 160, 16, cu, cd, halves, chord_prims, chord_faces)
    arrive(chord_vector)

    def first_store(row, outcome, carry):
        for k in range(6):
            cv[1, k, pl.ds(row, 16), :] = 0.5 * outcome[k]

    chord_product(cv.at[0], first_store)

    chord_vector = exchange(6, cv.at[1], True, 2)
    from_chord_rows(cv.at[1], wv.at[1], COL_OWN)
    to_span_rows(wv.at[1], sv.at[1], 6)
    span_vector = exchange(7, sv.at[1], False, 2)
    nothing = jnp.zeros((16, CY), jnp.float32)

    def first_inner(row, carry):
        cc, cm, mm = carry
        here = pl.ds(row, 16)
        for k in range(6):
            c, m = cv[0, k, here, :], cv[1, k, here, :]
            cc, cm, mm = cc + c * c, cm + c * m, mm + m * m
        return cc, cm, mm

    keep_m = pltpu.make_async_copy(wv.at[1, :, own, :], m_out, keep_sem.at[0])
    keep_m.start()
    first_sums = blocks(40, 136, 16, first_inner, (nothing,) * 3)
    column_product(wv.at[1])
    arrive(span_vector)
    span_product(sv.at[1])
    column_and_span()
    arrive(chord_vector)

    def second_store(row, outcome, carry):
        cn, mn, nn = carry
        here = pl.ds(row, 16)
        for k in range(6):
            n = 0.5 * outcome[k]
            last[k, here, :] = n
            c, m = cv[0, k, here, :], cv[1, k, here, :]
            cn, mn, nn = cn + c * n, mn + m * n, nn + n * n
        return cn, mn, nn

    second_sums = chord_product(cv.at[1], second_store, (nothing,) * 3)

    row_of = lax.broadcasted_iota(jnp.int32, (8, CY), 0)
    lane_of = lax.broadcasted_iota(jnp.int32, (8, CY), 1)
    packed = jnp.zeros((8, CY), jnp.float32)
    for index, value in enumerate(first_sums + second_sums):
        packed = jnp.where(row_of == index, jnp.sum(value, axis=0, keepdims=True), packed)
    packed = jnp.broadcast_to(jnp.sum(packed, axis=1, keepdims=True), (8, CY))
    packed = jnp.where((lane_of >= 16 * row_of) & (lane_of < 16 * row_of + 16), packed, 0.0)
    mine = pl.multiple_of((chord_id * span_count + span_id) * 8, 8)
    sums[pl.ds(mine, 1), :] = jnp.sum(packed, axis=0, keepdims=True)

    pl.semaphore_wait(hello, chord_count - 1)
    copies = []
    for index, (chord_to, span_to) in enumerate(all_partners(chord_count, span_count)):
        copy = pltpu.make_async_remote_copy(
            src_ref=sums.at[pl.ds(mine, 1), :],
            dst_ref=sums.at[pl.ds(mine, 1), :],
            send_sem=sum_send.at[index],
            recv_sem=sum_recv.at[index],
            device_id=(chord_to(chord_id), span_to(span_id)),
            device_id_type=mesh_ids,
        )
        copy.start()
        copies.append(copy)
    started.extend(copies)
    from_chord_rows(last, last_plain, 0)
    keep_n = pltpu.make_async_copy(last_plain, n_out, keep_sem.at[1])
    keep_n.start()
    arrive(copies)
    spread = min(8, chord_count * span_count)
    total = sums[pl.ds(0, spread, stride=8), :]
    for group in range(1, chord_count * span_count // spread):
        total = total + sums[pl.ds(group * 64, spread, stride=8), :]
    total = jnp.sum(total, axis=0, keepdims=True) * (4.0 / entries)
    cc, cm, mm, cn, mn, nn = [
        jnp.broadcast_to(total[:, 16 * index : 16 * index + 1], (1, CY)) for index in range(6)
    ]

    scale = lax.rsqrt(cc + NORM_EPS)
    h11 = cm * scale * scale
    fresh = jnp.maximum(mm - 2.0 * h11 * cm + h11 * h11 * cc, 0.0)
    square = fresh * scale * scale + NORM_EPS
    inverse = lax.rsqrt(square)
    h21 = square * inverse
    gain = scale * inverse
    h12 = gain * scale * (cn - h11 * cm)
    h22 = gain * gain * (mn - h11 * cn - h11 * mm + h11 * h11 * cm)
    along_m = -gain * (h11 + h22)
    along_c = h22 * gain * h11 - h12 * scale
    fresh = (
        gain * gain * nn + along_m * along_m * mm + along_c * along_c * cc
        + 2.0 * (gain * along_m * mn + gain * along_c * cn + along_m * along_c * cm)
    )
    square = jnp.maximum(fresh, 0.0) + NORM_EPS
    inverse = lax.rsqrt(square)
    h32 = square * inverse
    factors = [f * inverse for f in (along_c, 2.0 * along_m, 2.0 * gain)]
    rows_out = jnp.zeros((8, CY), jnp.float32)
    for index, value in enumerate((h11, h21, h12, h22, h32) + tuple(factors)):
        rows_out = jnp.where(row_of == index, value, rows_out)
    table[...] = rows_out
    for copy in started:
        copy.wait_send()
    keep_m.wait()
    keep_n.wait()


def all_partners(chord_count, span_count):
    ys = min(4, chord_count)
    zh = chord_count // ys
    cores = min(2, span_count)
    zl = min(2, span_count // cores)
    xs = span_count // (cores * zl)

    def chord_to(dz, dy):
        return lambda c: lax.rem(lax.div(c, ys) + dz, zh) * ys + lax.rem(c + dy, ys)

    def span_to(dx, dz, dk):
        def place(s):
            x = lax.rem(lax.div(s, zl * cores) + dx, xs)
            z = lax.rem(lax.div(s, cores) + dz, zl)
            return (x * zl + z) * cores + lax.rem(s + dk, cores)

        return place

    found = []
    for high in range(zh):
        for dy in range(ys):
            for dx in range(xs):
                for low in range(zl):
                    for dk in range(cores):
                        hops = min(dy, ys - dy) + min(dx, xs - dx) + (2 if high > low else low)
                        if high + dy + dx + low + dk:
                            found.append((hops, chord_to(high, dy), span_to(dx, low, dk)))
    found.sort(key=lambda entry: -entry[0])
    return [entry[1:] for entry in found]


def final_kernel(
    table_in, cost_in, m_in, n_in, basis_out, hessenberg, cost, m, n, table, basis, load_sem, out_sem
):
    loads = [
        pltpu.make_async_copy(source_ref, target, load_sem.at[index])
        for index, (source_ref, target) in enumerate(
            ((table_in, table), (cost_in, cost), (m_in, m), (n_in, n))
        )
    ]
    for load in loads:
        load.start()
    loads[0].wait()
    factors = [jnp.broadcast_to(table[row : row + 1, :], (ROWS, CY)) for row in (5, 6, 7)]
    for index in range(5):
        hessenberg[index] = table[index, 0]
    for load in loads[1:]:
        load.wait()
    stores = []
    for k in range(6):
        basis[k] = factors[0] * cost[k] + factors[1] * m[k] + factors[2] * n[k]
        store = pltpu.make_async_copy(basis.at[k], basis_out.at[k], out_sem.at[k])
        store.start()
        stores.append(store)
    for store in stores:
        store.wait()


def on_device(chord_count, span_count, flow_state, displacement, wall_distance, face_codes, cost_gradient):
    entries = float(cost_gradient.size * chord_count * span_count)

    def vmem(*shape):
        return pltpu.VMEM(shape, jnp.float32)

    whole = pl.BlockSpec(memory_space=pltpu.VMEM)
    outside = pl.BlockSpec(memory_space=pl.ANY)
    devices = chord_count * span_count
    m, n, table = pl.pallas_call(
        functools.partial(kernel, chord_count, span_count, entries),
        out_shape=(
            jax.ShapeDtypeStruct((6, ROWS, CY), jnp.float32),
            jax.ShapeDtypeStruct((6, ROWS, CY), jnp.float32),
            jax.ShapeDtypeStruct((8, CY), jnp.float32),
        ),
        in_specs=[outside] * 5,
        out_specs=(outside, outside, whole),
        scratch_shapes=[
            vmem(6, ROWS, CY), vmem(3, ROWS, CY), vmem(ROWS, CY), pltpu.VMEM((CX, CY), jnp.int32),
            vmem(6, ROWS, CY),
            vmem(6, COL_ROWS, CY), vmem(3, COL_ROWS, CY), vmem(2, 6, COL_ROWS, CY),
            vmem(6, CHORD_ROWS, CY), vmem(3, CHORD_ROWS, CY), vmem(2, 6, CHORD_ROWS, CY),
            vmem(6, SPAN_ROWS, CY), vmem(3, SPAN_ROWS, CY), vmem(2, 6, SPAN_ROWS, CY),
            vmem(12, CHORD_ROWS, CY),
            vmem(18, COL_ROWS, CY), vmem(6, COL_ROWS, CY), vmem(FACE_COUNT, COL_ROWS, CY),
            vmem(18, CHORD_ROWS, CY), vmem(6, CHORD_ROWS, CY), vmem(FACE_COUNT, CHORD_ROWS, CY),
            vmem(18, SPAN_ROWS, CY), vmem(6, SPAN_ROWS, CY), vmem(FACE_COUNT, SPAN_ROWS, CY),
            vmem(RESULT_COUNT, CHORD_ROWS, CY), vmem(3, ROWS, CY), vmem(6, CX, CY),
            vmem(6, COL_ROWS, CY), vmem(6, CY, CY),
            vmem(6, ROWS, CY), vmem(6, CHORD_ROWS, CY), vmem(6, CHORD_ROWS, CY), vmem(6, ROWS, CY),
            vmem(8 * devices, CY),
            pltpu.SemaphoreType.DMA((5,)), pltpu.SemaphoreType.DMA((2,)),
            pltpu.SemaphoreType.DMA((8, 2)), pltpu.SemaphoreType.DMA((8, 2)),
            pltpu.SemaphoreType.DMA((devices,)), pltpu.SemaphoreType.DMA((devices,)),
            pltpu.SemaphoreType.REGULAR,
        ],
        compiler_params=pltpu.CompilerParams(
            collective_id=0, has_side_effects=True, vmem_limit_bytes=62 * 1024 * 1024
        ),
        name="arnoldi",
    )(
        flow_state.reshape(6, ROWS, CY),
        displacement.reshape(3, ROWS, CY),
        wall_distance.reshape(ROWS, CY),
        face_codes,
        cost_gradient.reshape(6, ROWS, CY),
    )
    basis, hessenberg = pl.pallas_call(
        final_kernel,
        out_shape=(
            jax.ShapeDtypeStruct((6, ROWS, CY), jnp.float32),
            jax.ShapeDtypeStruct((5,), jnp.float32),
        ),
        in_specs=[outside] * 4,
        out_specs=(outside, pl.BlockSpec(memory_space=pltpu.SMEM)),
        scratch_shapes=[
            vmem(6, ROWS, CY), vmem(6, ROWS, CY), vmem(6, ROWS, CY), vmem(8, CY), vmem(6, ROWS, CY),
            pltpu.SemaphoreType.DMA((4,)), pltpu.SemaphoreType.DMA((6,)),
        ],
        compiler_params=pltpu.CompilerParams(vmem_limit_bytes=62 * 1024 * 1024),
        name="combination",
    )(table, cost_gradient.reshape(6, ROWS, CY), m, n)
    return basis.reshape(cost_gradient.shape), hessenberg


def solution(mesh):
    return jax.shard_map(
        functools.partial(on_device, mesh.shape["chord"], mesh.shape["span"]),
        mesh=mesh,
        in_specs=(
            P(None, None, "chord", "span"),
            P(None, None, "chord", "span"),
            P(None, "chord", "span"),
            P("chord", "span"),
            P(None, None, "chord", "span"),
        ),
        out_specs=(P(None, None, "chord", "span"), P()),
        check_vma=False,
    )
```

```python
import functools

import jax
import jax.numpy as jnp
from jax import lax
from jax.experimental import pallas as pl
from jax.experimental.pallas import tpu as pltpu
from jax.sharding import PartitionSpec as P

HEAT_RATIO = 1.4
GAMMA_LESS = 0.4
VISCOSITY = 0.2
HEAT_FACTOR = 1.4 / (0.4 * 0.72)
CB_ONE = 0.1355
CW_ONE = 3.239
CV_CUBE = 7.1 * 7.1 * 7.1
TURB_SIGMA = 2.0 / 3.0
LIMIT_EPS = 0.01
NORM_EPS = 1e-06
FREESTREAM = (1.0, 0.2, 0.0, 0.05, 2.5, 0.1)
SLIP_SIGNS = (1.0, 1.0, 1.0, -1.0, 1.0, 1.0)
WALL_SIGNS = (1.0, -1.0, -1.0, -1.0, 1.0, -1.0)

HEAT_E = GAMMA_LESS * HEAT_FACTOR
HEAT_K = 1.0 - GAMMA_LESS * HEAT_FACTOR
CUBE_SHIFT = VISCOSITY * VISCOSITY * VISCOSITY * CV_CUBE

LAYERS, CX, CY = 12, 8, 128
ROWS = LAYERS * CX

COL_STEP, COL_OWN, COL_ROWS = 8, 32, 160
CHORD_STEP, CHORD_OWN, CHORD_ROWS = 12, 40, 176
SPAN_STEP, SPAN_OWN, SPAN_ROWS = 1, 16, 160

FL, FR, FN, FD, FM, FS, FQ, FK, FE, FRH, FTH = 0, 7, 14, 17, 23, 28, 29, 30, 31, 36, 37
FACE_COUNT = 38
GL, GR, PU, PH, TL, TR, RB = 0, 6, 12, 15, 16, 17, 18
RESULT_COUNT = 19


def blocks(first, last, size, body, start=0, gap=None):
    before = ((gap[0] if gap else last) - first) // size
    after = (last - gap[1]) // size if gap else 0

    def step(index, carry):
        row = first + index * size
        if gap:
            row = row + lax.div(index, before) * (gap[1] - gap[0])
        result = body(pl.multiple_of(row, 8 if first % 8 == 0 else 4), carry)
        return carry if result is None else result

    return lax.fori_loop(0, before + after, step, start)


def dot3(a, b):
    return a[0] * b[0] + a[1] * b[1] + a[2] * b[2]


def primitives(state):
    inverse = 1.0 / state[0]
    velocity = [state[1 + j] * inverse for j in range(3)]
    return inverse, velocity, state[5] * inverse, state[4] * inverse


def slopes_stage(step, first, last, size, window, halves, pulls, prims):
    def body(row, carry):
        here_all = []
        for k in range(6):
            before = window[k, pl.ds(row - step, size), :]
            here = window[k, pl.ds(row, size), :]
            after = window[k, pl.ds(row + step, size), :]
            p = here - before
            q = after - here
            pp = p * p + LIMIT_EPS
            qq = q * q + LIMIT_EPS
            inverse = 1.0 / (pp + qq)
            slope = (qq * p + pp * q) * inverse
            half_inverse = 0.5 * inverse
            a = (qq + 2.0 * p * (q - slope)) * half_inverse
            b = (pp + 2.0 * q * (p - slope)) * half_inverse
            rows = pl.ds(row, size)
            halves[k, rows, :] = here + 0.5 * slope
            halves[6 + k, rows, :] = here - 0.5 * slope
            pulls[k, rows, :] = a
            pulls[6 + k, rows, :] = b
            pulls[12 + k, rows, :] = a - b
            here_all.append(here)
        inverse, velocity, turbulence, specific = primitives(here_all)
        rows = pl.ds(row, size)
        prims[0, rows, :] = inverse
        for j in range(3):
            prims[1 + j, rows, :] = velocity[j]
        prims[4, rows, :] = turbulence
        prims[5, rows, :] = specific

    blocks(first, last, size, body)


def side_coefficients(state, normal):
    inverse, velocity, turbulence, specific = primitives(state)
    kinetic = 0.5 * dot3(velocity, velocity)
    pressure_ratio = GAMMA_LESS * (specific - kinetic)
    return velocity + [kinetic, specific + pressure_ratio, turbulence, dot3(velocity, normal)]


def faces_stage(step, direction, first, last, size, window, offsets, halves, prims, faces):
    def body(row, carry):
        here = pl.ds(row, size)
        after = pl.ds(row + step, size)
        spacing = [offsets[j, after, :] - offsets[j, here, :] for j in range(3)]
        spacing[direction] = spacing[direction] + 1.0
        weight = lax.rsqrt(dot3(spacing, spacing))
        normal = [spacing[j] * weight for j in range(3)]
        left = [halves[k, here, :] for k in range(6)]
        right = [halves[6 + k, after, :] for k in range(6)]
        for slot, value in enumerate(side_coefficients(left, normal)):
            faces[FL + slot, here, :] = value
        for slot, value in enumerate(side_coefficients(right, normal)):
            faces[FR + slot, here, :] = value
        for j in range(3):
            faces[FN + j, here, :] = normal[j]
        for k in range(6):
            faces[FD + k, here, :] = left[k] - right[k]
        middle = [0.5 * (left[k] + right[k]) for k in range(5)] + [left[5]]
        inverse, velocity, unused, specific = primitives(middle)
        kinetic = 0.5 * dot3(velocity, velocity)
        speed = dot3(velocity, normal)
        sound_square = HEAT_RATIO * GAMMA_LESS * (specific - kinetic)
        sound_inverse = lax.rsqrt(sound_square)
        size_speed = jnp.abs(speed)
        sign = jnp.where(speed > 0.0, 1.0, jnp.where(speed < 0.0, -1.0, 0.0))
        half_inverse = 0.5 * inverse
        factor = 0.5 * HEAT_RATIO * GAMMA_LESS * sound_inverse
        faces[FS, here, :] = size_speed + sound_square * sound_inverse
        faces[FM, here, :] = half_inverse * (factor * (2.0 * kinetic - specific) - size_speed)
        for j in range(3):
            faces[FM + 1 + j, here, :] = half_inverse * (sign * normal[j] - factor * velocity[j])
        faces[FM + 4, here, :] = half_inverse * factor
        velocity_l = [prims[1 + j, here, :] for j in range(3)]
        velocity_r = [prims[1 + j, after, :] for j in range(3)]
        jump = [velocity_r[j] - velocity_l[j] for j in range(3)]
        kinetic_jump = 0.5 * (dot3(velocity_r, velocity_r) - dot3(velocity_l, velocity_l))
        heat_jump = HEAT_E * (prims[5, after, :] - prims[5, here, :]) + HEAT_K * kinetic_jump
        turbulence_l, turbulence_r = prims[4, here, :], prims[4, after, :]
        half_density = 0.25 * (window[0, here, :] + window[0, after, :])
        half_turbulence = 0.25 * (turbulence_l + turbulence_r)
        mixed = 4.0 * half_density * half_turbulence
        cube = mixed * mixed * mixed
        ratio = cube / (cube + CUBE_SHIFT)
        twice = 2.0 * weight
        pull = -twice * ratio * (4.0 - 3.0 * ratio)
        faces[FQ, here, :] = twice * (VISCOSITY + mixed * ratio)
        faces[FK, here, :] = (VISCOSITY + mixed) * (twice / TURB_SIGMA)
        for j in range(3):
            faces[FE + j, here, :] = pull * jump[j]
        faces[FE + 3, here, :] = pull * heat_jump
        faces[FE + 4, here, :] = -(twice / TURB_SIGMA) * (turbulence_r - turbulence_l)
        faces[FRH, here, :] = half_density
        faces[FTH, here, :] = half_turbulence

    blocks(first, last, size, body)


def side_pullback(faces, here, base, normal, wave, shared, g):
    velocity = [faces[base + j, here, :] for j in range(3)]
    kinetic = faces[base + 3, here, :]
    enthalpy = faces[base + 4, here, :]
    turbulence = faces[base + 5, here, :]
    speed = faces[base + 6, here, :]
    total = g[0] + dot3(velocity, g[1:4]) + enthalpy * g[4] + turbulence * g[5]
    pressure = GAMMA_LESS * (shared + speed * g[4])
    carried = speed + wave
    result = [carried * g[0] - total * speed + pressure * kinetic]
    for j in range(3):
        result.append(carried * g[1 + j] + total * normal[j] - pressure * velocity[j])
    result.append(carried * g[4] + pressure)
    result.append(carried * g[5])
    return result


def pull_stage(step, first, last, size, vector, faces, results, gap=None):
    def body(row, carry):
        here = pl.ds(row, size)
        after = pl.ds(row + step, size)
        g = [vector[k, here, :] - vector[k, after, :] for k in range(6)]
        normal = [faces[FN + j, here, :] for j in range(3)]
        wave = faces[FS, here, :]
        shared = dot3(normal, g[1:4])
        left = side_pullback(faces, here, FL, normal, wave, shared, g)
        right = side_pullback(faces, here, FR, normal, -wave, shared, g)
        wave_bar = faces[FD, here, :] * g[0]
        for k in range(1, 6):
            wave_bar = wave_bar + faces[FD + k, here, :] * g[k]
        for k in range(6):
            if k < 5:
                middle = wave_bar * faces[FM + k, here, :]
                results[GL + k, here, :] = left[k] + middle
                results[GR + k, here, :] = right[k] + middle
            else:
                results[GL + k, here, :] = left[k]
                results[GR + k, here, :] = right[k]
        viscous = faces[FQ, here, :]
        mixed_bar = faces[FE, here, :] * g[1]
        for k in range(1, 5):
            mixed_bar = mixed_bar + faces[FE + k, here, :] * g[1 + k]
        for j in range(3):
            results[PU + j, here, :] = viscous * g[1 + j]
        results[PH, here, :] = viscous * g[4]
        diffused = faces[FK, here, :] * g[5]
        shift = faces[FRH, here, :] * mixed_bar
        results[TL, here, :] = shift + diffused
        results[TR, here, :] = shift - diffused
        results[RB, here, :] = faces[FTH, here, :] * mixed_bar

    blocks(first, last, size, body, gap=gap)


def cells_stage(step, first, last, size, pulls, prims, results, store, extra=None, start=0, gap=None):
    def body(row, carry):
        here = pl.ds(row, size)
        before = pl.ds(row - step, size)
        after = pl.ds(row + step, size)
        twice = pl.ds(row - 2 * step, size)
        outcome = []
        for k in range(6):
            gl, gr = results[GL + k, here, :], results[GR + k, before, :]
            value = gl + gr + pulls[12 + k, here, :] * (gl - gr)
            value = value + pulls[6 + k, before, :] * (
                results[GL + k, before, :] - results[GR + k, twice, :]
            )
            value = value - pulls[k, after, :] * (
                results[GL + k, after, :] - results[GR + k, here, :]
            )
            outcome.append(value)
        velocity_bar = [results[PU + j, here, :] - results[PU + j, before, :] for j in range(3)]
        heat_bar = results[PH, here, :] - results[PH, before, :]
        turbulence_bar = results[TL, here, :] + results[TR, before, :]
        density_bar = results[RB, here, :] + results[RB, before, :]
        inverse = prims[0, here, :]
        velocity = [prims[1 + j, here, :] for j in range(3)]
        if extra is not None:
            velocity_bar, turbulence_bar, density_bar = extra(
                row, velocity, velocity_bar, turbulence_bar, density_bar
            )
        kinetic_bar = HEAT_K * heat_bar
        energy_bar = HEAT_E * heat_bar
        velocity_bar = [velocity_bar[j] + kinetic_bar * velocity[j] for j in range(3)]
        scaled = (
            dot3(velocity_bar, velocity)
            + energy_bar * prims[5, here, :]
            + turbulence_bar * prims[4, here, :]
        )
        outcome[0] = outcome[0] + density_bar - scaled * inverse
        for j in range(3):
            outcome[1 + j] = outcome[1 + j] + velocity_bar[j] * inverse
        outcome[4] = outcome[4] + energy_bar * inverse
        outcome[5] = outcome[5] + turbulence_bar * inverse
        return store(row, outcome, carry)

    return blocks(first, last, size, body, start, gap)


def kernel(
    chord_count, span_count, entries,
    flow_in, offset_in, wall_in, codes_in, cost_in, m_out, n_out, table,
    flow, offset, wall, codes, cost,
    wu, wd, wv, cu, cd, cv, su, sd, sv, halves,
    col_pulls, col_prims, col_faces, chord_pulls, chord_prims, chord_faces,
    span_pulls, span_prims, span_faces, results, source, signs, col_out, span_out,
    plain, partial, last, last_plain, sums, others, load_sem, keep_sem, send_sem, recv_sem, sum_send, sum_recv, hello,
):
    chord_id, span_id = lax.axis_index("chord"), lax.axis_index("span")
    mesh_ids = pl.DeviceIdType.MESH

    def chord_at(distance):
        return lax.rem(chord_id + (distance + chord_count), chord_count)

    def span_at(distance):
        return lax.rem(span_id + (distance + span_count), span_count)

    barrier = pltpu.get_barrier_semaphore()
    chord_mates = sorted(range(1, chord_count), key=lambda d: min(d, chord_count - d))
    span_mates = sorted(range(1, span_count), key=lambda d: min(d, span_count - d))
    mates = [(chord_at(d), span_id) for d in chord_mates[:2]]
    mates += [(chord_id, span_at(d)) for d in span_mates]
    mates += [(chord_at(d), span_id) for d in chord_mates[2:]]
    for mate in mates[:4]:
        pl.semaphore_signal(barrier, inc=1, device_id=mate, device_id_type=mesh_ids)

    loads = [
        pltpu.make_async_copy(source_ref, target, load_sem.at[index])
        for index, (source_ref, target) in enumerate(
            ((flow_in, flow), (offset_in, offset), (cost_in, cost), (codes_in, codes), (wall_in, wall))
        )
    ]
    for load in loads:
        load.start()
    for mate in mates[4:]:
        pl.semaphore_signal(barrier, inc=1, device_id=mate, device_id_type=mesh_ids)

    def to_chord_rows(source_ref, target, count, first=0, gain=None):
        def body(k, carry):
            for cell in range(CX):
                base = CHORD_OWN + cell * LAYERS
                high = source_ref[k, pl.ds(first + cell, 8, stride=CX), :]
                low = source_ref[k, pl.ds(first + 8 * CX + cell, 4, stride=CX), :]
                target[k, pl.ds(base, 8), :] = high if gain is None else gain * high
                target[k, pl.ds(base + 8, 4), :] = low if gain is None else gain * low
            return carry

        lax.fori_loop(0, count, body, 0)

    def to_span_rows(source_ref, target, count):
        def body(k, carry):
            target[k, pl.ds(SPAN_OWN, CY), :] = source_ref[k, pl.ds(COL_OWN, CY), :].T
            return carry

        lax.fori_loop(0, count, body, 0, unroll=count)

    started = []

    def exchange(slot, ref, chordwise, depth):
        if chordwise:
            rows = 40 if depth == 3 else 24
            tail = CHORD_OWN + ROWS - rows
            moves = (
                (tail, CHORD_OWN - rows, (chord_at(1), span_id)),
                (CHORD_OWN, CHORD_OWN + ROWS, (chord_at(-1), span_id)),
            )
        else:
            rows = 8
            moves = (
                (SPAN_OWN + CY - rows, SPAN_OWN - rows, (chord_id, span_at(1))),
                (SPAN_OWN, SPAN_OWN + CY, (chord_id, span_at(-1))),
            )
        copies = []
        for side, (first, landing, target) in enumerate(moves):
            copy = pltpu.make_async_remote_copy(
                src_ref=ref.at[:, pl.ds(first, rows), :],
                dst_ref=ref.at[:, pl.ds(landing, rows), :],
                send_sem=send_sem.at[slot, side],
                recv_sem=recv_sem.at[slot, side],
                device_id=target,
                device_id_type=mesh_ids,
            )
            copy.start()
            copies.append(copy)
        started.extend(copies)
        return copies

    def arrive(copies):
        for copy in copies:
            copy.wait_recv()

    loads[0].wait()
    to_chord_rows(flow, cu, 6)
    pl.semaphore_wait(barrier, len(mates))
    chord_flow = exchange(0, cu, True, 3)
    loads[1].wait()
    to_chord_rows(offset, cd, 3)
    chord_offset = exchange(2, cd, True, 2)
    loads[2].wait()
    to_chord_rows(cost, cv.at[0], 6, gain=0.5)
    chord_vector = exchange(4, cv.at[0], True, 2)
    loads[3].wait()
    loads[4].wait()
    for d in chord_mates:
        pl.semaphore_signal(hello, inc=1, device_id=(chord_at(d), span_id), device_id_type=mesh_ids)

    own = pl.ds(COL_OWN, ROWS)
    code = codes[...]
    for k in range(6):
        near, far = flow[k, 0:8, :], flow[k, 8:16, :]
        sign = jnp.where(code == 0, SLIP_SIGNS[k], jnp.where(code == 1, WALL_SIGNS[k], 0.0))
        level = jnp.where((code == 0) | (code == 1), 0.0, FREESTREAM[k])
        signs[k] = sign
        wu[k, 0:16, :] = jnp.full((16, CY), FREESTREAM[k], jnp.float32)
        wu[k, 16:24, :] = sign * far + level
        wu[k, 24:32, :] = sign * near + level
        wu[k, own, :] = flow[k]
        wu[k, 128:160, :] = jnp.full((32, CY), FREESTREAM[k], jnp.float32)
        wv[0, k, 0:32, :] = jnp.zeros((32, CY), jnp.float32)
        wv[0, k, own, :] = 0.5 * cost[k]
        wv[0, k, 128:160, :] = jnp.zeros((32, CY), jnp.float32)
        wv[1, k, 0:32, :] = jnp.zeros((32, CY), jnp.float32)
        wv[1, k, 128:160, :] = jnp.zeros((32, CY), jnp.float32)
    for j in range(3):
        near, far, top = offset[j, 0:8, :], offset[j, 8:16, :], offset[j, 88:96, :]
        wd[j, 0:8, :] = far
        wd[j, 8:16, :] = far
        wd[j, 16:24, :] = far
        wd[j, 24:32, :] = near
        wd[j, own, :] = offset[j]
        for layer in range(4):
            wd[j, 128 + 8 * layer : 136 + 8 * layer, :] = top

    to_span_rows(wu, su, 6)
    span_flow = exchange(1, su, False, 3)
    to_span_rows(wd, sd, 3)
    span_offset = exchange(3, sd, False, 2)
    to_span_rows(wv.at[0], sv.at[0], 6)
    span_vector = exchange(5, sv.at[0], False, 2)

    def source_body(row, carry):
        here = pl.ds(row, 16)
        cells = pl.ds(row + COL_OWN, 16)
        density = wu[0, cells, :]
        inverse = 1.0 / density
        velocity = [wu[1 + j, cells, :] * inverse for j in range(3)]
        turbulence = wu[5, cells, :] * inverse
        near = 1.0 / wall[here, :]
        square = dot3(velocity, velocity) + 0.01
        root_inverse = lax.rsqrt(square)
        slope = CB_ONE * near
        shear = slope * (square * root_inverse)
        decay = CW_ONE * turbulence * near * near
        source[0, here, :] = -2.0 * turbulence * (shear - decay)
        source[1, here, :] = -2.0 * density * (shear - 2.0 * decay)
        source[2, here, :] = -2.0 * density * turbulence * slope * root_inverse

    blocks(0, ROWS, 16, source_body)

    def column_ready():
        slopes_stage(COL_STEP, 16, 144, 16, wu, halves, col_pulls, col_prims)
        faces_stage(COL_STEP, 2, 24, 136, 16, wu, wd, halves, col_prims, col_faces)
        for k in range(6):
            col_pulls[6 + k, 8:16, :] = jnp.zeros((8, CY), jnp.float32)

    def column_product(vector):
        for slot in range(RESULT_COUNT):
            results[slot, 0:24, :] = jnp.zeros((24, CY), jnp.float32)
        pull_stage(COL_STEP, 24, 136, 16, vector, col_faces, results)

        def column_store(row, outcome, carry):
            for k in range(6):
                col_out[k, pl.ds(row, 16), :] = outcome[k]

        def with_source(row, velocity, velocity_bar, turbulence_bar, density_bar):
            here = pl.ds(pl.multiple_of(row - COL_OWN, 8), 16)
            value = vector[5, pl.ds(row, 16), :]
            pulled = source[2, here, :] * value
            return (
                [velocity_bar[j] + pulled * velocity[j] for j in range(3)],
                turbulence_bar + source[1, here, :] * value,
                density_bar + source[0, here, :] * value,
            )

        cells_stage(COL_STEP, 16, 32, 16, col_pulls, col_prims, results, column_store)
        cells_stage(COL_STEP, 32, 128, 16, col_pulls, col_prims, results, column_store, with_source)
        for k in range(6):
            sign = signs[k]
            col_out[k, 32:40, :] = col_out[k, 32:40, :] + sign * col_out[k, 24:32, :]
            col_out[k, 40:48, :] = col_out[k, 40:48, :] + sign * col_out[k, 16:24, :]

    def span_ready():
        slopes_stage(SPAN_STEP, 8, 152, 16, su, halves, span_pulls, span_prims)
        faces_stage(SPAN_STEP, 1, 8, 152, 16, su, sd, halves, span_prims, span_faces)

    def span_product(vector):
        pull_stage(SPAN_STEP, 8, 152, 16, vector, span_faces, results)

        def span_store(row, outcome, carry):
            for k in range(6):
                span_out[k, pl.ds(pl.multiple_of(row - SPAN_OWN, 8), 16), :] = outcome[k]

        cells_stage(SPAN_STEP, 16, 144, 16, span_pulls, span_prims, results, span_store)

    def column_and_span():
        def body(k, carry):
            plain[k] = span_out[k].T[0:ROWS, :] + col_out[k, own, :]
            return carry

        lax.fori_loop(0, 6, body, 0, unroll=6)
        to_chord_rows(plain, partial, 6)

    def chord_product(vector, arrivals, store, start=0):
        def add_store(row, outcome, carry):
            here = pl.ds(row, outcome[0].shape[0])
            return store(row, [outcome[k] + partial[k, here, :] for k in range(6)], carry)

        def some_faces(first, last, size, gap=None):
            pull_stage(CHORD_STEP, first, last, size, vector, chord_faces, results, gap)

        def some_cells(first, last, size, start, gap=None):
            return cells_stage(
                CHORD_STEP, first, last, size, chord_pulls, chord_prims, results, add_store, None, start, gap
            )

        some_faces(40, 120, 16)
        some_faces(116, 124, 8)
        start = some_cells(64, 112, 16, start)
        arrive(arrivals)
        some_faces(16, 152, 16, (48, 120))
        return some_cells(40, 136, 24, start, (64, 112))

    def from_chord_rows(source_ref, target, first):
        def body(k, carry):
            for layer in range(LAYERS):
                rows = pl.ds(CHORD_OWN + layer, CX, stride=LAYERS)
                target[k, pl.ds(first + layer * CX, CX), :] = source_ref[k, rows, :]
            return carry

        lax.fori_loop(0, 6, body, 0)

    column_ready()
    column_product(wv.at[0])
    arrive(span_flow + span_offset)
    span_ready()
    arrive(span_vector)
    span_product(sv.at[0])
    column_and_span()
    arrive(chord_flow)
    slopes_stage(CHORD_STEP, 16, 160, 16, cu, halves, chord_pulls, chord_prims)
    arrive(chord_offset)
    faces_stage(CHORD_STEP, 0, 16, 160, 16, cu, cd, halves, chord_prims, chord_faces)

    def first_store(row, outcome, carry):
        for k in range(6):
            cv[1, k, pl.ds(row, outcome[k].shape[0]), :] = 0.5 * outcome[k]

    chord_product(cv.at[0], chord_vector, first_store)

    chord_vector = exchange(6, cv.at[1], True, 2)
    from_chord_rows(cv.at[1], wv.at[1], COL_OWN)
    to_span_rows(wv.at[1], sv.at[1], 6)
    span_vector = exchange(7, sv.at[1], False, 2)
    nothing = jnp.zeros((8, CY), jnp.float32)

    def add_product(total, one, two):
        product = one * two
        for part in range(0, product.shape[0], 8):
            total = total + product[part : part + 8, :]
        return total

    def first_inner(row, carry):
        cc, cm, mm = carry
        here = pl.ds(row, 16)
        for k in range(6):
            c, m = cv[0, k, here, :], cv[1, k, here, :]
            cc, cm, mm = add_product(cc, c, c), add_product(cm, c, m), add_product(mm, m, m)
        return cc, cm, mm

    row_of = lax.broadcasted_iota(jnp.int32, (8, CY), 0)
    lane_of = lax.broadcasted_iota(jnp.int32, (8, CY), 1)

    def pack(packed, first, values):
        for index, value in enumerate(values):
            packed = jnp.where(row_of == first + index, jnp.sum(value, axis=0, keepdims=True), packed)
        return packed

    keep_m = pltpu.make_async_copy(wv.at[1, :, own, :], m_out, keep_sem.at[0])
    keep_m.start()
    packed = pack(nothing, 0, blocks(40, 136, 16, first_inner, (nothing,) * 3))
    column_product(wv.at[1])
    arrive(span_vector)
    span_product(sv.at[1])
    column_and_span()

    def second_store(row, outcome, carry):
        cn, mn, nn = carry
        here = pl.ds(row, outcome[0].shape[0])
        for k in range(6):
            n = 0.5 * outcome[k]
            last[k, here, :] = n
            c, m = cv[0, k, here, :], cv[1, k, here, :]
            cn, mn, nn = add_product(cn, c, n), add_product(mn, m, n), add_product(nn, n, n)
        return cn, mn, nn

    packed = pack(packed, 3, chord_product(cv.at[1], chord_vector, second_store, (nothing,) * 3))

    packed = jnp.broadcast_to(jnp.sum(packed, axis=1, keepdims=True), (8, CY))
    packed = jnp.where((lane_of >= 16 * row_of) & (lane_of < 16 * row_of + 16), packed, 0.0)
    mine = pl.multiple_of((chord_id * span_count + span_id) * 8, 8)
    sums[pl.ds(mine, 1), :] = jnp.sum(packed, axis=0, keepdims=True)

    pl.semaphore_wait(hello, chord_count - 1)
    for chord_to, span_to in all_partners(chord_count, span_count):
        copy = pltpu.make_async_remote_copy(
            src_ref=sums.at[pl.ds(mine, 1), :],
            dst_ref=sums.at[pl.ds(mine, 1), :],
            send_sem=sum_send,
            recv_sem=sum_recv,
            device_id=(chord_to(chord_id), span_to(span_id)),
            device_id_type=mesh_ids,
        )
        copy.start()
    from_chord_rows(last, last_plain, 0)
    keep_n = pltpu.make_async_copy(last_plain, n_out, keep_sem.at[1])
    keep_n.start()
    pltpu.make_async_copy(others, others, sum_recv).wait()
    spread = min(8, chord_count * span_count)
    total = sums[pl.ds(0, spread, stride=8), :]
    for group in range(1, chord_count * span_count // spread):
        total = total + sums[pl.ds(group * 64, spread, stride=8), :]
    total = jnp.sum(total, axis=0, keepdims=True) * (4.0 / entries)
    cc, cm, mm, cn, mn, nn = [
        jnp.broadcast_to(total[:, 16 * index : 16 * index + 1], (1, CY)) for index in range(6)
    ]

    scale = lax.rsqrt(cc + NORM_EPS)
    h11 = cm * scale * scale
    fresh = jnp.maximum(mm - 2.0 * h11 * cm + h11 * h11 * cc, 0.0)
    square = fresh * scale * scale + NORM_EPS
    inverse = lax.rsqrt(square)
    h21 = square * inverse
    gain = scale * inverse
    h12 = gain * scale * (cn - h11 * cm)
    h22 = gain * gain * (mn - h11 * cn - h11 * mm + h11 * h11 * cm)
    along_m = -gain * (h11 + h22)
    along_c = h22 * gain * h11 - h12 * scale
    fresh = (
        gain * gain * nn + along_m * along_m * mm + along_c * along_c * cc
        + 2.0 * (gain * along_m * mn + gain * along_c * cn + along_m * along_c * cm)
    )
    square = jnp.maximum(fresh, 0.0) + NORM_EPS
    inverse = lax.rsqrt(square)
    h32 = square * inverse
    factors = [f * inverse for f in (along_c, 2.0 * along_m, 2.0 * gain)]
    rows_out = jnp.zeros((8, CY), jnp.float32)
    for index, value in enumerate((h11, h21, h12, h22, h32) + tuple(factors)):
        rows_out = jnp.where(row_of == index, value, rows_out)
    table[...] = rows_out
    pltpu.make_async_copy(others, others, sum_send).wait()
    for copy in started:
        copy.wait_send()
    keep_m.wait()
    keep_n.wait()


def all_partners(chord_count, span_count):
    ys = min(4, chord_count)
    zh = chord_count // ys
    cores = min(2, span_count)
    zl = min(2, span_count // cores)
    xs = span_count // (cores * zl)

    def chord_to(dz, dy):
        return lambda c: lax.rem(lax.div(c, ys) + dz, zh) * ys + lax.rem(c + dy, ys)

    def span_to(dx, dz, dk):
        def place(s):
            x = lax.rem(lax.div(s, zl * cores) + dx, xs)
            z = lax.rem(lax.div(s, cores) + dz, zl)
            return (x * zl + z) * cores + lax.rem(s + dk, cores)

        return place

    found = []
    for high in range(zh):
        for dy in range(ys):
            for dx in range(xs):
                for low in range(zl):
                    for dk in range(cores):
                        hops = min(dy, ys - dy) + min(dx, xs - dx) + (2 if high > low else low)
                        if high + dy + dx + low + dk:
                            found.append((hops, chord_to(high, dy), span_to(dx, low, dk)))
    found.sort(key=lambda entry: -entry[0])
    return [entry[1:] for entry in found]


def final_kernel(
    table_in, cost_in, m_in, n_in, basis_out, hessenberg, cost, m, n, table, basis, table_sem, load_sem, out_sem
):
    first = pltpu.make_async_copy(table_in, table, table_sem)
    first.start()
    loads = []
    for k in range(6):
        for index, (source_ref, target) in enumerate(((cost_in, cost), (m_in, m), (n_in, n))):
            load = pltpu.make_async_copy(source_ref.at[k], target.at[k], load_sem.at[k, index])
            load.start()
            loads.append(load)
    first.wait()
    factors = [jnp.broadcast_to(table[row : row + 1, :], (ROWS, CY)) for row in (5, 6, 7)]
    stores = []
    for k in range(6):
        for load in loads[3 * k : 3 * k + 3]:
            load.wait()
        basis[k] = factors[0] * cost[k] + factors[1] * m[k] + factors[2] * n[k]
        store = pltpu.make_async_copy(basis.at[k], basis_out.at[k], out_sem.at[k])
        store.start()
        stores.append(store)
    for index in range(5):
        hessenberg[index] = table[index, 0]
    for store in stores:
        store.wait()


def on_device(chord_count, span_count, flow_state, displacement, wall_distance, face_codes, cost_gradient):
    entries = float(cost_gradient.size * chord_count * span_count)

    def vmem(*shape):
        return pltpu.VMEM(shape, jnp.float32)

    whole = pl.BlockSpec(memory_space=pltpu.VMEM)
    outside = pl.BlockSpec(memory_space=pl.ANY)
    devices = chord_count * span_count
    m, n, table = pl.pallas_call(
        functools.partial(kernel, chord_count, span_count, entries),
        out_shape=(
            jax.ShapeDtypeStruct((6, ROWS, CY), jnp.float32),
            jax.ShapeDtypeStruct((6, ROWS, CY), jnp.float32),
            jax.ShapeDtypeStruct((8, CY), jnp.float32),
        ),
        in_specs=[outside] * 5,
        out_specs=(outside, outside, whole),
        scratch_shapes=[
            vmem(6, ROWS, CY), vmem(3, ROWS, CY), vmem(ROWS, CY), pltpu.VMEM((CX, CY), jnp.int32),
            vmem(6, ROWS, CY),
            vmem(6, COL_ROWS, CY), vmem(3, COL_ROWS, CY), vmem(2, 6, COL_ROWS, CY),
            vmem(6, CHORD_ROWS, CY), vmem(3, CHORD_ROWS, CY), vmem(2, 6, CHORD_ROWS, CY),
            vmem(6, SPAN_ROWS, CY), vmem(3, SPAN_ROWS, CY), vmem(2, 6, SPAN_ROWS, CY),
            vmem(12, CHORD_ROWS, CY),
            vmem(18, COL_ROWS, CY), vmem(6, COL_ROWS, CY), vmem(FACE_COUNT, COL_ROWS, CY),
            vmem(18, CHORD_ROWS, CY), vmem(6, CHORD_ROWS, CY), vmem(FACE_COUNT, CHORD_ROWS, CY),
            vmem(18, SPAN_ROWS, CY), vmem(6, SPAN_ROWS, CY), vmem(FACE_COUNT, SPAN_ROWS, CY),
            vmem(RESULT_COUNT, CHORD_ROWS, CY), vmem(3, ROWS, CY), vmem(6, CX, CY),
            vmem(6, COL_ROWS, CY), vmem(6, CY, CY),
            vmem(6, ROWS, CY), vmem(6, CHORD_ROWS, CY), vmem(6, CHORD_ROWS, CY), vmem(6, ROWS, CY),
            vmem(8 * devices, CY), vmem(devices - 1, CY),
            pltpu.SemaphoreType.DMA((5,)), pltpu.SemaphoreType.DMA((2,)),
            pltpu.SemaphoreType.DMA((8, 2)), pltpu.SemaphoreType.DMA((8, 2)),
            pltpu.SemaphoreType.DMA, pltpu.SemaphoreType.DMA,
            pltpu.SemaphoreType.REGULAR,
        ],
        compiler_params=pltpu.CompilerParams(
            collective_id=0, has_side_effects=True, vmem_limit_bytes=62 * 1024 * 1024
        ),
        name="arnoldi",
    )(
        flow_state.reshape(6, ROWS, CY),
        displacement.reshape(3, ROWS, CY),
        wall_distance.reshape(ROWS, CY),
        face_codes,
        cost_gradient.reshape(6, ROWS, CY),
    )
    basis, hessenberg = pl.pallas_call(
        final_kernel,
        out_shape=(
            jax.ShapeDtypeStruct((6, ROWS, CY), jnp.float32),
            jax.ShapeDtypeStruct((5,), jnp.float32),
        ),
        in_specs=[outside] * 4,
        out_specs=(outside, pl.BlockSpec(memory_space=pltpu.SMEM)),
        scratch_shapes=[
            vmem(6, ROWS, CY), vmem(6, ROWS, CY), vmem(6, ROWS, CY), vmem(8, CY), vmem(6, ROWS, CY),
            pltpu.SemaphoreType.DMA, pltpu.SemaphoreType.DMA((6, 3)), pltpu.SemaphoreType.DMA((6,)),
        ],
        compiler_params=pltpu.CompilerParams(vmem_limit_bytes=62 * 1024 * 1024),
        name="combination",
    )(table, cost_gradient.reshape(6, ROWS, CY), m, n)
    return basis.reshape(cost_gradient.shape), hessenberg


def solution(mesh):
    return jax.shard_map(
        functools.partial(on_device, mesh.shape["chord"], mesh.shape["span"]),
        mesh=mesh,
        in_specs=(
            P(None, None, "chord", "span"),
            P(None, None, "chord", "span"),
            P(None, "chord", "span"),
            P("chord", "span"),
            P(None, None, "chord", "span"),
        ),
        out_specs=(P(None, None, "chord", "span"), P()),
        check_vma=False,
    )
```

```python
import functools

import jax
import jax.numpy as jnp
from jax import lax
from jax.experimental import pallas as pl
from jax.experimental.pallas import tpu as pltpu
from jax.sharding import PartitionSpec as P

HEAT_RATIO = 1.4
GAMMA_LESS = 0.4
VISCOSITY = 0.2
HEAT_FACTOR = 1.4 / (0.4 * 0.72)
CB_ONE = 0.1355
CW_ONE = 3.239
CV_CUBE = 7.1 * 7.1 * 7.1
TURB_SIGMA = 2.0 / 3.0
LIMIT_EPS = 0.01
NORM_EPS = 1e-06
FREESTREAM = (1.0, 0.2, 0.0, 0.05, 2.5, 0.1)
SLIP_SIGNS = (1.0, 1.0, 1.0, -1.0, 1.0, 1.0)
WALL_SIGNS = (1.0, -1.0, -1.0, -1.0, 1.0, -1.0)

HEAT_E = GAMMA_LESS * HEAT_FACTOR
HEAT_K = 1.0 - GAMMA_LESS * HEAT_FACTOR
CUBE_SHIFT = VISCOSITY * VISCOSITY * VISCOSITY * CV_CUBE

LAYERS, CX, CY = 12, 8, 128
ROWS = LAYERS * CX

COL_STEP, COL_OWN, COL_ROWS = 8, 32, 160
CHORD_STEP, CHORD_OWN, CHORD_ROWS = 12, 40, 176
SPAN_STEP, SPAN_OWN, SPAN_ROWS = 1, 16, 160

FL, FR, FN, FD, FM, FS, FQ, FK, FE, FRH, FTH = 0, 7, 14, 17, 23, 28, 29, 30, 31, 36, 37
FACE_COUNT = 38
GL, GR, PU, PH, TL, TR, RB = 0, 6, 12, 15, 16, 17, 18
RESULT_COUNT = 19


def blocks(first, last, size, body, start=0, gap=None):
    before = ((gap[0] if gap else last) - first) // size
    after = (last - gap[1]) // size if gap else 0

    def step(index, carry):
        row = first + index * size
        if gap:
            row = row + lax.div(index, before) * (gap[1] - gap[0])
        result = body(pl.multiple_of(row, 8 if first % 8 == 0 else 4), carry)
        return carry if result is None else result

    return lax.fori_loop(0, before + after, step, start)


def dot3(a, b):
    return a[0] * b[0] + a[1] * b[1] + a[2] * b[2]


def primitives(state):
    inverse = 1.0 / state[0]
    velocity = [state[1 + j] * inverse for j in range(3)]
    return inverse, velocity, state[5] * inverse, state[4] * inverse


def slopes_stage(step, first, last, size, window, halves, pulls, prims):
    def body(row, carry):
        here_all = []
        for k in range(6):
            before = window[k, pl.ds(row - step, size), :]
            here = window[k, pl.ds(row, size), :]
            after = window[k, pl.ds(row + step, size), :]
            p = here - before
            q = after - here
            pp = p * p + LIMIT_EPS
            qq = q * q + LIMIT_EPS
            inverse = 1.0 / (pp + qq)
            slope = (qq * p + pp * q) * inverse
            half_inverse = 0.5 * inverse
            a = (qq + 2.0 * p * (q - slope)) * half_inverse
            b = (pp + 2.0 * q * (p - slope)) * half_inverse
            rows = pl.ds(row, size)
            halves[k, rows, :] = here + 0.5 * slope
            halves[6 + k, rows, :] = here - 0.5 * slope
            pulls[k, rows, :] = a
            pulls[6 + k, rows, :] = b
            pulls[12 + k, rows, :] = a - b
            here_all.append(here)
        inverse, velocity, turbulence, specific = primitives(here_all)
        rows = pl.ds(row, size)
        prims[0, rows, :] = inverse
        for j in range(3):
            prims[1 + j, rows, :] = velocity[j]
        prims[4, rows, :] = turbulence
        prims[5, rows, :] = specific

    blocks(first, last, size, body)


def side_coefficients(state, normal):
    inverse, velocity, turbulence, specific = primitives(state)
    kinetic = 0.5 * dot3(velocity, velocity)
    pressure_ratio = GAMMA_LESS * (specific - kinetic)
    return velocity + [kinetic, specific + pressure_ratio, turbulence, dot3(velocity, normal)]


def faces_stage(step, direction, first, last, size, window, offsets, halves, prims, faces):
    def body(row, carry):
        here = pl.ds(row, size)
        after = pl.ds(row + step, size)
        spacing = [offsets[j, after, :] - offsets[j, here, :] for j in range(3)]
        spacing[direction] = spacing[direction] + 1.0
        weight = lax.rsqrt(dot3(spacing, spacing))
        normal = [spacing[j] * weight for j in range(3)]
        left = [halves[k, here, :] for k in range(6)]
        right = [halves[6 + k, after, :] for k in range(6)]
        for slot, value in enumerate(side_coefficients(left, normal)):
            faces[FL + slot, here, :] = value
        for slot, value in enumerate(side_coefficients(right, normal)):
            faces[FR + slot, here, :] = value
        for j in range(3):
            faces[FN + j, here, :] = normal[j]
        for k in range(6):
            faces[FD + k, here, :] = left[k] - right[k]
        middle = [0.5 * (left[k] + right[k]) for k in range(5)] + [left[5]]
        inverse, velocity, unused, specific = primitives(middle)
        kinetic = 0.5 * dot3(velocity, velocity)
        speed = dot3(velocity, normal)
        sound_square = HEAT_RATIO * GAMMA_LESS * (specific - kinetic)
        sound_inverse = lax.rsqrt(sound_square)
        size_speed = jnp.abs(speed)
        sign = jnp.where(speed > 0.0, 1.0, jnp.where(speed < 0.0, -1.0, 0.0))
        half_inverse = 0.5 * inverse
        factor = 0.5 * HEAT_RATIO * GAMMA_LESS * sound_inverse
        faces[FS, here, :] = size_speed + sound_square * sound_inverse
        faces[FM, here, :] = half_inverse * (factor * (2.0 * kinetic - specific) - size_speed)
        for j in range(3):
            faces[FM + 1 + j, here, :] = half_inverse * (sign * normal[j] - factor * velocity[j])
        faces[FM + 4, here, :] = half_inverse * factor
        velocity_l = [prims[1 + j, here, :] for j in range(3)]
        velocity_r = [prims[1 + j, after, :] for j in range(3)]
        jump = [velocity_r[j] - velocity_l[j] for j in range(3)]
        kinetic_jump = 0.5 * (dot3(velocity_r, velocity_r) - dot3(velocity_l, velocity_l))
        heat_jump = HEAT_E * (prims[5, after, :] - prims[5, here, :]) + HEAT_K * kinetic_jump
        turbulence_l, turbulence_r = prims[4, here, :], prims[4, after, :]
        half_density = 0.25 * (window[0, here, :] + window[0, after, :])
        half_turbulence = 0.25 * (turbulence_l + turbulence_r)
        mixed = 4.0 * half_density * half_turbulence
        cube = mixed * mixed * mixed
        ratio = cube / (cube + CUBE_SHIFT)
        twice = 2.0 * weight
        pull = -twice * ratio * (4.0 - 3.0 * ratio)
        faces[FQ, here, :] = twice * (VISCOSITY + mixed * ratio)
        faces[FK, here, :] = (VISCOSITY + mixed) * (twice / TURB_SIGMA)
        for j in range(3):
            faces[FE + j, here, :] = pull * jump[j]
        faces[FE + 3, here, :] = pull * heat_jump
        faces[FE + 4, here, :] = -(twice / TURB_SIGMA) * (turbulence_r - turbulence_l)
        faces[FRH, here, :] = half_density
        faces[FTH, here, :] = half_turbulence

    blocks(first, last, size, body)


def side_pullback(faces, here, base, normal, wave, shared, g):
    velocity = [faces[base + j, here, :] for j in range(3)]
    kinetic = faces[base + 3, here, :]
    enthalpy = faces[base + 4, here, :]
    turbulence = faces[base + 5, here, :]
    speed = faces[base + 6, here, :]
    total = g[0] + dot3(velocity, g[1:4]) + enthalpy * g[4] + turbulence * g[5]
    pressure = GAMMA_LESS * (shared + speed * g[4])
    carried = speed + wave
    result = [carried * g[0] - total * speed + pressure * kinetic]
    for j in range(3):
        result.append(carried * g[1 + j] + total * normal[j] - pressure * velocity[j])
    result.append(carried * g[4] + pressure)
    result.append(carried * g[5])
    return result


def pull_stage(step, first, last, size, vector, faces, results, gap=None):
    def body(row, carry):
        here = pl.ds(row, size)
        after = pl.ds(row + step, size)
        g = [vector[k, here, :] - vector[k, after, :] for k in range(6)]
        normal = [faces[FN + j, here, :] for j in range(3)]
        wave = faces[FS, here, :]
        shared = dot3(normal, g[1:4])
        left = side_pullback(faces, here, FL, normal, wave, shared, g)
        right = side_pullback(faces, here, FR, normal, -wave, shared, g)
        wave_bar = faces[FD, here, :] * g[0]
        for k in range(1, 6):
            wave_bar = wave_bar + faces[FD + k, here, :] * g[k]
        for k in range(6):
            if k < 5:
                middle = wave_bar * faces[FM + k, here, :]
                results[GL + k, here, :] = left[k] + middle
                results[GR + k, here, :] = right[k] + middle
            else:
                results[GL + k, here, :] = left[k]
                results[GR + k, here, :] = right[k]
        viscous = faces[FQ, here, :]
        mixed_bar = faces[FE, here, :] * g[1]
        for k in range(1, 5):
            mixed_bar = mixed_bar + faces[FE + k, here, :] * g[1 + k]
        for j in range(3):
            results[PU + j, here, :] = viscous * g[1 + j]
        results[PH, here, :] = viscous * g[4]
        diffused = faces[FK, here, :] * g[5]
        shift = faces[FRH, here, :] * mixed_bar
        results[TL, here, :] = shift + diffused
        results[TR, here, :] = shift - diffused
        results[RB, here, :] = faces[FTH, here, :] * mixed_bar

    blocks(first, last, size, body, gap=gap)


def cells_stage(step, first, last, size, pulls, prims, results, store, extra=None, start=0, gap=None):
    def body(row, carry):
        here = pl.ds(row, size)
        before = pl.ds(row - step, size)
        after = pl.ds(row + step, size)
        twice = pl.ds(row - 2 * step, size)
        outcome = []
        for k in range(6):
            gl, gr = results[GL + k, here, :], results[GR + k, before, :]
            value = gl + gr + pulls[12 + k, here, :] * (gl - gr)
            value = value + pulls[6 + k, before, :] * (
                results[GL + k, before, :] - results[GR + k, twice, :]
            )
            value = value - pulls[k, after, :] * (
                results[GL + k, after, :] - results[GR + k, here, :]
            )
            outcome.append(value)
        velocity_bar = [results[PU + j, here, :] - results[PU + j, before, :] for j in range(3)]
        heat_bar = results[PH, here, :] - results[PH, before, :]
        turbulence_bar = results[TL, here, :] + results[TR, before, :]
        density_bar = results[RB, here, :] + results[RB, before, :]
        inverse = prims[0, here, :]
        velocity = [prims[1 + j, here, :] for j in range(3)]
        if extra is not None:
            velocity_bar, turbulence_bar, density_bar = extra(
                row, velocity, velocity_bar, turbulence_bar, density_bar
            )
        kinetic_bar = HEAT_K * heat_bar
        energy_bar = HEAT_E * heat_bar
        velocity_bar = [velocity_bar[j] + kinetic_bar * velocity[j] for j in range(3)]
        scaled = (
            dot3(velocity_bar, velocity)
            + energy_bar * prims[5, here, :]
            + turbulence_bar * prims[4, here, :]
        )
        outcome[0] = outcome[0] + density_bar - scaled * inverse
        for j in range(3):
            outcome[1 + j] = outcome[1 + j] + velocity_bar[j] * inverse
        outcome[4] = outcome[4] + energy_bar * inverse
        outcome[5] = outcome[5] + turbulence_bar * inverse
        return store(row, outcome, carry)

    return blocks(first, last, size, body, start, gap)


def kernel(
    chord_count, span_count, entries,
    flow_in, offset_in, wall_in, codes_in, cost_in, m_out, n_out, table,
    flow, offset, wall, codes, cost,
    wu, wd, wv, cu, cd, cv, su, sd, sv, halves,
    col_pulls, col_prims, col_faces, chord_pulls, chord_prims, chord_faces,
    span_pulls, span_prims, span_faces, results, source, signs, col_out, span_out,
    plain, partial, last, last_plain, sums, others, load_sem, keep_sem, send_sem, recv_sem, sum_send, sum_recv, hello,
):
    chord_id, span_id = lax.axis_index("chord"), lax.axis_index("span")
    mesh_ids = pl.DeviceIdType.MESH

    def chord_at(distance):
        return lax.rem(chord_id + (distance + chord_count), chord_count)

    def span_at(distance):
        return lax.rem(span_id + (distance + span_count), span_count)

    barrier = pltpu.get_barrier_semaphore()
    chord_mates = sorted(range(1, chord_count), key=lambda d: min(d, chord_count - d))
    span_mates = sorted(range(1, span_count), key=lambda d: min(d, span_count - d))
    mates = [(chord_at(d), span_id) for d in chord_mates[:2]]
    mates += [(chord_id, span_at(d)) for d in span_mates]
    mates += [(chord_at(d), span_id) for d in chord_mates[2:]]
    for mate in mates[:4]:
        pl.semaphore_signal(barrier, inc=1, device_id=mate, device_id_type=mesh_ids)

    loads = [
        pltpu.make_async_copy(source_ref, target, load_sem.at[index])
        for index, (source_ref, target) in enumerate(
            ((flow_in, flow), (offset_in, offset), (cost_in, cost), (codes_in, codes), (wall_in, wall))
        )
    ]
    for load in loads:
        load.start()
    for mate in mates[4:]:
        pl.semaphore_signal(barrier, inc=1, device_id=mate, device_id_type=mesh_ids)

    def to_chord_rows(source_ref, target, count, first=0, gain=None):
        def body(k, carry):
            for cell in range(CX):
                base = CHORD_OWN + cell * LAYERS
                high = source_ref[k, pl.ds(first + cell, 8, stride=CX), :]
                low = source_ref[k, pl.ds(first + 8 * CX + cell, 4, stride=CX), :]
                target[k, pl.ds(base, 8), :] = high if gain is None else gain * high
                target[k, pl.ds(base + 8, 4), :] = low if gain is None else gain * low
            return carry

        lax.fori_loop(0, count, body, 0)

    def to_span_rows(source_ref, target, count):
        def body(k, carry):
            target[k, pl.ds(SPAN_OWN, CY), :] = source_ref[k, pl.ds(COL_OWN, CY), :].T
            return carry

        lax.fori_loop(0, count, body, 0, unroll=count)

    started = []

    def exchange(slot, ref, chordwise, depth):
        if chordwise:
            rows = 40 if depth == 3 else 24
            tail = CHORD_OWN + ROWS - rows
            moves = (
                (tail, CHORD_OWN - rows, (chord_at(1), span_id)),
                (CHORD_OWN, CHORD_OWN + ROWS, (chord_at(-1), span_id)),
            )
        else:
            rows = 8
            moves = (
                (SPAN_OWN + CY - rows, SPAN_OWN - rows, (chord_id, span_at(1))),
                (SPAN_OWN, SPAN_OWN + CY, (chord_id, span_at(-1))),
            )
        copies = []
        for side, (first, landing, target) in enumerate(moves):
            copy = pltpu.make_async_remote_copy(
                src_ref=ref.at[:, pl.ds(first, rows), :],
                dst_ref=ref.at[:, pl.ds(landing, rows), :],
                send_sem=send_sem.at[slot, side],
                recv_sem=recv_sem.at[slot, side],
                device_id=target,
                device_id_type=mesh_ids,
            )
            copy.start()
            copies.append(copy)
        started.extend(copies)
        return copies

    def arrive(copies):
        for copy in copies:
            copy.wait_recv()

    for load in loads:
        load.wait()
    to_chord_rows(flow, cu, 6)
    to_chord_rows(offset, cd, 3)
    to_chord_rows(cost, cv.at[0], 6, gain=0.5)

    own = pl.ds(COL_OWN, ROWS)
    code = codes[...]
    for k in range(6):
        near, far = flow[k, 0:8, :], flow[k, 8:16, :]
        sign = jnp.where(code == 0, SLIP_SIGNS[k], jnp.where(code == 1, WALL_SIGNS[k], 0.0))
        level = jnp.where((code == 0) | (code == 1), 0.0, FREESTREAM[k])
        signs[k] = sign
        wu[k, 0:16, :] = jnp.full((16, CY), FREESTREAM[k], jnp.float32)
        wu[k, 16:24, :] = sign * far + level
        wu[k, 24:32, :] = sign * near + level
        wu[k, own, :] = flow[k]
        wu[k, 128:160, :] = jnp.full((32, CY), FREESTREAM[k], jnp.float32)
        wv[0, k, 0:32, :] = jnp.zeros((32, CY), jnp.float32)
        wv[0, k, own, :] = 0.5 * cost[k]
        wv[0, k, 128:160, :] = jnp.zeros((32, CY), jnp.float32)
        wv[1, k, 0:32, :] = jnp.zeros((32, CY), jnp.float32)
        wv[1, k, 128:160, :] = jnp.zeros((32, CY), jnp.float32)
    for j in range(3):
        near, far, top = offset[j, 0:8, :], offset[j, 8:16, :], offset[j, 88:96, :]
        wd[j, 0:8, :] = far
        wd[j, 8:16, :] = far
        wd[j, 16:24, :] = far
        wd[j, 24:32, :] = near
        wd[j, own, :] = offset[j]
        for layer in range(4):
            wd[j, 128 + 8 * layer : 136 + 8 * layer, :] = top

    to_span_rows(wu, su, 6)
    to_span_rows(wd, sd, 3)
    to_span_rows(wv.at[0], sv.at[0], 6)

    def source_body(row, carry):
        here = pl.ds(row, 16)
        cells = pl.ds(row + COL_OWN, 16)
        density = wu[0, cells, :]
        inverse = 1.0 / density
        velocity = [wu[1 + j, cells, :] * inverse for j in range(3)]
        turbulence = wu[5, cells, :] * inverse
        near = 1.0 / wall[here, :]
        square = dot3(velocity, velocity) + 0.01
        root_inverse = lax.rsqrt(square)
        slope = CB_ONE * near
        shear = slope * (square * root_inverse)
        decay = CW_ONE * turbulence * near * near
        source[0, here, :] = -2.0 * turbulence * (shear - decay)
        source[1, here, :] = -2.0 * density * (shear - 2.0 * decay)
        source[2, here, :] = -2.0 * density * turbulence * slope * root_inverse

    blocks(0, ROWS, 16, source_body)

    def column_ready():
        slopes_stage(COL_STEP, 16, 144, 16, wu, halves, col_pulls, col_prims)
        faces_stage(COL_STEP, 2, 24, 136, 16, wu, wd, halves, col_prims, col_faces)
        for k in range(6):
            col_pulls[6 + k, 8:16, :] = jnp.zeros((8, CY), jnp.float32)

    def column_product(vector):
        for slot in range(RESULT_COUNT):
            results[slot, 0:24, :] = jnp.zeros((24, CY), jnp.float32)
        pull_stage(COL_STEP, 24, 136, 16, vector, col_faces, results)

        def column_store(row, outcome, carry):
            for k in range(6):
                col_out[k, pl.ds(row, 16), :] = outcome[k]

        def with_source(row, velocity, velocity_bar, turbulence_bar, density_bar):
            here = pl.ds(pl.multiple_of(row - COL_OWN, 8), 16)
            value = vector[5, pl.ds(row, 16), :]
            pulled = source[2, here, :] * value
            return (
                [velocity_bar[j] + pulled * velocity[j] for j in range(3)],
                turbulence_bar + source[1, here, :] * value,
                density_bar + source[0, here, :] * value,
            )

        cells_stage(COL_STEP, 16, 32, 16, col_pulls, col_prims, results, column_store)
        cells_stage(COL_STEP, 32, 128, 16, col_pulls, col_prims, results, column_store, with_source)
        for k in range(6):
            sign = signs[k]
            col_out[k, 32:40, :] = col_out[k, 32:40, :] + sign * col_out[k, 24:32, :]
            col_out[k, 40:48, :] = col_out[k, 40:48, :] + sign * col_out[k, 16:24, :]

    def span_ready():
        slopes_stage(SPAN_STEP, 8, 152, 16, su, halves, span_pulls, span_prims)
        faces_stage(SPAN_STEP, 1, 8, 152, 16, su, sd, halves, span_prims, span_faces)

    def span_product(vector):
        pull_stage(SPAN_STEP, 8, 152, 16, vector, span_faces, results)

        def span_store(row, outcome, carry):
            for k in range(6):
                span_out[k, pl.ds(pl.multiple_of(row - SPAN_OWN, 8), 16), :] = outcome[k]

        cells_stage(SPAN_STEP, 16, 144, 16, span_pulls, span_prims, results, span_store)

    def column_and_span():
        def body(k, carry):
            plain[k] = span_out[k].T[0:ROWS, :] + col_out[k, own, :]
            return carry

        lax.fori_loop(0, 6, body, 0, unroll=6)
        to_chord_rows(plain, partial, 6)

    def chord_product(vector, arrivals, store, start=0):
        def add_store(row, outcome, carry):
            here = pl.ds(row, outcome[0].shape[0])
            return store(row, [outcome[k] + partial[k, here, :] for k in range(6)], carry)

        def some_faces(first, last, size, gap=None):
            pull_stage(CHORD_STEP, first, last, size, vector, chord_faces, results, gap)

        def some_cells(first, last, size, start, gap=None):
            return cells_stage(
                CHORD_STEP, first, last, size, chord_pulls, chord_prims, results, add_store, None, start, gap
            )

        some_faces(40, 120, 16)
        some_faces(116, 124, 8)
        start = some_cells(64, 112, 16, start)
        arrive(arrivals)
        some_faces(16, 152, 16, (48, 120))
        return some_cells(40, 136, 24, start, (64, 112))

    def from_chord_rows(source_ref, target, first):
        def body(k, carry):
            for layer in range(LAYERS):
                rows = pl.ds(CHORD_OWN + layer, CX, stride=LAYERS)
                target[k, pl.ds(first + layer * CX, CX), :] = source_ref[k, rows, :]
            return carry

        lax.fori_loop(0, 6, body, 0)

    column_ready()
    pl.semaphore_wait(barrier, len(mates))
    chord_flow = exchange(0, cu, True, 3)
    chord_offset = exchange(2, cd, True, 2)
    chord_vector = exchange(4, cv.at[0], True, 2)
    span_flow = exchange(1, su, False, 3)
    span_offset = exchange(3, sd, False, 2)
    span_vector = exchange(5, sv.at[0], False, 2)
    for d in chord_mates:
        pl.semaphore_signal(hello, inc=1, device_id=(chord_at(d), span_id), device_id_type=mesh_ids)
    column_product(wv.at[0])
    arrive(span_flow + span_offset)
    span_ready()
    arrive(span_vector)
    span_product(sv.at[0])
    column_and_span()
    arrive(chord_flow)
    slopes_stage(CHORD_STEP, 16, 160, 16, cu, halves, chord_pulls, chord_prims)
    arrive(chord_offset)
    faces_stage(CHORD_STEP, 0, 16, 160, 16, cu, cd, halves, chord_prims, chord_faces)

    def first_store(row, outcome, carry):
        for k in range(6):
            cv[1, k, pl.ds(row, outcome[k].shape[0]), :] = 0.5 * outcome[k]

    chord_product(cv.at[0], chord_vector, first_store)

    chord_vector = exchange(6, cv.at[1], True, 2)
    from_chord_rows(cv.at[1], wv.at[1], COL_OWN)
    to_span_rows(wv.at[1], sv.at[1], 6)
    span_vector = exchange(7, sv.at[1], False, 2)
    nothing = jnp.zeros((8, CY), jnp.float32)

    def add_product(total, one, two):
        product = one * two
        for part in range(0, product.shape[0], 8):
            total = total + product[part : part + 8, :]
        return total

    def first_inner(row, carry):
        cc, cm, mm = carry
        here = pl.ds(row, 16)
        for k in range(6):
            c, m = cv[0, k, here, :], cv[1, k, here, :]
            cc, cm, mm = add_product(cc, c, c), add_product(cm, c, m), add_product(mm, m, m)
        return cc, cm, mm

    row_of = lax.broadcasted_iota(jnp.int32, (8, CY), 0)
    lane_of = lax.broadcasted_iota(jnp.int32, (8, CY), 1)

    def pack(packed, first, values):
        for index, value in enumerate(values):
            packed = jnp.where(row_of == first + index, jnp.sum(value, axis=0, keepdims=True), packed)
        return packed

    keep_m = pltpu.make_async_copy(wv.at[1, :, own, :], m_out, keep_sem.at[0])
    keep_m.start()
    packed = pack(nothing, 0, blocks(40, 136, 16, first_inner, (nothing,) * 3))
    column_product(wv.at[1])
    arrive(span_vector)
    span_product(sv.at[1])
    column_and_span()

    def second_store(row, outcome, carry):
        cn, mn, nn = carry
        here = pl.ds(row, outcome[0].shape[0])
        for k in range(6):
            n = 0.5 * outcome[k]
            last[k, here, :] = n
            c, m = cv[0, k, here, :], cv[1, k, here, :]
            cn, mn, nn = add_product(cn, c, n), add_product(mn, m, n), add_product(nn, n, n)
        return cn, mn, nn

    packed = pack(packed, 3, chord_product(cv.at[1], chord_vector, second_store, (nothing,) * 3))

    packed = jnp.broadcast_to(jnp.sum(packed, axis=1, keepdims=True), (8, CY))
    packed = jnp.where((lane_of >= 16 * row_of) & (lane_of < 16 * row_of + 16), packed, 0.0)
    mine = pl.multiple_of((chord_id * span_count + span_id) * 8, 8)
    sums[pl.ds(mine, 1), :] = jnp.sum(packed, axis=0, keepdims=True)

    pl.semaphore_wait(hello, chord_count - 1)
    for chord_to, span_to in all_partners(chord_count, span_count):
        copy = pltpu.make_async_remote_copy(
            src_ref=sums.at[pl.ds(mine, 1), :],
            dst_ref=sums.at[pl.ds(mine, 1), :],
            send_sem=sum_send,
            recv_sem=sum_recv,
            device_id=(chord_to(chord_id), span_to(span_id)),
            device_id_type=mesh_ids,
        )
        copy.start()
    from_chord_rows(last, last_plain, 0)
    keep_n = pltpu.make_async_copy(last_plain, n_out, keep_sem.at[1])
    keep_n.start()
    pltpu.make_async_copy(others, others, sum_recv).wait()
    spread = min(8, chord_count * span_count)
    total = sums[pl.ds(0, spread, stride=8), :]
    for group in range(1, chord_count * span_count // spread):
        total = total + sums[pl.ds(group * 64, spread, stride=8), :]
    total = jnp.sum(total, axis=0, keepdims=True) * (4.0 / entries)
    cc, cm, mm, cn, mn, nn = [
        jnp.broadcast_to(total[:, 16 * index : 16 * index + 1], (1, CY)) for index in range(6)
    ]

    scale = lax.rsqrt(cc + NORM_EPS)
    h11 = cm * scale * scale
    fresh = jnp.maximum(mm - 2.0 * h11 * cm + h11 * h11 * cc, 0.0)
    square = fresh * scale * scale + NORM_EPS
    inverse = lax.rsqrt(square)
    h21 = square * inverse
    gain = scale * inverse
    h12 = gain * scale * (cn - h11 * cm)
    h22 = gain * gain * (mn - h11 * cn - h11 * mm + h11 * h11 * cm)
    along_m = -gain * (h11 + h22)
    along_c = h22 * gain * h11 - h12 * scale
    fresh = (
        gain * gain * nn + along_m * along_m * mm + along_c * along_c * cc
        + 2.0 * (gain * along_m * mn + gain * along_c * cn + along_m * along_c * cm)
    )
    square = jnp.maximum(fresh, 0.0) + NORM_EPS
    inverse = lax.rsqrt(square)
    h32 = square * inverse
    factors = [f * inverse for f in (along_c, 2.0 * along_m, 2.0 * gain)]
    rows_out = jnp.zeros((8, CY), jnp.float32)
    for index, value in enumerate((h11, h21, h12, h22, h32) + tuple(factors)):
        rows_out = jnp.where(row_of == index, value, rows_out)
    table[...] = rows_out
    pltpu.make_async_copy(others, others, sum_send).wait()
    for copy in started:
        copy.wait_send()
    keep_m.wait()
    keep_n.wait()


def all_partners(chord_count, span_count):
    ys = min(4, chord_count)
    zh = chord_count // ys
    cores = min(2, span_count)
    zl = min(2, span_count // cores)
    xs = span_count // (cores * zl)

    def chord_to(dz, dy):
        return lambda c: lax.rem(lax.div(c, ys) + dz, zh) * ys + lax.rem(c + dy, ys)

    def span_to(dx, dz, dk):
        def place(s):
            x = lax.rem(lax.div(s, zl * cores) + dx, xs)
            z = lax.rem(lax.div(s, cores) + dz, zl)
            return (x * zl + z) * cores + lax.rem(s + dk, cores)

        return place

    found = []
    for high in range(zh):
        for dy in range(ys):
            for dx in range(xs):
                for low in range(zl):
                    for dk in range(cores):
                        hops = min(dy, ys - dy) + min(dx, xs - dx) + (2 if high > low else low)
                        if high + dy + dx + low + dk:
                            found.append((hops, chord_to(high, dy), span_to(dx, low, dk)))
    found.sort(key=lambda entry: -entry[0])
    return [entry[1:] for entry in found]


def final_kernel(
    table_in, cost_in, m_in, n_in, basis_out, hessenberg, cost, m, n, table, basis, table_sem, load_sem, out_sem
):
    first = pltpu.make_async_copy(table_in, table, table_sem)
    first.start()
    loads = []
    for k in range(6):
        for index, (source_ref, target) in enumerate(((cost_in, cost), (m_in, m), (n_in, n))):
            load = pltpu.make_async_copy(source_ref.at[k], target.at[k], load_sem.at[k, index])
            load.start()
            loads.append(load)
    first.wait()
    factors = [jnp.broadcast_to(table[row : row + 1, :], (ROWS, CY)) for row in (5, 6, 7)]
    stores = []
    for k in range(6):
        for load in loads[3 * k : 3 * k + 3]:
            load.wait()
        basis[k] = factors[0] * cost[k] + factors[1] * m[k] + factors[2] * n[k]
        store = pltpu.make_async_copy(basis.at[k], basis_out.at[k], out_sem.at[k])
        store.start()
        stores.append(store)
    for index in range(5):
        hessenberg[index] = table[index, 0]
    for store in stores:
        store.wait()


def on_device(chord_count, span_count, flow_state, displacement, wall_distance, face_codes, cost_gradient):
    entries = float(cost_gradient.size * chord_count * span_count)

    def vmem(*shape):
        return pltpu.VMEM(shape, jnp.float32)

    whole = pl.BlockSpec(memory_space=pltpu.VMEM)
    outside = pl.BlockSpec(memory_space=pl.ANY)
    devices = chord_count * span_count
    m, n, table = pl.pallas_call(
        functools.partial(kernel, chord_count, span_count, entries),
        out_shape=(
            jax.ShapeDtypeStruct((6, ROWS, CY), jnp.float32),
            jax.ShapeDtypeStruct((6, ROWS, CY), jnp.float32),
            jax.ShapeDtypeStruct((8, CY), jnp.float32),
        ),
        in_specs=[outside] * 5,
        out_specs=(outside, outside, whole),
        scratch_shapes=[
            vmem(6, ROWS, CY), vmem(3, ROWS, CY), vmem(ROWS, CY), pltpu.VMEM((CX, CY), jnp.int32),
            vmem(6, ROWS, CY),
            vmem(6, COL_ROWS, CY), vmem(3, COL_ROWS, CY), vmem(2, 6, COL_ROWS, CY),
            vmem(6, CHORD_ROWS, CY), vmem(3, CHORD_ROWS, CY), vmem(2, 6, CHORD_ROWS, CY),
            vmem(6, SPAN_ROWS, CY), vmem(3, SPAN_ROWS, CY), vmem(2, 6, SPAN_ROWS, CY),
            vmem(12, CHORD_ROWS, CY),
            vmem(18, COL_ROWS, CY), vmem(6, COL_ROWS, CY), vmem(FACE_COUNT, COL_ROWS, CY),
            vmem(18, CHORD_ROWS, CY), vmem(6, CHORD_ROWS, CY), vmem(FACE_COUNT, CHORD_ROWS, CY),
            vmem(18, SPAN_ROWS, CY), vmem(6, SPAN_ROWS, CY), vmem(FACE_COUNT, SPAN_ROWS, CY),
            vmem(RESULT_COUNT, CHORD_ROWS, CY), vmem(3, ROWS, CY), vmem(6, CX, CY),
            vmem(6, COL_ROWS, CY), vmem(6, CY, CY),
            vmem(6, ROWS, CY), vmem(6, CHORD_ROWS, CY), vmem(6, CHORD_ROWS, CY), vmem(6, ROWS, CY),
            vmem(8 * devices, CY), vmem(devices - 1, CY),
            pltpu.SemaphoreType.DMA((5,)), pltpu.SemaphoreType.DMA((2,)),
            pltpu.SemaphoreType.DMA((8, 2)), pltpu.SemaphoreType.DMA((8, 2)),
            pltpu.SemaphoreType.DMA, pltpu.SemaphoreType.DMA,
            pltpu.SemaphoreType.REGULAR,
        ],
        compiler_params=pltpu.CompilerParams(
            collective_id=0, has_side_effects=True, vmem_limit_bytes=62 * 1024 * 1024
        ),
        name="arnoldi",
    )(
        flow_state.reshape(6, ROWS, CY),
        displacement.reshape(3, ROWS, CY),
        wall_distance.reshape(ROWS, CY),
        face_codes,
        cost_gradient.reshape(6, ROWS, CY),
    )
    basis, hessenberg = pl.pallas_call(
        final_kernel,
        out_shape=(
            jax.ShapeDtypeStruct((6, ROWS, CY), jnp.float32),
            jax.ShapeDtypeStruct((5,), jnp.float32),
        ),
        in_specs=[outside] * 4,
        out_specs=(outside, pl.BlockSpec(memory_space=pltpu.SMEM)),
        scratch_shapes=[
            vmem(6, ROWS, CY), vmem(6, ROWS, CY), vmem(6, ROWS, CY), vmem(8, CY), vmem(6, ROWS, CY),
            pltpu.SemaphoreType.DMA, pltpu.SemaphoreType.DMA((6, 3)), pltpu.SemaphoreType.DMA((6,)),
        ],
        compiler_params=pltpu.CompilerParams(vmem_limit_bytes=62 * 1024 * 1024),
        name="combination",
    )(table, cost_gradient.reshape(6, ROWS, CY), m, n)
    return basis.reshape(cost_gradient.shape), hessenberg


def solution(mesh):
    return jax.shard_map(
        functools.partial(on_device, mesh.shape["chord"], mesh.shape["span"]),
        mesh=mesh,
        in_specs=(
            P(None, None, "chord", "span"),
            P(None, None, "chord", "span"),
            P(None, "chord", "span"),
            P("chord", "span"),
            P(None, None, "chord", "span"),
        ),
        out_specs=(P(None, None, "chord", "span"), P()),
        check_vma=False,
    )
```

```python
import functools

import jax
import jax.numpy as jnp
from jax import lax
from jax.experimental import pallas as pl
from jax.experimental.pallas import tpu as pltpu
from jax.sharding import PartitionSpec as P

HEAT_RATIO = 1.4
GAMMA_LESS = 0.4
VISCOSITY = 0.2
HEAT_FACTOR = 1.4 / (0.4 * 0.72)
CB_ONE = 0.1355
CW_ONE = 3.239
CV_CUBE = 7.1 * 7.1 * 7.1
TURB_SIGMA = 2.0 / 3.0
LIMIT_EPS = 0.01
NORM_EPS = 1e-06
FREESTREAM = (1.0, 0.2, 0.0, 0.05, 2.5, 0.1)
SLIP_SIGNS = (1.0, 1.0, 1.0, -1.0, 1.0, 1.0)
WALL_SIGNS = (1.0, -1.0, -1.0, -1.0, 1.0, -1.0)

HEAT_E = GAMMA_LESS * HEAT_FACTOR
HEAT_K = 1.0 - GAMMA_LESS * HEAT_FACTOR
CUBE_SHIFT = VISCOSITY * VISCOSITY * VISCOSITY * CV_CUBE

LAYERS, CX, CY = 12, 8, 128
ROWS = LAYERS * CX

COL_STEP, COL_OWN, COL_ROWS = 8, 32, 160
CHORD_STEP, CHORD_OWN, CHORD_ROWS = 12, 40, 176
SPAN_STEP, SPAN_OWN, SPAN_ROWS = 1, 16, 160

FL, FR, FN, FD, FM, FS, FQ, FK, FE, FRH, FTH = 0, 7, 14, 17, 23, 28, 29, 30, 31, 36, 37
FACE_COUNT = 38
GL, GR, PU, PH, TL, TR, RB = 0, 6, 12, 15, 16, 17, 18
RESULT_COUNT = 19


def blocks(first, last, size, body, start=0, gap=None):
    before = ((gap[0] if gap else last) - first) // size
    after = (last - gap[1]) // size if gap else 0

    def step(index, carry):
        row = first + index * size
        if gap:
            row = row + lax.min(lax.div(index, before), 1) * (gap[1] - gap[0])
        result = body(pl.multiple_of(row, 8 if first % 8 == 0 else 4), carry)
        return carry if result is None else result

    return lax.fori_loop(0, before + after, step, start)


def dot3(a, b):
    return a[0] * b[0] + a[1] * b[1] + a[2] * b[2]


def primitives(state):
    inverse = 1.0 / state[0]
    velocity = [state[1 + j] * inverse for j in range(3)]
    return inverse, velocity, state[5] * inverse, state[4] * inverse


def slopes_stage(step, first, last, size, window, halves, pulls, prims, gap=None):
    def body(row, carry):
        here_all = []
        for k in range(6):
            before = window[k, pl.ds(row - step, size), :]
            here = window[k, pl.ds(row, size), :]
            after = window[k, pl.ds(row + step, size), :]
            p = here - before
            q = after - here
            pp = p * p + LIMIT_EPS
            qq = q * q + LIMIT_EPS
            inverse = 1.0 / (pp + qq)
            slope = (qq * p + pp * q) * inverse
            half_inverse = 0.5 * inverse
            a = (qq + 2.0 * p * (q - slope)) * half_inverse
            b = (pp + 2.0 * q * (p - slope)) * half_inverse
            rows = pl.ds(row, size)
            halves[k, rows, :] = here + 0.5 * slope
            halves[6 + k, rows, :] = here - 0.5 * slope
            pulls[k, rows, :] = a
            pulls[6 + k, rows, :] = b
            pulls[12 + k, rows, :] = a - b
            here_all.append(here)
        inverse, velocity, turbulence, specific = primitives(here_all)
        rows = pl.ds(row, size)
        prims[0, rows, :] = inverse
        for j in range(3):
            prims[1 + j, rows, :] = velocity[j]
        prims[4, rows, :] = turbulence
        prims[5, rows, :] = specific

    blocks(first, last, size, body, gap=gap)


def side_coefficients(state, normal):
    inverse, velocity, turbulence, specific = primitives(state)
    kinetic = 0.5 * dot3(velocity, velocity)
    pressure_ratio = GAMMA_LESS * (specific - kinetic)
    return velocity + [kinetic, specific + pressure_ratio, turbulence, dot3(velocity, normal)]


def faces_stage(
    step, direction, first, last, size, window, offsets, halves, prims, faces, gap=None
):
    def body(row, carry):
        here = pl.ds(row, size)
        after = pl.ds(row + step, size)
        spacing = [offsets[j, after, :] - offsets[j, here, :] for j in range(3)]
        spacing[direction] = spacing[direction] + 1.0
        weight = lax.rsqrt(dot3(spacing, spacing))
        normal = [spacing[j] * weight for j in range(3)]
        left = [halves[k, here, :] for k in range(6)]
        right = [halves[6 + k, after, :] for k in range(6)]
        for slot, value in enumerate(side_coefficients(left, normal)):
            faces[FL + slot, here, :] = value
        for slot, value in enumerate(side_coefficients(right, normal)):
            faces[FR + slot, here, :] = value
        for j in range(3):
            faces[FN + j, here, :] = normal[j]
        for k in range(6):
            faces[FD + k, here, :] = left[k] - right[k]
        middle = [0.5 * (left[k] + right[k]) for k in range(5)] + [left[5]]
        inverse, velocity, unused, specific = primitives(middle)
        kinetic = 0.5 * dot3(velocity, velocity)
        speed = dot3(velocity, normal)
        sound_square = HEAT_RATIO * GAMMA_LESS * (specific - kinetic)
        sound_inverse = lax.rsqrt(sound_square)
        size_speed = jnp.abs(speed)
        sign = jnp.where(speed > 0.0, 1.0, jnp.where(speed < 0.0, -1.0, 0.0))
        half_inverse = 0.5 * inverse
        factor = 0.5 * HEAT_RATIO * GAMMA_LESS * sound_inverse
        faces[FS, here, :] = size_speed + sound_square * sound_inverse
        faces[FM, here, :] = half_inverse * (factor * (2.0 * kinetic - specific) - size_speed)
        for j in range(3):
            faces[FM + 1 + j, here, :] = half_inverse * (sign * normal[j] - factor * velocity[j])
        faces[FM + 4, here, :] = half_inverse * factor
        velocity_l = [prims[1 + j, here, :] for j in range(3)]
        velocity_r = [prims[1 + j, after, :] for j in range(3)]
        jump = [velocity_r[j] - velocity_l[j] for j in range(3)]
        kinetic_jump = 0.5 * (dot3(velocity_r, velocity_r) - dot3(velocity_l, velocity_l))
        heat_jump = HEAT_E * (prims[5, after, :] - prims[5, here, :]) + HEAT_K * kinetic_jump
        turbulence_l, turbulence_r = prims[4, here, :], prims[4, after, :]
        half_density = 0.25 * (window[0, here, :] + window[0, after, :])
        half_turbulence = 0.25 * (turbulence_l + turbulence_r)
        mixed = 4.0 * half_density * half_turbulence
        cube = mixed * mixed * mixed
        ratio = cube / (cube + CUBE_SHIFT)
        twice = 2.0 * weight
        pull = -twice * ratio * (4.0 - 3.0 * ratio)
        faces[FQ, here, :] = twice * (VISCOSITY + mixed * ratio)
        faces[FK, here, :] = (VISCOSITY + mixed) * (twice / TURB_SIGMA)
        for j in range(3):
            faces[FE + j, here, :] = pull * jump[j]
        faces[FE + 3, here, :] = pull * heat_jump
        faces[FE + 4, here, :] = -(twice / TURB_SIGMA) * (turbulence_r - turbulence_l)
        faces[FRH, here, :] = half_density
        faces[FTH, here, :] = half_turbulence

    blocks(first, last, size, body, gap=gap)


def side_pullback(faces, here, base, normal, wave, shared, g):
    velocity = [faces[base + j, here, :] for j in range(3)]
    kinetic = faces[base + 3, here, :]
    enthalpy = faces[base + 4, here, :]
    turbulence = faces[base + 5, here, :]
    speed = faces[base + 6, here, :]
    total = g[0] + dot3(velocity, g[1:4]) + enthalpy * g[4] + turbulence * g[5]
    pressure = GAMMA_LESS * (shared + speed * g[4])
    carried = speed + wave
    result = [carried * g[0] - total * speed + pressure * kinetic]
    for j in range(3):
        result.append(carried * g[1 + j] + total * normal[j] - pressure * velocity[j])
    result.append(carried * g[4] + pressure)
    result.append(carried * g[5])
    return result


def pull_stage(step, first, last, size, vector, faces, results, gap=None):
    def body(row, carry):
        here = pl.ds(row, size)
        after = pl.ds(row + step, size)
        g = [vector[k, here, :] - vector[k, after, :] for k in range(6)]
        normal = [faces[FN + j, here, :] for j in range(3)]
        wave = faces[FS, here, :]
        shared = dot3(normal, g[1:4])
        left = side_pullback(faces, here, FL, normal, wave, shared, g)
        right = side_pullback(faces, here, FR, normal, -wave, shared, g)
        wave_bar = faces[FD, here, :] * g[0]
        for k in range(1, 6):
            wave_bar = wave_bar + faces[FD + k, here, :] * g[k]
        for k in range(6):
            if k < 5:
                middle = wave_bar * faces[FM + k, here, :]
                results[GL + k, here, :] = left[k] + middle
                results[GR + k, here, :] = right[k] + middle
            else:
                results[GL + k, here, :] = left[k]
                results[GR + k, here, :] = right[k]
        viscous = faces[FQ, here, :]
        mixed_bar = faces[FE, here, :] * g[1]
        for k in range(1, 5):
            mixed_bar = mixed_bar + faces[FE + k, here, :] * g[1 + k]
        for j in range(3):
            results[PU + j, here, :] = viscous * g[1 + j]
        results[PH, here, :] = viscous * g[4]
        diffused = faces[FK, here, :] * g[5]
        shift = faces[FRH, here, :] * mixed_bar
        results[TL, here, :] = shift + diffused
        results[TR, here, :] = shift - diffused
        results[RB, here, :] = faces[FTH, here, :] * mixed_bar

    blocks(first, last, size, body, gap=gap)


def cells_stage(step, first, last, size, pulls, prims, results, store, extra=None, start=0, gap=None):
    def body(row, carry):
        here = pl.ds(row, size)
        before = pl.ds(row - step, size)
        after = pl.ds(row + step, size)
        twice = pl.ds(row - 2 * step, size)
        outcome = []
        for k in range(6):
            gl, gr = results[GL + k, here, :], results[GR + k, before, :]
            value = gl + gr + pulls[12 + k, here, :] * (gl - gr)
            value = value + pulls[6 + k, before, :] * (
                results[GL + k, before, :] - results[GR + k, twice, :]
            )
            value = value - pulls[k, after, :] * (
                results[GL + k, after, :] - results[GR + k, here, :]
            )
            outcome.append(value)
        velocity_bar = [results[PU + j, here, :] - results[PU + j, before, :] for j in range(3)]
        heat_bar = results[PH, here, :] - results[PH, before, :]
        turbulence_bar = results[TL, here, :] + results[TR, before, :]
        density_bar = results[RB, here, :] + results[RB, before, :]
        inverse = prims[0, here, :]
        velocity = [prims[1 + j, here, :] for j in range(3)]
        if extra is not None:
            velocity_bar, turbulence_bar, density_bar = extra(
                row, velocity, velocity_bar, turbulence_bar, density_bar
            )
        kinetic_bar = HEAT_K * heat_bar
        energy_bar = HEAT_E * heat_bar
        velocity_bar = [velocity_bar[j] + kinetic_bar * velocity[j] for j in range(3)]
        scaled = (
            dot3(velocity_bar, velocity)
            + energy_bar * prims[5, here, :]
            + turbulence_bar * prims[4, here, :]
        )
        outcome[0] = outcome[0] + density_bar - scaled * inverse
        for j in range(3):
            outcome[1 + j] = outcome[1 + j] + velocity_bar[j] * inverse
        outcome[4] = outcome[4] + energy_bar * inverse
        outcome[5] = outcome[5] + turbulence_bar * inverse
        return store(row, outcome, carry)

    return blocks(first, last, size, body, start, gap)


def kernel(
    chord_count, span_count, entries,
    flow_in, offset_in, wall_in, codes_in, cost_in, m_out, n_out, sums,
    flow, offset, wall, codes, cost,
    wu, wd, wv, cu, cd, cv, su, sd, sv, halves,
    col_pulls, col_prims, col_faces, chord_pulls, chord_prims, chord_faces,
    span_pulls, span_prims, span_faces, results, source, signs, col_out, span_out,
    plain, partial, last, last_plain, row, others, load_sem, keep_sem, send_sem, recv_sem, sum_send, sum_recv, hello,
):
    chord_id, span_id = lax.axis_index("chord"), lax.axis_index("span")
    mesh_ids = pl.DeviceIdType.MESH

    def chord_at(distance):
        return lax.rem(chord_id + (distance + chord_count), chord_count)

    def span_at(distance):
        return lax.rem(span_id + (distance + span_count), span_count)

    barrier = pltpu.get_barrier_semaphore()
    chord_mates = sorted(range(1, chord_count), key=lambda d: min(d, chord_count - d))
    span_mates = sorted(range(1, span_count), key=lambda d: min(d, span_count - d))
    mates = [(chord_at(d), span_id) for d in chord_mates[:2]]
    mates += [(chord_id, span_at(d)) for d in span_mates]
    mates += [(chord_at(d), span_id) for d in chord_mates[2:]]
    for mate in mates[:4]:
        pl.semaphore_signal(barrier, inc=1, device_id=mate, device_id_type=mesh_ids)

    loads = [
        pltpu.make_async_copy(source_ref, target, load_sem.at[index])
        for index, (source_ref, target) in enumerate(
            ((flow_in, flow), (offset_in, offset), (cost_in, cost), (codes_in, codes), (wall_in, wall))
        )
    ]
    for load in loads:
        load.start()
    for mate in mates[4:]:
        pl.semaphore_signal(barrier, inc=1, device_id=mate, device_id_type=mesh_ids)

    def to_chord_rows(source_ref, target, count, first=0, gain=None):
        def body(k, carry):
            for cell in range(CX):
                base = CHORD_OWN + cell * LAYERS
                high = source_ref[k, pl.ds(first + cell, 8, stride=CX), :]
                low = source_ref[k, pl.ds(first + 8 * CX + cell, 4, stride=CX), :]
                target[k, pl.ds(base, 8), :] = high if gain is None else gain * high
                target[k, pl.ds(base + 8, 4), :] = low if gain is None else gain * low
            return carry

        lax.fori_loop(0, count, body, 0)

    def to_span_rows(source_ref, target, count):
        def body(k, carry):
            target[k, pl.ds(SPAN_OWN, CY), :] = source_ref[k, pl.ds(COL_OWN, CY), :].T
            return carry

        lax.fori_loop(0, count, body, 0, unroll=count)

    started = []

    def exchange(slot, ref, chordwise, depth):
        if chordwise:
            rows = 40 if depth == 3 else 24
            tail = CHORD_OWN + ROWS - rows
            moves = (
                (tail, CHORD_OWN - rows, (chord_at(1), span_id)),
                (CHORD_OWN, CHORD_OWN + ROWS, (chord_at(-1), span_id)),
            )
        else:
            rows = 8
            moves = (
                (SPAN_OWN + CY - rows, SPAN_OWN - rows, (chord_id, span_at(1))),
                (SPAN_OWN, SPAN_OWN + CY, (chord_id, span_at(-1))),
            )
        copies = []
        for side, (first, landing, target) in enumerate(moves):
            copy = pltpu.make_async_remote_copy(
                src_ref=ref.at[:, pl.ds(first, rows), :],
                dst_ref=ref.at[:, pl.ds(landing, rows), :],
                send_sem=send_sem.at[slot, side],
                recv_sem=recv_sem.at[slot, side],
                device_id=target,
                device_id_type=mesh_ids,
            )
            copy.start()
            copies.append(copy)
        started.extend(copies)
        return copies

    def arrive(copies):
        for copy in copies:
            copy.wait_recv()

    for load in loads:
        load.wait()
    to_chord_rows(flow, cu, 6)
    to_chord_rows(offset, cd, 3)
    to_chord_rows(cost, cv.at[0], 6, gain=0.5)

    own = pl.ds(COL_OWN, ROWS)
    code = codes[...]
    for k in range(6):
        near, far = flow[k, 0:8, :], flow[k, 8:16, :]
        sign = jnp.where(code == 0, SLIP_SIGNS[k], jnp.where(code == 1, WALL_SIGNS[k], 0.0))
        level = jnp.where((code == 0) | (code == 1), 0.0, FREESTREAM[k])
        signs[k] = sign
        wu[k, 0:16, :] = jnp.full((16, CY), FREESTREAM[k], jnp.float32)
        wu[k, 16:24, :] = sign * far + level
        wu[k, 24:32, :] = sign * near + level
        wu[k, own, :] = flow[k]
        wu[k, 128:160, :] = jnp.full((32, CY), FREESTREAM[k], jnp.float32)
        wv[0, k, 0:32, :] = jnp.zeros((32, CY), jnp.float32)
        wv[0, k, own, :] = 0.5 * cost[k]
        wv[0, k, 128:160, :] = jnp.zeros((32, CY), jnp.float32)
        wv[1, k, 0:32, :] = jnp.zeros((32, CY), jnp.float32)
        wv[1, k, 128:160, :] = jnp.zeros((32, CY), jnp.float32)
    for j in range(3):
        near, far, top = offset[j, 0:8, :], offset[j, 8:16, :], offset[j, 88:96, :]
        wd[j, 0:8, :] = far
        wd[j, 8:16, :] = far
        wd[j, 16:24, :] = far
        wd[j, 24:32, :] = near
        wd[j, own, :] = offset[j]
        for layer in range(4):
            wd[j, 128 + 8 * layer : 136 + 8 * layer, :] = top

    to_span_rows(wu, su, 6)
    to_span_rows(wd, sd, 3)
    to_span_rows(wv.at[0], sv.at[0], 6)

    def source_body(row, carry):
        here = pl.ds(row, 16)
        cells = pl.ds(row + COL_OWN, 16)
        density = wu[0, cells, :]
        inverse = 1.0 / density
        velocity = [wu[1 + j, cells, :] * inverse for j in range(3)]
        turbulence = wu[5, cells, :] * inverse
        near = 1.0 / wall[here, :]
        square = dot3(velocity, velocity) + 0.01
        root_inverse = lax.rsqrt(square)
        slope = CB_ONE * near
        shear = slope * (square * root_inverse)
        decay = CW_ONE * turbulence * near * near
        source[0, here, :] = -2.0 * turbulence * (shear - decay)
        source[1, here, :] = -2.0 * density * (shear - 2.0 * decay)
        source[2, here, :] = -2.0 * density * turbulence * slope * root_inverse

    blocks(0, ROWS, 16, source_body)

    def column_ready():
        slopes_stage(COL_STEP, 16, 144, 16, wu, halves, col_pulls, col_prims)
        faces_stage(COL_STEP, 2, 24, 136, 16, wu, wd, halves, col_prims, col_faces)
        for k in range(6):
            col_pulls[6 + k, 8:16, :] = jnp.zeros((8, CY), jnp.float32)

    def column_product(vector):
        for slot in range(RESULT_COUNT):
            results[slot, 0:24, :] = jnp.zeros((24, CY), jnp.float32)
        pull_stage(COL_STEP, 24, 136, 16, vector, col_faces, results)

        def column_store(row, outcome, carry):
            for k in range(6):
                col_out[k, pl.ds(row, 16), :] = outcome[k]

        def with_source(row, velocity, velocity_bar, turbulence_bar, density_bar):
            here = pl.ds(pl.multiple_of(row - COL_OWN, 8), 16)
            value = vector[5, pl.ds(row, 16), :]
            pulled = source[2, here, :] * value
            return (
                [velocity_bar[j] + pulled * velocity[j] for j in range(3)],
                turbulence_bar + source[1, here, :] * value,
                density_bar + source[0, here, :] * value,
            )

        cells_stage(COL_STEP, 16, 32, 16, col_pulls, col_prims, results, column_store)
        cells_stage(COL_STEP, 32, 128, 16, col_pulls, col_prims, results, column_store, with_source)
        for k in range(6):
            sign = signs[k]
            col_out[k, 32:40, :] = col_out[k, 32:40, :] + sign * col_out[k, 24:32, :]
            col_out[k, 40:48, :] = col_out[k, 40:48, :] + sign * col_out[k, 16:24, :]

    def span_ready(first, last, faces_last, gap=None, faces_gap=None):
        slopes_stage(SPAN_STEP, first, last, 16, su, halves, span_pulls, span_prims, gap)
        faces_stage(
            SPAN_STEP, 1, first, faces_last, 16, su, sd, halves, span_prims, span_faces, faces_gap
        )

    def span_product(vector, first, last, cells_first, cells_last, gap=None, cells_gap=None):
        pull_stage(SPAN_STEP, first, last, 16, vector, span_faces, results, gap)

        def span_store(row, outcome, carry):
            for k in range(6):
                span_out[k, pl.ds(pl.multiple_of(row - SPAN_OWN, 8), 16), :] = outcome[k]

        cells_stage(
            SPAN_STEP, cells_first, cells_last, 16, span_pulls, span_prims, results, span_store,
            gap=cells_gap,
        )

    def span_inside(vector):
        span_product(vector, 24, 120, 32, 112)

    def span_edges(vector):
        span_product(vector, 8, 152, 16, 144, (24, 120), (32, 112))

    def column_and_span():
        def body(k, carry):
            plain[k] = span_out[k].T[0:ROWS, :] + col_out[k, own, :]
            return carry

        lax.fori_loop(0, 6, body, 0, unroll=6)
        to_chord_rows(plain, partial, 6)

    def chord_product(vector, arrivals, store, start=0):
        def add_store(row, outcome, carry):
            here = pl.ds(row, outcome[0].shape[0])
            return store(row, [outcome[k] + partial[k, here, :] for k in range(6)], carry)

        def some_faces(first, last, size, gap=None):
            pull_stage(CHORD_STEP, first, last, size, vector, chord_faces, results, gap)

        def some_cells(first, last, size, start, gap=None):
            return cells_stage(
                CHORD_STEP, first, last, size, chord_pulls, chord_prims, results, add_store, None, start, gap
            )

        some_faces(40, 120, 16)
        some_faces(116, 124, 8)
        start = some_cells(64, 112, 16, start)
        arrive(arrivals)
        some_faces(16, 152, 16, (48, 120))
        return some_cells(40, 136, 24, start, (64, 112))

    def from_chord_rows(source_ref, target, first):
        def body(k, carry):
            for layer in range(LAYERS):
                rows = pl.ds(CHORD_OWN + layer, CX, stride=LAYERS)
                target[k, pl.ds(first + layer * CX, CX), :] = source_ref[k, rows, :]
            return carry

        lax.fori_loop(0, 6, body, 0)

    column_ready()
    pl.semaphore_wait(barrier, len(mates))
    chord_flow = exchange(0, cu, True, 3)
    chord_offset = exchange(2, cd, True, 2)
    chord_vector = exchange(4, cv.at[0], True, 2)
    span_flow = exchange(1, su, False, 3)
    span_offset = exchange(3, sd, False, 2)
    span_vector = exchange(5, sv.at[0], False, 2)
    for d in chord_mates:
        pl.semaphore_signal(hello, inc=1, device_id=(chord_at(d), span_id), device_id_type=mesh_ids)
    column_product(wv.at[0])
    span_ready(24, 136, 120)
    span_inside(sv.at[0])
    arrive(span_flow + span_offset)
    span_ready(8, 152, 152, (24, 136), (24, 120))
    arrive(span_vector)
    span_edges(sv.at[0])
    column_and_span()
    arrive(chord_flow)
    slopes_stage(CHORD_STEP, 16, 160, 16, cu, halves, chord_pulls, chord_prims)
    arrive(chord_offset)
    faces_stage(CHORD_STEP, 0, 16, 160, 16, cu, cd, halves, chord_prims, chord_faces)

    def first_store(row, outcome, carry):
        for k in range(6):
            cv[1, k, pl.ds(row, outcome[k].shape[0]), :] = 0.5 * outcome[k]

    chord_product(cv.at[0], chord_vector, first_store)

    chord_vector = exchange(6, cv.at[1], True, 2)
    from_chord_rows(cv.at[1], wv.at[1], COL_OWN)
    to_span_rows(wv.at[1], sv.at[1], 6)
    span_vector = exchange(7, sv.at[1], False, 2)
    nothing = jnp.zeros((8, CY), jnp.float32)

    def add_product(total, one, two):
        product = one * two
        for part in range(0, product.shape[0], 8):
            total = total + product[part : part + 8, :]
        return total

    def first_inner(row, carry):
        cc, cm, mm = carry
        here = pl.ds(row, 16)
        for k in range(6):
            c, m = cv[0, k, here, :], cv[1, k, here, :]
            cc, cm, mm = add_product(cc, c, c), add_product(cm, c, m), add_product(mm, m, m)
        return cc, cm, mm

    row_of = lax.broadcasted_iota(jnp.int32, (8, CY), 0)
    lane_of = lax.broadcasted_iota(jnp.int32, (8, CY), 1)

    def pack(packed, first, values):
        for index, value in enumerate(values):
            packed = jnp.where(row_of == first + index, jnp.sum(value, axis=0, keepdims=True), packed)
        return packed

    keep_m = pltpu.make_async_copy(wv.at[1, :, own, :], m_out, keep_sem.at[0])
    keep_m.start()
    packed = pack(nothing, 0, blocks(40, 136, 16, first_inner, (nothing,) * 3))
    column_product(wv.at[1])
    span_inside(sv.at[1])
    arrive(span_vector)
    span_edges(sv.at[1])
    column_and_span()

    def second_store(row, outcome, carry):
        cn, mn, nn = carry
        here = pl.ds(row, outcome[0].shape[0])
        for k in range(6):
            n = 0.5 * outcome[k]
            last[k, here, :] = n
            c, m = cv[0, k, here, :], cv[1, k, here, :]
            cn, mn, nn = add_product(cn, c, n), add_product(mn, m, n), add_product(nn, n, n)
        return cn, mn, nn

    packed = pack(packed, 3, chord_product(cv.at[1], chord_vector, second_store, (nothing,) * 3))

    packed = jnp.broadcast_to(jnp.sum(packed, axis=1, keepdims=True), (8, CY))
    packed = jnp.where((lane_of >= 16 * row_of) & (lane_of < 16 * row_of + 16), packed, 0.0)
    row[...] = jnp.broadcast_to(jnp.sum(packed, axis=0, keepdims=True), (8, CY))
    mine = sums.at[chord_id * span_count + span_id, pl.ds(0, 1), :]
    keep_row = pltpu.make_async_copy(row.at[pl.ds(0, 1), :], mine, keep_sem.at[2])
    keep_row.start()

    pl.semaphore_wait(hello, chord_count - 1)
    for chord_to, span_to in all_partners(chord_count, span_count):
        copy = pltpu.make_async_remote_copy(
            src_ref=row.at[pl.ds(0, 1), :],
            dst_ref=mine,
            send_sem=sum_send,
            recv_sem=sum_recv,
            device_id=(chord_to(chord_id), span_to(span_id)),
            device_id_type=mesh_ids,
        )
        copy.start()
    from_chord_rows(last, last_plain, 0)
    keep_n = pltpu.make_async_copy(last_plain, n_out, keep_sem.at[1])
    keep_n.start()
    pltpu.make_async_copy(others, others, sum_recv).wait()
    pltpu.make_async_copy(others, others, sum_send).wait()
    for copy in started:
        copy.wait_send()
    keep_m.wait()
    keep_n.wait()
    keep_row.wait()


def all_partners(chord_count, span_count):
    ys = min(4, chord_count)
    zh = chord_count // ys
    cores = min(2, span_count)
    zl = min(2, span_count // cores)
    xs = span_count // (cores * zl)

    def chord_to(dz, dy):
        return lambda c: lax.rem(lax.div(c, ys) + dz, zh) * ys + lax.rem(c + dy, ys)

    def span_to(dx, dz, dk):
        def place(s):
            x = lax.rem(lax.div(s, zl * cores) + dx, xs)
            z = lax.rem(lax.div(s, cores) + dz, zl)
            return (x * zl + z) * cores + lax.rem(s + dk, cores)

        return place

    found = []
    for high in range(zh):
        for dy in range(ys):
            for dx in range(xs):
                for low in range(zl):
                    for dk in range(cores):
                        hops = min(dy, ys - dy) + min(dx, xs - dx) + (2 if high > low else low)
                        if high + dy + dx + low + dk:
                            found.append((hops, chord_to(high, dy), span_to(dx, low, dk)))
    found.sort(key=lambda entry: -entry[0])
    return [entry[1:] for entry in found]


def final_kernel(
    entries, sums_in, cost_in, m_in, n_in, basis_out, hessenberg,
    cost, m, n, sums, table, basis, sums_sem, load_sem, out_sem,
):
    first_row = pl.ds(0, 1)
    first = pltpu.make_async_copy(sums_in.at[:, first_row, :], sums.at[:, first_row, :], sums_sem)
    first.start()
    loads = []
    for k in range(6):
        for index, (source_ref, target) in enumerate(((cost_in, cost), (m_in, m), (n_in, n))):
            load = pltpu.make_async_copy(source_ref.at[k], target.at[k], load_sem.at[k, index])
            load.start()
            loads.append(load)
    first.wait()
    parts = [sums[device, first_row, :] for device in range(sums.shape[0])]
    while len(parts) > 1:
        parts = [sum(parts[index : index + 2]) for index in range(0, len(parts), 2)]
    total = parts[0] * (4.0 / entries)
    cc, cm, mm, cn, mn, nn = [
        jnp.broadcast_to(total[:, 16 * index : 16 * index + 1], (1, CY)) for index in range(6)
    ]

    scale = lax.rsqrt(cc + NORM_EPS)
    h11 = cm * scale * scale
    fresh = jnp.maximum(mm - 2.0 * h11 * cm + h11 * h11 * cc, 0.0)
    square = fresh * scale * scale + NORM_EPS
    inverse = lax.rsqrt(square)
    h21 = square * inverse
    gain = scale * inverse
    h12 = gain * scale * (cn - h11 * cm)
    h22 = gain * gain * (mn - h11 * cn - h11 * mm + h11 * h11 * cm)
    along_m = -gain * (h11 + h22)
    along_c = h22 * gain * h11 - h12 * scale
    fresh = (
        gain * gain * nn + along_m * along_m * mm + along_c * along_c * cc
        + 2.0 * (gain * along_m * mn + gain * along_c * cn + along_m * along_c * cm)
    )
    square = jnp.maximum(fresh, 0.0) + NORM_EPS
    inverse = lax.rsqrt(square)
    h32 = square * inverse
    factors = [f * inverse for f in (along_c, 2.0 * along_m, 2.0 * gain)]
    row_of = lax.broadcasted_iota(jnp.int32, (8, CY), 0)
    rows_out = jnp.zeros((8, CY), jnp.float32)
    for index, value in enumerate((h11, h21, h12, h22, h32)):
        rows_out = jnp.where(row_of == index, value, rows_out)
    table[...] = rows_out
    factors = [jnp.broadcast_to(factor, (ROWS, CY)) for factor in factors]
    stores = []
    for k in range(6):
        for load in loads[3 * k : 3 * k + 3]:
            load.wait()
        basis[k] = factors[0] * cost[k] + factors[1] * m[k] + factors[2] * n[k]
        store = pltpu.make_async_copy(basis.at[k], basis_out.at[k], out_sem.at[k])
        store.start()
        stores.append(store)
    for index in range(5):
        hessenberg[index] = table[index, 0]
    for store in stores:
        store.wait()


def on_device(chord_count, span_count, flow_state, displacement, wall_distance, face_codes, cost_gradient):
    entries = float(cost_gradient.size * chord_count * span_count)

    def vmem(*shape):
        return pltpu.VMEM(shape, jnp.float32)

    outside = pl.BlockSpec(memory_space=pl.ANY)
    devices = chord_count * span_count
    m, n, sums = pl.pallas_call(
        functools.partial(kernel, chord_count, span_count, entries),
        out_shape=(
            jax.ShapeDtypeStruct((6, ROWS, CY), jnp.float32),
            jax.ShapeDtypeStruct((6, ROWS, CY), jnp.float32),
            jax.ShapeDtypeStruct((devices, 8, CY), jnp.float32),
        ),
        in_specs=[outside] * 5,
        out_specs=(outside, outside, outside),
        scratch_shapes=[
            vmem(6, ROWS, CY), vmem(3, ROWS, CY), vmem(ROWS, CY), pltpu.VMEM((CX, CY), jnp.int32),
            vmem(6, ROWS, CY),
            vmem(6, COL_ROWS, CY), vmem(3, COL_ROWS, CY), vmem(2, 6, COL_ROWS, CY),
            vmem(6, CHORD_ROWS, CY), vmem(3, CHORD_ROWS, CY), vmem(2, 6, CHORD_ROWS, CY),
            vmem(6, SPAN_ROWS, CY), vmem(3, SPAN_ROWS, CY), vmem(2, 6, SPAN_ROWS, CY),
            vmem(12, CHORD_ROWS, CY),
            vmem(18, COL_ROWS, CY), vmem(6, COL_ROWS, CY), vmem(FACE_COUNT, COL_ROWS, CY),
            vmem(18, CHORD_ROWS, CY), vmem(6, CHORD_ROWS, CY), vmem(FACE_COUNT, CHORD_ROWS, CY),
            vmem(18, SPAN_ROWS, CY), vmem(6, SPAN_ROWS, CY), vmem(FACE_COUNT, SPAN_ROWS, CY),
            vmem(RESULT_COUNT, CHORD_ROWS, CY), vmem(3, ROWS, CY), vmem(6, CX, CY),
            vmem(6, COL_ROWS, CY), vmem(6, CY, CY),
            vmem(6, ROWS, CY), vmem(6, CHORD_ROWS, CY), vmem(6, CHORD_ROWS, CY), vmem(6, ROWS, CY),
            vmem(8, CY), vmem(devices - 1, CY),
            pltpu.SemaphoreType.DMA((5,)), pltpu.SemaphoreType.DMA((3,)),
            pltpu.SemaphoreType.DMA((8, 2)), pltpu.SemaphoreType.DMA((8, 2)),
            pltpu.SemaphoreType.DMA, pltpu.SemaphoreType.DMA,
            pltpu.SemaphoreType.REGULAR,
        ],
        compiler_params=pltpu.CompilerParams(
            collective_id=0, has_side_effects=True, vmem_limit_bytes=62 * 1024 * 1024
        ),
        name="arnoldi",
    )(
        flow_state.reshape(6, ROWS, CY),
        displacement.reshape(3, ROWS, CY),
        wall_distance.reshape(ROWS, CY),
        face_codes,
        cost_gradient.reshape(6, ROWS, CY),
    )
    basis, hessenberg = pl.pallas_call(
        functools.partial(final_kernel, entries),
        out_shape=(
            jax.ShapeDtypeStruct((6, ROWS, CY), jnp.float32),
            jax.ShapeDtypeStruct((5,), jnp.float32),
        ),
        in_specs=[outside] * 4,
        out_specs=(outside, pl.BlockSpec(memory_space=pltpu.SMEM)),
        scratch_shapes=[
            vmem(6, ROWS, CY), vmem(6, ROWS, CY), vmem(6, ROWS, CY), vmem(devices, 8, CY), vmem(8, CY),
            vmem(6, ROWS, CY),
            pltpu.SemaphoreType.DMA, pltpu.SemaphoreType.DMA((6, 3)), pltpu.SemaphoreType.DMA((6,)),
        ],
        compiler_params=pltpu.CompilerParams(vmem_limit_bytes=62 * 1024 * 1024),
        name="combination",
    )(sums, cost_gradient.reshape(6, ROWS, CY), m, n)
    return basis.reshape(cost_gradient.shape), hessenberg


def solution(mesh):
    return jax.shard_map(
        functools.partial(on_device, mesh.shape["chord"], mesh.shape["span"]),
        mesh=mesh,
        in_specs=(
            P(None, None, "chord", "span"),
            P(None, None, "chord", "span"),
            P(None, "chord", "span"),
            P("chord", "span"),
            P(None, None, "chord", "span"),
        ),
        out_specs=(P(None, None, "chord", "span"), P()),
        check_vma=False,
    )
```

```python
import functools

import jax
import jax.numpy as jnp
from jax import lax
from jax.experimental import pallas as pl
from jax.experimental.pallas import tpu as pltpu
from jax.sharding import PartitionSpec as P

HEAT_RATIO = 1.4
GAMMA_LESS = 0.4
VISCOSITY = 0.2
HEAT_FACTOR = 1.4 / (0.4 * 0.72)
CB_ONE = 0.1355
CW_ONE = 3.239
CV_CUBE = 7.1 * 7.1 * 7.1
TURB_SIGMA = 2.0 / 3.0
LIMIT_EPS = 0.01
NORM_EPS = 1e-06
FREESTREAM = (1.0, 0.2, 0.0, 0.05, 2.5, 0.1)
SLIP_SIGNS = (1.0, 1.0, 1.0, -1.0, 1.0, 1.0)
WALL_SIGNS = (1.0, -1.0, -1.0, -1.0, 1.0, -1.0)

HEAT_E = GAMMA_LESS * HEAT_FACTOR
HEAT_K = 1.0 - GAMMA_LESS * HEAT_FACTOR
CUBE_SHIFT = VISCOSITY * VISCOSITY * VISCOSITY * CV_CUBE

LAYERS, CX, CY = 12, 8, 128
ROWS = LAYERS * CX
PADDED = ROWS + CX

COL_STEP, COL_OWN, COL_ROWS = 8, 32, 160
CHORD_STEP, CHORD_OWN, CHORD_ROWS = 12, 40, 176
SPAN_STEP, SPAN_OWN, SPAN_ROWS = 1, 16, 160

FL, FR, FN, FD, FM, FS, FQ, FK, FE, FRH, FTH = 0, 7, 14, 17, 23, 28, 29, 30, 31, 36, 37
FACE_COUNT = 38
GL, GR, PU, PH, TL, TR, RB = 0, 6, 12, 15, 16, 17, 18
RESULT_COUNT = 19


def blocks(first, last, size, body, start=0, gap=None):
    before = ((gap[0] if gap else last) - first) // size
    after = (last - gap[1]) // size if gap else 0

    def step(index, carry):
        row = first + index * size
        if gap:
            row = row + lax.min(lax.div(index, before), 1) * (gap[1] - gap[0])
        result = body(pl.multiple_of(row, 8 if first % 8 == 0 else 4), carry)
        return carry if result is None else result

    return lax.fori_loop(0, before + after, step, start)


def dot3(a, b):
    return a[0] * b[0] + a[1] * b[1] + a[2] * b[2]


def primitives(state):
    inverse = 1.0 / state[0]
    velocity = [state[1 + j] * inverse for j in range(3)]
    return inverse, velocity, state[5] * inverse, state[4] * inverse


def slopes_stage(step, first, last, size, window, halves, pulls, prims, gap=None):
    def body(row, carry):
        here_all = []
        for k in range(6):
            before = window[k, pl.ds(row - step, size), :]
            here = window[k, pl.ds(row, size), :]
            after = window[k, pl.ds(row + step, size), :]
            p = here - before
            q = after - here
            pp = p * p + LIMIT_EPS
            qq = q * q + LIMIT_EPS
            inverse = 1.0 / (pp + qq)
            slope = (qq * p + pp * q) * inverse
            half_inverse = 0.5 * inverse
            a = (qq + 2.0 * p * (q - slope)) * half_inverse
            b = (pp + 2.0 * q * (p - slope)) * half_inverse
            rows = pl.ds(row, size)
            halves[k, rows, :] = here + 0.5 * slope
            halves[6 + k, rows, :] = here - 0.5 * slope
            pulls[k, rows, :] = a
            pulls[6 + k, rows, :] = b
            pulls[12 + k, rows, :] = a - b
            here_all.append(here)
        inverse, velocity, turbulence, specific = primitives(here_all)
        rows = pl.ds(row, size)
        prims[0, rows, :] = inverse
        for j in range(3):
            prims[1 + j, rows, :] = velocity[j]
        prims[4, rows, :] = turbulence
        prims[5, rows, :] = specific

    blocks(first, last, size, body, gap=gap)


def side_coefficients(state, normal):
    inverse, velocity, turbulence, specific = primitives(state)
    kinetic = 0.5 * dot3(velocity, velocity)
    pressure_ratio = GAMMA_LESS * (specific - kinetic)
    return velocity + [kinetic, specific + pressure_ratio, turbulence, dot3(velocity, normal)]


def faces_stage(
    step, direction, first, last, size, window, offsets, halves, prims, faces, gap=None
):
    def body(row, carry):
        here = pl.ds(row, size)
        after = pl.ds(row + step, size)
        spacing = [offsets[j, after, :] - offsets[j, here, :] for j in range(3)]
        spacing[direction] = spacing[direction] + 1.0
        weight = lax.rsqrt(dot3(spacing, spacing))
        normal = [spacing[j] * weight for j in range(3)]
        left = [halves[k, here, :] for k in range(6)]
        right = [halves[6 + k, after, :] for k in range(6)]
        for slot, value in enumerate(side_coefficients(left, normal)):
            faces[FL + slot, here, :] = value
        for slot, value in enumerate(side_coefficients(right, normal)):
            faces[FR + slot, here, :] = value
        for j in range(3):
            faces[FN + j, here, :] = normal[j]
        for k in range(6):
            faces[FD + k, here, :] = left[k] - right[k]
        middle = [0.5 * (left[k] + right[k]) for k in range(5)] + [left[5]]
        inverse, velocity, unused, specific = primitives(middle)
        kinetic = 0.5 * dot3(velocity, velocity)
        speed = dot3(velocity, normal)
        sound_square = HEAT_RATIO * GAMMA_LESS * (specific - kinetic)
        sound_inverse = lax.rsqrt(sound_square)
        size_speed = jnp.abs(speed)
        sign = jnp.where(speed > 0.0, 1.0, jnp.where(speed < 0.0, -1.0, 0.0))
        half_inverse = 0.5 * inverse
        factor = 0.5 * HEAT_RATIO * GAMMA_LESS * sound_inverse
        faces[FS, here, :] = size_speed + sound_square * sound_inverse
        faces[FM, here, :] = half_inverse * (factor * (2.0 * kinetic - specific) - size_speed)
        for j in range(3):
            faces[FM + 1 + j, here, :] = half_inverse * (sign * normal[j] - factor * velocity[j])
        faces[FM + 4, here, :] = half_inverse * factor
        velocity_l = [prims[1 + j, here, :] for j in range(3)]
        velocity_r = [prims[1 + j, after, :] for j in range(3)]
        jump = [velocity_r[j] - velocity_l[j] for j in range(3)]
        kinetic_jump = 0.5 * (dot3(velocity_r, velocity_r) - dot3(velocity_l, velocity_l))
        heat_jump = HEAT_E * (prims[5, after, :] - prims[5, here, :]) + HEAT_K * kinetic_jump
        turbulence_l, turbulence_r = prims[4, here, :], prims[4, after, :]
        half_density = 0.25 * (window[0, here, :] + window[0, after, :])
        half_turbulence = 0.25 * (turbulence_l + turbulence_r)
        mixed = 4.0 * half_density * half_turbulence
        cube = mixed * mixed * mixed
        ratio = cube / (cube + CUBE_SHIFT)
        twice = 2.0 * weight
        pull = -twice * ratio * (4.0 - 3.0 * ratio)
        faces[FQ, here, :] = twice * (VISCOSITY + mixed * ratio)
        faces[FK, here, :] = (VISCOSITY + mixed) * (twice / TURB_SIGMA)
        for j in range(3):
            faces[FE + j, here, :] = pull * jump[j]
        faces[FE + 3, here, :] = pull * heat_jump
        faces[FE + 4, here, :] = -(twice / TURB_SIGMA) * (turbulence_r - turbulence_l)
        faces[FRH, here, :] = half_density
        faces[FTH, here, :] = half_turbulence

    blocks(first, last, size, body, gap=gap)


def side_pullback(faces, here, base, normal, wave, shared, g):
    velocity = [faces[base + j, here, :] for j in range(3)]
    kinetic = faces[base + 3, here, :]
    enthalpy = faces[base + 4, here, :]
    turbulence = faces[base + 5, here, :]
    speed = faces[base + 6, here, :]
    total = g[0] + dot3(velocity, g[1:4]) + enthalpy * g[4] + turbulence * g[5]
    pressure = GAMMA_LESS * (shared + speed * g[4])
    carried = speed + wave
    result = [carried * g[0] - total * speed + pressure * kinetic]
    for j in range(3):
        result.append(carried * g[1 + j] + total * normal[j] - pressure * velocity[j])
    result.append(carried * g[4] + pressure)
    result.append(carried * g[5])
    return result


def pull_stage(step, first, last, size, vector, faces, results, gap=None):
    def body(row, carry):
        here = pl.ds(row, size)
        after = pl.ds(row + step, size)
        g = [vector[k, here, :] - vector[k, after, :] for k in range(6)]
        normal = [faces[FN + j, here, :] for j in range(3)]
        wave = faces[FS, here, :]
        shared = dot3(normal, g[1:4])
        left = side_pullback(faces, here, FL, normal, wave, shared, g)
        right = side_pullback(faces, here, FR, normal, -wave, shared, g)
        wave_bar = faces[FD, here, :] * g[0]
        for k in range(1, 6):
            wave_bar = wave_bar + faces[FD + k, here, :] * g[k]
        for k in range(6):
            if k < 5:
                middle = wave_bar * faces[FM + k, here, :]
                results[GL + k, here, :] = left[k] + middle
                results[GR + k, here, :] = right[k] + middle
            else:
                results[GL + k, here, :] = left[k]
                results[GR + k, here, :] = right[k]
        viscous = faces[FQ, here, :]
        mixed_bar = faces[FE, here, :] * g[1]
        for k in range(1, 5):
            mixed_bar = mixed_bar + faces[FE + k, here, :] * g[1 + k]
        for j in range(3):
            results[PU + j, here, :] = viscous * g[1 + j]
        results[PH, here, :] = viscous * g[4]
        diffused = faces[FK, here, :] * g[5]
        shift = faces[FRH, here, :] * mixed_bar
        results[TL, here, :] = shift + diffused
        results[TR, here, :] = shift - diffused
        results[RB, here, :] = faces[FTH, here, :] * mixed_bar

    blocks(first, last, size, body, gap=gap)


def cells_stage(step, first, last, size, pulls, prims, results, store, extra=None, start=0, gap=None):
    def body(row, carry):
        here = pl.ds(row, size)
        before = pl.ds(row - step, size)
        after = pl.ds(row + step, size)
        twice = pl.ds(row - 2 * step, size)
        outcome = []
        for k in range(6):
            gl, gr = results[GL + k, here, :], results[GR + k, before, :]
            value = gl + gr + pulls[12 + k, here, :] * (gl - gr)
            value = value + pulls[6 + k, before, :] * (
                results[GL + k, before, :] - results[GR + k, twice, :]
            )
            value = value - pulls[k, after, :] * (
                results[GL + k, after, :] - results[GR + k, here, :]
            )
            outcome.append(value)
        velocity_bar = [results[PU + j, here, :] - results[PU + j, before, :] for j in range(3)]
        heat_bar = results[PH, here, :] - results[PH, before, :]
        turbulence_bar = results[TL, here, :] + results[TR, before, :]
        density_bar = results[RB, here, :] + results[RB, before, :]
        inverse = prims[0, here, :]
        velocity = [prims[1 + j, here, :] for j in range(3)]
        if extra is not None:
            velocity_bar, turbulence_bar, density_bar = extra(
                row, velocity, velocity_bar, turbulence_bar, density_bar
            )
        kinetic_bar = HEAT_K * heat_bar
        energy_bar = HEAT_E * heat_bar
        velocity_bar = [velocity_bar[j] + kinetic_bar * velocity[j] for j in range(3)]
        scaled = (
            dot3(velocity_bar, velocity)
            + energy_bar * prims[5, here, :]
            + turbulence_bar * prims[4, here, :]
        )
        outcome[0] = outcome[0] + density_bar - scaled * inverse
        for j in range(3):
            outcome[1 + j] = outcome[1 + j] + velocity_bar[j] * inverse
        outcome[4] = outcome[4] + energy_bar * inverse
        outcome[5] = outcome[5] + turbulence_bar * inverse
        return store(row, outcome, carry)

    return blocks(first, last, size, body, start, gap)


def kernel(
    chord_count, span_count, entries,
    flow_in, offset_in, wall_in, codes_in, cost_in, m_out, n_out, sums,
    flow, offset, wall, codes, cost,
    wu, wd, wv, cu, cd, cv, su, sd, sv, halves,
    col_pulls, col_prims, col_faces, chord_pulls, chord_prims, chord_faces,
    span_pulls, span_prims, span_faces, results, source, signs, col_out, span_out,
    plain, partial, last, last_plain, row, others, load_sem, keep_sem, send_sem, recv_sem, sum_send, sum_recv, hello,
):
    chord_id, span_id = lax.axis_index("chord"), lax.axis_index("span")
    mesh_ids = pl.DeviceIdType.MESH

    def chord_at(distance):
        return lax.rem(chord_id + (distance + chord_count), chord_count)

    def span_at(distance):
        return lax.rem(span_id + (distance + span_count), span_count)

    barrier = pltpu.get_barrier_semaphore()
    chord_mates = sorted(range(1, chord_count), key=lambda d: min(d, chord_count - d))
    span_mates = sorted(range(1, span_count), key=lambda d: min(d, span_count - d))
    mates = [(chord_at(d), span_id) for d in chord_mates[:2]]
    mates += [(chord_id, span_at(d)) for d in span_mates]
    mates += [(chord_at(d), span_id) for d in chord_mates[2:]]
    for mate in mates[:4]:
        pl.semaphore_signal(barrier, inc=1, device_id=mate, device_id_type=mesh_ids)

    block = pl.ds(0, ROWS)
    loads = [
        pltpu.make_async_copy(source_ref, target, load_sem.at[index])
        for index, (source_ref, target) in enumerate(
            (
                (flow_in, flow.at[:, block, :]),
                (offset_in, offset.at[:, block, :]),
                (cost_in, cost.at[:, block, :]),
                (codes_in, codes),
                (wall_in, wall),
            )
        )
    ]
    for load in loads:
        load.start()
    for mate in mates[4:]:
        pl.semaphore_signal(barrier, inc=1, device_id=mate, device_id_type=mesh_ids)

    def to_chord_rows(source_ref, target, count, first=0, gain=None):
        def body(k, carry):
            for cell in range(CX):
                base = CHORD_OWN + cell * LAYERS
                high = source_ref[k, pl.ds(first + cell, 8, stride=CX), :]
                low = source_ref[k, pl.ds(first + 8 * CX + cell, 4, stride=CX), :]
                target[k, pl.ds(base, 8), :] = high if gain is None else gain * high
                target[k, pl.ds(base + 8, 4), :] = low if gain is None else gain * low
            return carry

        lax.fori_loop(0, count, body, 0)

    def to_span_rows(source_ref, target, count):
        def body(k, carry):
            target[k, pl.ds(SPAN_OWN, CY), :] = source_ref[k, pl.ds(COL_OWN, CY), :].T
            return carry

        lax.fori_loop(0, count, body, 0, unroll=count)

    started = []

    def exchange(slot, ref, chordwise, depth):
        if chordwise:
            rows = 40 if depth == 3 else 24
            tail = CHORD_OWN + ROWS - rows
            moves = (
                (tail, CHORD_OWN - rows, (chord_at(1), span_id)),
                (CHORD_OWN, CHORD_OWN + ROWS, (chord_at(-1), span_id)),
            )
        else:
            rows = 8
            moves = (
                (SPAN_OWN + CY - rows, SPAN_OWN - rows, (chord_id, span_at(1))),
                (SPAN_OWN, SPAN_OWN + CY, (chord_id, span_at(-1))),
            )
        copies = []
        for side, (first, landing, target) in enumerate(moves):
            copy = pltpu.make_async_remote_copy(
                src_ref=ref.at[:, pl.ds(first, rows), :],
                dst_ref=ref.at[:, pl.ds(landing, rows), :],
                send_sem=send_sem.at[slot, side],
                recv_sem=recv_sem.at[slot, side],
                device_id=target,
                device_id_type=mesh_ids,
            )
            copy.start()
            copies.append(copy)
        started.extend(copies)
        return copies

    def arrive(copies):
        for copy in copies:
            copy.wait_recv()

    for load in loads:
        load.wait()
    to_chord_rows(flow, cu, 6)
    to_chord_rows(offset, cd, 3)
    to_chord_rows(cost, cv.at[0], 6, gain=0.5)

    own = pl.ds(COL_OWN, ROWS)
    code = codes[...]
    for k in range(6):
        near, far = flow[k, 0:8, :], flow[k, 8:16, :]
        sign = jnp.where(code == 0, SLIP_SIGNS[k], jnp.where(code == 1, WALL_SIGNS[k], 0.0))
        level = jnp.where((code == 0) | (code == 1), 0.0, FREESTREAM[k])
        signs[k] = sign
        wu[k, 0:16, :] = jnp.full((16, CY), FREESTREAM[k], jnp.float32)
        wu[k, 16:24, :] = sign * far + level
        wu[k, 24:32, :] = sign * near + level
        wu[k, own, :] = flow[k, block, :]
        wu[k, 128:160, :] = jnp.full((32, CY), FREESTREAM[k], jnp.float32)
        wv[0, k, 0:32, :] = jnp.zeros((32, CY), jnp.float32)
        wv[0, k, own, :] = 0.5 * cost[k, block, :]
        wv[0, k, 128:160, :] = jnp.zeros((32, CY), jnp.float32)
        wv[1, k, 0:32, :] = jnp.zeros((32, CY), jnp.float32)
        wv[1, k, 128:160, :] = jnp.zeros((32, CY), jnp.float32)
    for j in range(3):
        near, far, top = offset[j, 0:8, :], offset[j, 8:16, :], offset[j, 88:96, :]
        wd[j, 0:8, :] = far
        wd[j, 8:16, :] = far
        wd[j, 16:24, :] = far
        wd[j, 24:32, :] = near
        wd[j, own, :] = offset[j, block, :]
        for layer in range(4):
            wd[j, 128 + 8 * layer : 136 + 8 * layer, :] = top

    to_span_rows(wu, su, 6)
    to_span_rows(wd, sd, 3)
    to_span_rows(wv.at[0], sv.at[0], 6)

    def source_body(row, carry):
        here = pl.ds(row, 16)
        cells = pl.ds(row + COL_OWN, 16)
        density = wu[0, cells, :]
        inverse = 1.0 / density
        velocity = [wu[1 + j, cells, :] * inverse for j in range(3)]
        turbulence = wu[5, cells, :] * inverse
        near = 1.0 / wall[here, :]
        square = dot3(velocity, velocity) + 0.01
        root_inverse = lax.rsqrt(square)
        slope = CB_ONE * near
        shear = slope * (square * root_inverse)
        decay = CW_ONE * turbulence * near * near
        source[0, here, :] = -2.0 * turbulence * (shear - decay)
        source[1, here, :] = -2.0 * density * (shear - 2.0 * decay)
        source[2, here, :] = -2.0 * density * turbulence * slope * root_inverse

    blocks(0, ROWS, 16, source_body)

    def column_ready():
        slopes_stage(COL_STEP, 16, 144, 16, wu, halves, col_pulls, col_prims)
        faces_stage(COL_STEP, 2, 24, 136, 16, wu, wd, halves, col_prims, col_faces)
        for k in range(6):
            col_pulls[6 + k, 8:16, :] = jnp.zeros((8, CY), jnp.float32)

    def column_product(vector):
        for slot in range(RESULT_COUNT):
            results[slot, 0:24, :] = jnp.zeros((24, CY), jnp.float32)
        pull_stage(COL_STEP, 24, 136, 16, vector, col_faces, results)

        def column_store(row, outcome, carry):
            for k in range(6):
                col_out[k, pl.ds(row, 16), :] = outcome[k]

        def with_source(row, velocity, velocity_bar, turbulence_bar, density_bar):
            here = pl.ds(pl.multiple_of(row - COL_OWN, 8), 16)
            value = vector[5, pl.ds(row, 16), :]
            pulled = source[2, here, :] * value
            return (
                [velocity_bar[j] + pulled * velocity[j] for j in range(3)],
                turbulence_bar + source[1, here, :] * value,
                density_bar + source[0, here, :] * value,
            )

        cells_stage(COL_STEP, 16, 32, 16, col_pulls, col_prims, results, column_store)
        cells_stage(COL_STEP, 32, 128, 16, col_pulls, col_prims, results, column_store, with_source)
        for k in range(6):
            sign = signs[k]
            col_out[k, 32:40, :] = col_out[k, 32:40, :] + sign * col_out[k, 24:32, :]
            col_out[k, 40:48, :] = col_out[k, 40:48, :] + sign * col_out[k, 16:24, :]

    def span_ready(first, last, faces_last, gap=None, faces_gap=None):
        slopes_stage(SPAN_STEP, first, last, 16, su, halves, span_pulls, span_prims, gap)
        faces_stage(
            SPAN_STEP, 1, first, faces_last, 16, su, sd, halves, span_prims, span_faces, faces_gap
        )

    def span_product(vector, first, last, cells_first, cells_last, gap=None, cells_gap=None):
        pull_stage(SPAN_STEP, first, last, 16, vector, span_faces, results, gap)

        def span_store(row, outcome, carry):
            for k in range(6):
                span_out[k, pl.ds(pl.multiple_of(row - SPAN_OWN, 8), 16), :] = outcome[k]

        cells_stage(
            SPAN_STEP, cells_first, cells_last, 16, span_pulls, span_prims, results, span_store,
            gap=cells_gap,
        )

    def span_inside(vector):
        span_product(vector, 24, 120, 32, 112)

    def span_edges(vector):
        span_product(vector, 8, 152, 16, 144, (24, 120), (32, 112))

    def column_and_span():
        def body(k, carry):
            plain[k, block, :] = span_out[k].T[0:ROWS, :] + col_out[k, own, :]
            return carry

        lax.fori_loop(0, 6, body, 0, unroll=6)
        to_chord_rows(plain, partial, 6)

    def chord_product(vector, arrivals, store, start=0):
        def add_store(row, outcome, carry):
            here = pl.ds(row, outcome[0].shape[0])
            return store(row, [outcome[k] + partial[k, here, :] for k in range(6)], carry)

        def some_faces(first, last, size, gap=None):
            pull_stage(CHORD_STEP, first, last, size, vector, chord_faces, results, gap)

        def some_cells(first, last, size, start, gap=None):
            return cells_stage(
                CHORD_STEP, first, last, size, chord_pulls, chord_prims, results, add_store, None, start, gap
            )

        some_faces(40, 120, 16)
        some_faces(116, 124, 8)
        start = some_cells(64, 112, 16, start)
        arrive(arrivals)
        some_faces(16, 152, 16, (48, 120))
        return some_cells(40, 136, 24, start, (64, 112))

    def from_chord_rows(source_ref, target, first):
        def body(k, carry):
            for layer in range(LAYERS):
                rows = pl.ds(CHORD_OWN + layer, CX, stride=LAYERS)
                target[k, pl.ds(first + layer * CX, CX), :] = source_ref[k, rows, :]
            return carry

        lax.fori_loop(0, 6, body, 0)

    column_ready()
    pl.semaphore_wait(barrier, len(mates))
    chord_flow = exchange(0, cu, True, 3)
    chord_offset = exchange(2, cd, True, 2)
    chord_vector = exchange(4, cv.at[0], True, 2)
    span_flow = exchange(1, su, False, 3)
    span_offset = exchange(3, sd, False, 2)
    span_vector = exchange(5, sv.at[0], False, 2)
    for d in chord_mates:
        pl.semaphore_signal(hello, inc=1, device_id=(chord_at(d), span_id), device_id_type=mesh_ids)
    column_product(wv.at[0])
    span_ready(24, 136, 120)
    span_inside(sv.at[0])
    arrive(span_flow + span_offset)
    span_ready(8, 152, 152, (24, 136), (24, 120))
    arrive(span_vector)
    span_edges(sv.at[0])
    column_and_span()
    arrive(chord_flow)
    slopes_stage(CHORD_STEP, 16, 160, 16, cu, halves, chord_pulls, chord_prims)
    arrive(chord_offset)
    faces_stage(CHORD_STEP, 0, 16, 160, 16, cu, cd, halves, chord_prims, chord_faces)

    def first_store(row, outcome, carry):
        for k in range(6):
            cv[1, k, pl.ds(row, outcome[k].shape[0]), :] = 0.5 * outcome[k]

    chord_product(cv.at[0], chord_vector, first_store)

    chord_vector = exchange(6, cv.at[1], True, 2)
    from_chord_rows(cv.at[1], wv.at[1], COL_OWN)
    to_span_rows(wv.at[1], sv.at[1], 6)
    span_vector = exchange(7, sv.at[1], False, 2)
    nothing = jnp.zeros((8, CY), jnp.float32)

    def add_product(total, one, two):
        product = one * two
        for part in range(0, product.shape[0], 8):
            total = total + product[part : part + 8, :]
        return total

    def first_inner(row, carry):
        cc, cm, mm = carry
        here = pl.ds(row, 16)
        for k in range(6):
            c, m = cv[0, k, here, :], cv[1, k, here, :]
            cc, cm, mm = add_product(cc, c, c), add_product(cm, c, m), add_product(mm, m, m)
        return cc, cm, mm

    row_of = lax.broadcasted_iota(jnp.int32, (8, CY), 0)
    lane_of = lax.broadcasted_iota(jnp.int32, (8, CY), 1)

    def pack(packed, first, values):
        for index, value in enumerate(values):
            packed = jnp.where(row_of == first + index, jnp.sum(value, axis=0, keepdims=True), packed)
        return packed

    keep_m = pltpu.make_async_copy(wv.at[1, :, own, :], m_out, keep_sem.at[0])
    keep_m.start()
    packed = pack(nothing, 0, blocks(40, 136, 16, first_inner, (nothing,) * 3))
    column_product(wv.at[1])
    span_inside(sv.at[1])
    arrive(span_vector)
    span_edges(sv.at[1])
    column_and_span()

    def second_store(row, outcome, carry):
        cn, mn, nn = carry
        here = pl.ds(row, outcome[0].shape[0])
        for k in range(6):
            n = 0.5 * outcome[k]
            last[k, here, :] = n
            c, m = cv[0, k, here, :], cv[1, k, here, :]
            cn, mn, nn = add_product(cn, c, n), add_product(mn, m, n), add_product(nn, n, n)
        return cn, mn, nn

    packed = pack(packed, 3, chord_product(cv.at[1], chord_vector, second_store, (nothing,) * 3))

    packed = jnp.broadcast_to(jnp.sum(packed, axis=1, keepdims=True), (8, CY))
    packed = jnp.where((lane_of >= 16 * row_of) & (lane_of < 16 * row_of + 16), packed, 0.0)
    row[...] = jnp.broadcast_to(jnp.sum(packed, axis=0, keepdims=True), (8, CY))
    mine = sums.at[chord_id * span_count + span_id, pl.ds(0, 1), :]
    keep_row = pltpu.make_async_copy(row.at[pl.ds(0, 1), :], mine, keep_sem.at[2])
    keep_row.start()

    pl.semaphore_wait(hello, chord_count - 1)
    for chord_to, span_to in all_partners(chord_count, span_count):
        copy = pltpu.make_async_remote_copy(
            src_ref=row.at[pl.ds(0, 1), :],
            dst_ref=mine,
            send_sem=sum_send,
            recv_sem=sum_recv,
            device_id=(chord_to(chord_id), span_to(span_id)),
            device_id_type=mesh_ids,
        )
        copy.start()
    from_chord_rows(last, last_plain, 0)
    keep_n = pltpu.make_async_copy(last_plain, n_out, keep_sem.at[1])
    keep_n.start()
    for copy in started:
        copy.wait_send()
    keep_m.wait()
    pltpu.make_async_copy(others, others, sum_recv).wait()
    pltpu.make_async_copy(others, others, sum_send).wait()
    keep_n.wait()
    keep_row.wait()


def all_partners(chord_count, span_count):
    ys = min(4, chord_count)
    zh = chord_count // ys
    cores = min(2, span_count)
    zl = min(2, span_count // cores)
    xs = span_count // (cores * zl)

    def chord_to(dz, dy):
        return lambda c: lax.rem(lax.div(c, ys) + dz, zh) * ys + lax.rem(c + dy, ys)

    def span_to(dx, dz, dk):
        def place(s):
            x = lax.rem(lax.div(s, zl * cores) + dx, xs)
            z = lax.rem(lax.div(s, cores) + dz, zl)
            return (x * zl + z) * cores + lax.rem(s + dk, cores)

        return place

    found = []
    for high in range(zh):
        for dy in range(ys):
            for dx in range(xs):
                for low in range(zl):
                    for dk in range(cores):
                        hops = min(dy, ys - dy) + min(dx, xs - dx) + (2 if high > low else low)
                        if high + dy + dx + low + dk:
                            found.append((hops, chord_to(high, dy), span_to(dx, low, dk)))
    found.sort(key=lambda entry: -entry[0])
    return [entry[1:] for entry in found]


def final_kernel(
    entries, sums_in, cost_in, m_in, n_in, basis_out, hessenberg,
    cost, m, n, sums, table, basis, sums_sem, load_sem, out_sem,
):
    first_row = pl.ds(0, 1)
    first = pltpu.make_async_copy(sums_in.at[:, first_row, :], sums.at[:, first_row, :], sums_sem)
    first.start()
    loads = []
    for k in range(6):
        for index, (source_ref, target) in enumerate(((cost_in, cost), (m_in, m), (n_in, n))):
            load = pltpu.make_async_copy(source_ref.at[k], target.at[k], load_sem.at[k, index])
            load.start()
            loads.append(load)
    first.wait()
    parts = [sums[device, first_row, :] for device in range(sums.shape[0])]
    while len(parts) > 1:
        parts = [sum(parts[index : index + 2]) for index in range(0, len(parts), 2)]
    total = parts[0] * (4.0 / entries)
    cc, cm, mm, cn, mn, nn = [
        jnp.broadcast_to(total[:, 16 * index : 16 * index + 1], (1, CY)) for index in range(6)
    ]

    scale = lax.rsqrt(cc + NORM_EPS)
    h11 = cm * scale * scale
    fresh = jnp.maximum(mm - 2.0 * h11 * cm + h11 * h11 * cc, 0.0)
    square = fresh * scale * scale + NORM_EPS
    inverse = lax.rsqrt(square)
    h21 = square * inverse
    gain = scale * inverse
    h12 = gain * scale * (cn - h11 * cm)
    h22 = gain * gain * (mn - h11 * cn - h11 * mm + h11 * h11 * cm)
    along_m = -gain * (h11 + h22)
    along_c = h22 * gain * h11 - h12 * scale
    fresh = (
        gain * gain * nn + along_m * along_m * mm + along_c * along_c * cc
        + 2.0 * (gain * along_m * mn + gain * along_c * cn + along_m * along_c * cm)
    )
    square = jnp.maximum(fresh, 0.0) + NORM_EPS
    inverse = lax.rsqrt(square)
    h32 = square * inverse
    factors = [f * inverse for f in (along_c, 2.0 * along_m, 2.0 * gain)]
    row_of = lax.broadcasted_iota(jnp.int32, (8, CY), 0)
    rows_out = jnp.zeros((8, CY), jnp.float32)
    for index, value in enumerate((h11, h21, h12, h22, h32)):
        rows_out = jnp.where(row_of == index, value, rows_out)
    table[...] = rows_out
    factors = [jnp.broadcast_to(factor, (ROWS, CY)) for factor in factors]
    stores = []
    for k in range(6):
        for load in loads[3 * k : 3 * k + 3]:
            load.wait()
        basis[k] = factors[0] * cost[k] + factors[1] * m[k] + factors[2] * n[k]
        store = pltpu.make_async_copy(basis.at[k], basis_out.at[k], out_sem.at[k])
        store.start()
        stores.append(store)
    for index in range(5):
        hessenberg[index] = table[index, 0]
    for store in stores:
        store.wait()


def on_device(chord_count, span_count, flow_state, displacement, wall_distance, face_codes, cost_gradient):
    entries = float(cost_gradient.size * chord_count * span_count)

    def vmem(*shape):
        return pltpu.VMEM(shape, jnp.float32)

    outside = pl.BlockSpec(memory_space=pl.ANY)
    devices = chord_count * span_count
    m, n, sums = pl.pallas_call(
        functools.partial(kernel, chord_count, span_count, entries),
        out_shape=(
            jax.ShapeDtypeStruct((6, ROWS, CY), jnp.float32),
            jax.ShapeDtypeStruct((6, ROWS, CY), jnp.float32),
            jax.ShapeDtypeStruct((devices, 8, CY), jnp.float32),
        ),
        in_specs=[outside] * 5,
        out_specs=(outside, outside, outside),
        scratch_shapes=[
            vmem(6, PADDED, CY), vmem(3, PADDED, CY), vmem(ROWS, CY), pltpu.VMEM((CX, CY), jnp.int32),
            vmem(6, PADDED, CY),
            vmem(6, COL_ROWS, CY), vmem(3, COL_ROWS, CY), vmem(2, 6, COL_ROWS, CY),
            vmem(6, CHORD_ROWS, CY), vmem(3, CHORD_ROWS, CY), vmem(2, 6, CHORD_ROWS, CY),
            vmem(6, SPAN_ROWS, CY), vmem(3, SPAN_ROWS, CY), vmem(2, 6, SPAN_ROWS, CY),
            vmem(12, CHORD_ROWS, CY),
            vmem(18, COL_ROWS, CY), vmem(6, COL_ROWS, CY), vmem(FACE_COUNT, COL_ROWS, CY),
            vmem(18, CHORD_ROWS, CY), vmem(6, CHORD_ROWS, CY), vmem(FACE_COUNT, CHORD_ROWS, CY),
            vmem(18, SPAN_ROWS, CY), vmem(6, SPAN_ROWS, CY), vmem(FACE_COUNT, SPAN_ROWS, CY),
            vmem(RESULT_COUNT, CHORD_ROWS, CY), vmem(3, ROWS, CY), vmem(6, CX, CY),
            vmem(6, COL_ROWS, CY), vmem(6, CY, CY),
            vmem(6, PADDED, CY), vmem(6, CHORD_ROWS, CY), vmem(6, CHORD_ROWS, CY), vmem(6, ROWS, CY),
            vmem(8, CY), vmem(devices - 1, CY),
            pltpu.SemaphoreType.DMA((5,)), pltpu.SemaphoreType.DMA((3,)),
            pltpu.SemaphoreType.DMA((8, 2)), pltpu.SemaphoreType.DMA((8, 2)),
            pltpu.SemaphoreType.DMA, pltpu.SemaphoreType.DMA,
            pltpu.SemaphoreType.REGULAR,
        ],
        compiler_params=pltpu.CompilerParams(
            collective_id=0, has_side_effects=True, vmem_limit_bytes=62 * 1024 * 1024
        ),
        name="arnoldi",
    )(
        flow_state.reshape(6, ROWS, CY),
        displacement.reshape(3, ROWS, CY),
        wall_distance.reshape(ROWS, CY),
        face_codes,
        cost_gradient.reshape(6, ROWS, CY),
    )
    basis, hessenberg = pl.pallas_call(
        functools.partial(final_kernel, entries),
        out_shape=(
            jax.ShapeDtypeStruct((6, ROWS, CY), jnp.float32),
            jax.ShapeDtypeStruct((5,), jnp.float32),
        ),
        in_specs=[outside] * 4,
        out_specs=(outside, pl.BlockSpec(memory_space=pltpu.SMEM)),
        scratch_shapes=[
            vmem(6, ROWS, CY), vmem(6, ROWS, CY), vmem(6, ROWS, CY), vmem(devices, 8, CY), vmem(8, CY),
            vmem(6, ROWS, CY),
            pltpu.SemaphoreType.DMA, pltpu.SemaphoreType.DMA((6, 3)), pltpu.SemaphoreType.DMA((6,)),
        ],
        compiler_params=pltpu.CompilerParams(vmem_limit_bytes=62 * 1024 * 1024),
        name="combination",
    )(sums, cost_gradient.reshape(6, ROWS, CY), m, n)
    return basis.reshape(cost_gradient.shape), hessenberg


def solution(mesh):
    return jax.shard_map(
        functools.partial(on_device, mesh.shape["chord"], mesh.shape["span"]),
        mesh=mesh,
        in_specs=(
            P(None, None, "chord", "span"),
            P(None, None, "chord", "span"),
            P(None, "chord", "span"),
            P("chord", "span"),
            P(None, None, "chord", "span"),
        ),
        out_specs=(P(None, None, "chord", "span"), P()),
        check_vma=False,
    )
```
